32 devices in a mesh: mem: 2 (over core), gy: 4 (over y, x), gx: 4 (over z).
Axes of the slice: x: 2, y: 2, z: 4, core: 2. Of those that a mesh axis runs over, the one named last changes fastest.
Arguments:
- increment: float32 [4, 256, 4096], P(None, 'gy', 'gx'), may hold values from -6 to 6
- members: float32 [2, 4, 256, 4096], P('mem', None, 'gy', 'gx'), may hold values from -6 to 6
- zonal_diff: float32 [256, 4096], P('gy', 'gx'), may hold values from 0.05 to 0.35
- merid_diff: float32 [256, 4096], P('gy', 'gx'), may hold values from 0.02 to 0.15
- sea_mask: int32 [256, 4096], P('gy', 'gx'), may hold values 0 or 1
Outputs:
- product: float32 [4, 256, 4096], P(None, 'gy', 'gx')
The draws below stay inside these ranges and needn't reach their ends.
All inputs are finite; a program needn't handle non-finite values. No bound on the sum of `sea_mask` on one device may be relied on, other than what follows from the above.
Results may differ from the reference program's by a relative error of at most 0.00002.
Values sent between devices are 32-bit elements; how exact they have to be, the bound alone decides.
No kernel may reach another device: no remote copies, remote signals or barrier semaphores. Data moves between devices by JAX's collectives and lax.ppermute only.
A program may use at most 64 MiB of HBM per device.

```python
import math
import jax
import jax.numpy as jnp
from jax import lax

LEVELS = 4
STEPS = 4
MEMBERS = 2
NX = 4096
NY = 256


def place_ends(entries, rng, smallest, top_value):
    extent = entries.shape
    place = [jax.random.randint(jax.random.fold_in(rng, axis), (), 0, extent[axis]) for axis in range(len(extent))]
    entries = entries.at[tuple(place)].set(smallest)
    longest = extent.index(max(extent))
    place[longest] = (place[longest] + 1) % extent[longest]
    return entries.at[tuple(place)].set(top_value)


def levels(stream_key, extent, pieces, low, high):
    def one(axis_at, parts):
        steps = jax.random.uniform(jax.random.fold_in(jax.random.fold_in(stream_key, 6), axis_at), (parts,), jnp.float32, low / len(pieces), high / len(pieces))
        return jnp.repeat(jnp.exp(steps), extent[axis_at] // parts).reshape((-1,) + (1,) * (len(extent) - axis_at - 1))

    level = one(*pieces[0])
    for cut in pieces[1:]:
        level = level * one(*cut)
    return level


def noise(stream_key, dims, deviation, reach, split=(), dtype=jnp.bfloat16):
    level = levels(stream_key, dims, split, -0.22, 0.18) if split else 1.0
    drawn = jax.random.normal(stream_key, dims, jnp.float32) * deviation * level
    return jnp.minimum(jnp.maximum(drawn, -reach), reach).astype(dtype)


def setup_inputs(seed: int = 0) -> dict:
    seeds = jax.random.split(jax.random.key(seed), 6)
    increment = noise(seeds[0], (LEVELS, NY, NX), 1.0, 6.0, ((1, 4), (2, 4)), jnp.float32)
    members = noise(seeds[1], (MEMBERS, LEVELS, NY, NX), 1.0, 6.0, ((0, 2), (2, 4), (3, 4)), jnp.float32)
    zonal_diff = jnp.clip(jnp.exp(math.log(0.35) - 1.9459101 * jax.random.uniform(seeds[2], (NY, NX), jnp.float32) ** levels(seeds[2], (NY, NX), ((0, 4), (1, 4)), -0.2, 0.2)), 0.05, 0.35)
    merid_diff = jnp.clip(jnp.exp(math.log(0.15) - 2.014903 * jax.random.uniform(seeds[3], (NY, NX), jnp.float32) ** levels(seeds[3], (NY, NX), ((0, 4), (1, 4)), -0.2, 0.2)), 0.02, 0.15)
    sea_mask = place_ends((jax.random.randint(seeds[4], (NY, NX), 0, 8) < 7).astype(jnp.int32), jax.random.fold_in(seeds[4], 1), 0, 1)
    return dict(increment=increment, members=members, zonal_diff=zonal_diff, merid_diff=merid_diff, sea_mask=sea_mask)


def widen(field):
    field = jnp.concatenate([field[..., -1:], field, field[..., :1]], axis=-1)
    zero_row = jnp.zeros(field.shape[:-2] + (1, field.shape[-1]), jnp.float32)
    return jnp.concatenate([zero_row, field, zero_row], axis=-2)


def face_weights(zonal, merid, wet):
    east = zonal[:, :-1] * wet[:, :-1] * wet[:, 1:]
    north = merid[:-1, :] * wet[:-1, :] * wet[1:, :]
    return east, north


def sweep(field, east, north):
    centre = field[:, 1:-1, 1:-1]
    go_east = east[1:-1, 1:] * (field[:, 1:-1, 2:] - centre)
    go_west = east[1:-1, :-1] * (centre - field[:, 1:-1, :-2])
    go_north = north[1:, 1:-1] * (field[:, 2:, 1:-1] - centre)
    go_south = north[:-1, 1:-1] * (centre - field[:, :-2, 1:-1])
    return centre + go_east - go_west + go_north - go_south


def reference(increment, members, zonal_diff, merid_diff, sea_mask):
    wet = sea_mask.astype(jnp.float32)
    east, north = face_weights(widen(zonal_diff), widen(merid_diff), widen(wet))

    def one_member(total, member):
        field = member * increment * wet
        for step in range(STEPS):
            field = sweep(widen(field), east, north)
        return total + member * field, None

    total, unused = lax.scan(one_member, jnp.zeros(increment.shape, jnp.float32), members)
    return total
```

```python
import functools
import jax
import jax.numpy as jnp
from jax import lax
from jax.experimental import pallas as pl
from jax.experimental.pallas import tpu as pltpu
from jax.sharding import PartitionSpec as P

STEPS = 4
TILE = 8
LANES = 128
AXES = ("mem", "gy", "gx")
LEFT = 2 * TILE
DEPTH = LANES + 2 * LEFT
LOW = slice(LEFT - TILE, LEFT)
HIGH = slice(LEFT + LANES, LEFT + LANES + TILE)
BODY = slice(LEFT, LEFT + LANES)
WIDE = slice(LEFT - TILE, LEFT + LANES + TILE)
AFTER = slice(LEFT - TILE + 1, LEFT + LANES + TILE + 1)

F32 = jnp.float32
VMEM = pl.BlockSpec(memory_space=pltpu.VMEM)
HBM = pl.BlockSpec(memory_space=pltpu.HBM)


def half_of(gy_size):
    core = lax.rem(lax.axis_index("mem"), 2)
    later = (lax.axis_index("gy") >= gy_size // 2).astype(jnp.int32)
    return lax.rem(core + later, 2)


def kept(*shape):
    return pltpu.VMEM(shape, F32)


def pinned(x):
    return pltpu.with_memory_space_constraint(x, pltpu.VMEM)


def in_hbm(x):
    return pltpu.with_memory_space_constraint(x, pltpu.HBM)


def tile(c):
    return slice(c * LANES, (c + 1) * LANES)


def lane_ids(rows):
    return lax.broadcasted_iota(jnp.int32, (rows, LANES), 1)


def row_start(half, rows):
    return pl.multiple_of(half * (rows // 2 - TILE), TILE)


def run(copies):
    for copy in copies:
        copy.start()
    for copy in copies:
        copy.wait()


def partner_rows_kernel(gy_size, members, out, sem):
    rows = members.shape[2]
    part = pl.ds(row_start(1 - half_of(gy_size), rows), out.shape[2])
    run([
        pltpu.make_async_copy(members.at[0, :, part, tile(c)], out.at[:, c], sem.at[c])
        for c in range(out.shape[1])
    ])


def load_kernel(gy_size, members, increment, zonal, merid, mask, own, forcing, zm, mm, wet, mask_buf, sems):
    rows = increment.shape[1]
    tiles, tall = zm.shape[:2]
    part = pl.ds(row_start(half_of(gy_size), rows), tall)
    flat = [
        [pltpu.make_async_copy(ref.at[part, tile(c)], buf.at[c], sems.at[k, c]) for c in range(tiles)]
        for k, (ref, buf) in enumerate(((mask, mask_buf), (zonal, zm), (merid, mm)))
    ]
    deep = [
        pltpu.make_async_copy(increment.at[:, part, tile(c)], forcing.at[:, c], sems.at[3, c]) for c in range(tiles)
    ]
    last = [
        pltpu.make_async_copy(members.at[0, :, part, tile(c)], own.at[:, c], sems.at[4, c]) for c in range(tiles)
    ]
    for copy in sum(flat, []) + deep + last:
        copy.start()
    for copy in sum(flat, []):
        copy.wait()
    wet[...] = mask_buf[...].astype(F32)
    zm[...] = zm[...] * wet[...]
    mm[...] = mm[...] * wet[...]
    for copy in deep:
        copy.wait()
    forcing[...] = forcing[...] * wet[...][None]
    for copy in last:
        copy.wait()


def pack_rows_kernel(gy_size, own, other, forcing, zm, mm, wet, strip):
    levels, tiles, tall, _ = own.shape
    half = half_of(gy_size)
    j = lax.axis_index("gy")
    same_core = jnp.where(half == 0, j == gy_size // 2, j == gy_size // 2 - 1)
    edge = pl.ds(pl.multiple_of(half * (tall - TILE), TILE), TILE)
    low = lax.broadcasted_iota(jnp.int32, (tiles, TILE, LANES), 1) < TILE // 2

    def put(place, first, second):
        first = jnp.where(half == 0, first, pltpu.roll(first, TILE // 2, 1))
        second = jnp.where(half == 0, pltpu.roll(second, TILE // 2, 1), second)
        strip[place] = jnp.where(low, first, second)

    for level in range(levels):
        force = forcing[level, :, edge, :]
        mine = own[level, :, edge, :] * force
        theirs = other[level, :, edge, :] * force
        put(level, jnp.where(same_core, mine, theirs), jnp.where(same_core, theirs, mine))
    put(levels, zm[:, edge, :], mm[:, edge, :])
    put(levels + 1, wet[:, edge, :], wet[:, edge, :])


def mirror(ref, p):
    ref[p, LOW, :] = pltpu.roll(ref[p, slice(LEFT + LANES - TILE, LEFT + LANES), :], 1, 1)
    ref[p, HIGH, :] = pltpu.roll(ref[p, slice(LEFT, LEFT + TILE), :], LANES - 1, 1)


def faces_east(east, zon, wets, p):
    east[p, WIDE, :] = zon[p, WIDE, :] * wets[p, AFTER, :]


def faces_north(north, mer, wets, p):
    north[p, WIDE, :] = mer[p, WIDE, :] * wets[p + 1, WIDE, :]


def edge_strips(west_out, east_out, u, zon, mer, wets, p, at):
    slot = lane_ids(4) % TILE
    for out, rows, base in ((west_out, slice(LEFT, LEFT + 4), 0), (east_out, slice(LEFT + LANES - 4, LEFT + LANES), 7)):
        sign = 1 if base == 0 else -1
        value = pltpu.roll(u[p, rows, :], (7 - base - base) % LANES, 1)
        for k, ref in enumerate((zon, mer, wets)):
            here = 7 - base - sign * (k + 1)
            value = jnp.where(slot == here, pltpu.roll(ref[p, rows, :], (here - base) % LANES, 1), value)
        out[at, :] = value


def turn(ref, start, height):
    parts = [ref[pl.ds(s, TILE, stride=height), :] for s in start]
    return jnp.concatenate(parts, axis=0).T


def prepare_kernel(gy_size, own, other, forcing, zm, mm, wet, u, zon, mer, wets, east, north, west_out, east_out, plain, flat):
    levels, tiles, tall, _ = own.shape
    full = tall + TILE
    planes = full // 2
    half = half_of(gy_size)
    lead = (1 - half) * TILE
    for f in range(2 * levels):
        member = (own, other)[f % 2]
        for c in range(tiles):
            base = (f * tiles + c) * full
            plain[pl.ds(pl.multiple_of(base + lead, TILE), tall), :] = member[f // 2, c] * forcing[f // 2, c]
            plain[pl.ds(pl.multiple_of(base + half * tall, TILE), TILE), :] = jnp.zeros((TILE, LANES), F32)
    for k, ref in enumerate((zm, mm, wet)):
        for c in range(tiles):
            base = (k * tiles + c) * full
            flat[pl.ds(pl.multiple_of(base + lead, TILE), tall), :] = ref[c]
            flat[pl.ds(pl.multiple_of(base + half * tall, TILE), TILE), :] = jnp.zeros((TILE, LANES), F32)
    blank = jnp.zeros((TILE, LANES), F32)
    for ref in (u, zon, mer, wets, east, north):
        for p in range(planes + 2):
            ref[p, slice(0, TILE), :] = blank
            ref[p, slice(DEPTH - TILE, DEPTH), :] = blank
    for q in range(planes):
        u[q + 1, BODY, :] = turn(
            plain, [f * tiles * full + ch * planes + q for f in range(2 * levels) for ch in range(2)], full
        )
        for k, ref in enumerate((zon, mer, wets)):
            ref[q + 1, BODY, :] = turn(
                flat, [k * tiles * full + ch * planes + q for f in range(2 * levels) for ch in range(2)], full
            )
        for ref in (u, zon, mer, wets):
            mirror(ref, q + 1)
    wets[planes + 1, WIDE, :] = pltpu.roll(wets[1, WIDE, :], LANES - TILE, 1)
    for q in range(planes):
        faces_east(east, zon, wets, q + 1)
        faces_north(north, mer, wets, q + 1)
        edge_strips(west_out, east_out, u, zon, mer, wets, q + 1, slice(4 * q, 4 * q + 4))


def halo_rows_kernel(gy_size, strip, *refs):
    u, zon, mer, wets, east, north, west_out, east_out = refs[8:]
    tiles = TILE
    levels = strip.shape[0] // (tiles * TILE) - 2
    planes = u.shape[0] - 2
    half = half_of(gy_size)
    mine = (lane_ids(LANES) // TILE) % 2 == half
    first = 1 + 4 + half * (planes // 2)
    for r in range(4):
        p = first + r
        for ref, places in (
            (u, range(2 * levels)),
            (zon, [2 * levels] * 2 * levels),
            (mer, [2 * levels + 1] * 2 * levels),
            (wets, [2 * levels + 2] * 2 * levels),
        ):
            new = turn(strip, [k // 2 * tiles * TILE + 4 * (k % 2) + r for k in places for ch in range(2)], TILE)
            ref[p, BODY, :] = jnp.where(mine, new, ref[p, BODY, :])
            mirror(ref, p)
    for r in range(-1, 4):
        p = first + r
        if r >= 0:
            faces_east(east, zon, wets, p)
            edge_strips(west_out, east_out, u, zon, mer, wets, p, pl.ds(4 * (p - 1), 4))
        faces_north(north, mer, wets, p)


def diffuse_kernel(gy_size, from_east, from_west, own, other, *refs):
    u, zon, mer, wets, east, north = refs[6:12]
    out, u_next, plain = refs[12:]
    levels, tiles, tall, _ = own.shape
    planes = u.shape[0] - 2
    full = 2 * planes
    half = half_of(gy_size)
    slot = lane_ids(4) % TILE
    for strip, rows, base in (
        (from_west, slice(LEFT - 4, LEFT), 0),
        (from_east, slice(LEFT + LANES, LEFT + LANES + 4), 7),
    ):
        sign = 1 if base == 0 else -1
        for k, ref in enumerate((u, zon, mer, wets)):
            value = strip[...]
            if k:
                value = pltpu.roll(value, (-sign * k) % LANES, 1)
            for q in range(planes):
                ref[q + 1, rows, :] = jnp.where(slot == base, value[4 * q : 4 * q + 4], ref[q + 1, rows, :])
    wets[planes + 1, WIDE, :] = pltpu.roll(wets[1, WIDE, :], LANES - TILE, 1)
    for q in range(planes):
        for rows in (LEFT - TILE, LEFT + LANES - TILE, LEFT + LANES):
            at = slice(rows, rows + TILE)
            east[q + 1, at, :] = zon[q + 1, at, :] * wets[q + 1, slice(rows + 1, rows + TILE + 1), :]
            north[q + 1, at, :] = mer[q + 1, at, :] * wets[q + 2, at, :]
    north[0, WIDE, :] = pltpu.roll(north[planes, WIDE, :], TILE, 1)

    source, target = u, u_next
    for step in range(STEPS):
        source[0, WIDE, :] = pltpu.roll(source[planes, WIDE, :], TILE, 1)
        source[planes + 1, WIDE, :] = pltpu.roll(source[1, WIDE, :], LANES - TILE, 1)
        if step == 0:
            blank = jnp.zeros((TILE, LANES), F32)
            for p in range(planes + 2):
                target[p, slice(0, TILE), :] = blank
                target[p, slice(DEPTH - TILE, DEPTH), :] = blank
        span = BODY if step == STEPS - 1 else WIDE
        for start in range(span.start, span.stop, TILE):
            at, ahead, behind = slice(start, start + TILE), slice(start + 1, start + 1 + TILE), slice(start - 1, start - 1 + TILE)
            here = source[1, at, :]
            south = north[0, at, :] * (here - source[0, at, :])
            for p in range(1, planes + 1):
                above = source[p + 1, at, :]
                flux = north[p, at, :] * (above - here)
                go_east = east[p, at, :] * (source[p, ahead, :] - here)
                go_west = east[p, behind, :] * (here - source[p, behind, :])
                target[p, at, :] = here + go_east - go_west + flux - south
                here, south = above, flux
        source, target = target, source
    for q in range(planes):
        flat = source[q + 1, BODY, :].T
        for f in range(2 * levels):
            for ch in range(2):
                group = (2 * f + ch) * tiles
                plain[pl.ds(f * tiles * full + ch * planes + q, tiles, stride=full), :] = flat[group : group + tiles]
    rows = tall - TILE
    part = pl.ds(pl.multiple_of(half * TILE, TILE), rows)
    for level in range(levels):
        for c in range(tiles):
            a, b = (((2 * level + k) * tiles + c) * full + TILE for k in range(2))
            out[level, c] = (
                own[level, c, part, :] * plain[pl.ds(a, rows), :] + other[level, c, part, :] * plain[pl.ds(b, rows), :]
            )


def join_kernel(gy_size, mine, theirs, out, sems):
    half = half_of(gy_size)
    tiles, rows = mine.shape[1:3]
    run([
        pltpu.make_async_copy(
            ref.at[:, c], out.at[:, pl.ds(pl.multiple_of(where * rows, TILE), rows), tile(c)], sems.at[k, c]
        )
        for k, (ref, where) in enumerate(((mine, half), (theirs, 1 - half)))
        for c in range(tiles)
    ])


def shards(sizes, increment, members, zonal_diff, merid_diff, sea_mask):
    n_mem, n_gy, n_gx = sizes
    levels, rows, width = increment.shape
    tiles = width // LANES
    mid = rows // 2
    tall = mid + TILE
    full = tall + TILE
    planes = full // 2
    assert tiles == TILE and 4 * levels * tiles == LANES and n_mem % 2 == 0

    def call(kernel, ins, specs, outs, scratch=(), out_specs=None, aliases={}):
        return pl.pallas_call(
            functools.partial(kernel, n_gy),
            out_shape=outs,
            in_specs=specs,
            out_specs=out_specs if out_specs is not None else jax.tree.map(lambda _: VMEM, outs),
            scratch_shapes=scratch,
            input_output_aliases=aliases,
            compiler_params=pltpu.CompilerParams(vmem_limit_bytes=40 * 1024 * 1024),
        )(*ins)

    def swap(x):
        return lax.ppermute(x, "mem", [(i, i ^ 1) for i in range(n_mem)])

    def along(x, shift):
        return lax.ppermute(x, "gx", [(i, (i + shift) % n_gx) for i in range(n_gx)])

    def across(x):
        def place(chip, core, j, i):
            return ((2 * chip + core) * n_gy + j) * n_gx + i

        first = [0 if j < n_gy // 2 else 1 for j in range(n_gy)]
        pairs = []
        for chip in range(n_mem // 2):
            for j in range(n_gy - 1):
                for i in range(n_gx):
                    a = place(chip, 1 - first[j], j, i)
                    b = place(chip, first[j + 1], j + 1, i)
                    pairs += [(a, b), (b, a)]
        return lax.ppermute(x, AXES, pairs)

    increment, members, zonal_diff, merid_diff, sea_mask = (
        in_hbm(x) for x in (increment, members, zonal_diff, merid_diff, sea_mask)
    )
    sent = call(
        partner_rows_kernel, [members], [HBM], kept(levels, tiles, tall, LANES), [pltpu.SemaphoreType.DMA((tiles,))]
    )
    other = pinned(swap(sent))
    local = call(
        load_kernel,
        [members, increment, zonal_diff, merid_diff, sea_mask],
        [HBM] * 5,
        [kept(levels, tiles, tall, LANES)] * 2 + [kept(tiles, tall, LANES)] * 3,
        [pltpu.VMEM((tiles, tall, LANES), jnp.int32), pltpu.SemaphoreType.DMA((5, tiles))],
    )
    local = [pinned(x) for x in local]
    local = [local[0], other] + local[1:]
    strip = call(pack_rows_kernel, local, [VMEM] * 6, kept(levels + 2, tiles, TILE, LANES))
    strip = pinned(across(strip).reshape((levels + 2) * tiles * TILE, LANES))
    turned = [kept(planes + 2, DEPTH, LANES)] * 6 + [kept(4 * planes, LANES)] * 2
    state = call(
        prepare_kernel,
        local,
        [VMEM] * 6,
        turned,
        [pltpu.VMEM((2 * levels * tiles * full, LANES), F32), pltpu.VMEM((3 * tiles * full, LANES), F32)],
    )
    state = call(
        halo_rows_kernel,
        [strip] + [pinned(x) for x in state],
        [VMEM] * 9,
        turned,
        aliases={k + 1: k for k in range(8)},
    )
    from_west = pinned(along(state[7], 1))
    from_east = pinned(along(state[6], -1))
    mine = call(
        diffuse_kernel,
        [from_east, from_west] + local[:2] + [pinned(x) for x in state[:6]],
        [VMEM] * 10,
        turned[:6] + [kept(levels, tiles, mid, LANES)],
        [
            pltpu.VMEM((planes + 2, DEPTH, LANES), F32),
            pltpu.VMEM((2 * levels * tiles * full, LANES), F32),
        ],
        aliases={k + 4: k for k in range(6)},
    )[6]
    if n_mem > 2:
        mine = lax.psum(mine, "mem", axis_index_groups=[list(range(k, n_mem, 2)) for k in range(2)])
    theirs = swap(mine)
    return call(
        join_kernel,
        [pinned(mine), pinned(theirs)],
        [VMEM] * 2,
        jax.ShapeDtypeStruct(increment.shape, F32),
        [pltpu.SemaphoreType.DMA((2, tiles))],
        HBM,
    )


def solution(mesh):
    return jax.shard_map(
        functools.partial(shards, tuple(mesh.shape[axis] for axis in AXES)),
        mesh=mesh,
        in_specs=(
            P(None, "gy", "gx"),
            P("mem", None, "gy", "gx"),
            P("gy", "gx"),
            P("gy", "gx"),
            P("gy", "gx"),
        ),
        out_specs=P(None, "gy", "gx"),
        check_vma=False,
    )
```

```python
import functools
import jax
import jax.numpy as jnp
from jax import lax
from jax.experimental import pallas as pl
from jax.experimental.pallas import tpu as pltpu
from jax.sharding import PartitionSpec as P

STEPS = 4
TILE = 8
LANES = 128
AXES = ("mem", "gy", "gx")
F32 = jnp.float32
VMEM = pl.BlockSpec(memory_space=pltpu.VMEM)
HBM = pl.BlockSpec(memory_space=pltpu.HBM)

BODY = slice(TILE, TILE + LANES)
DEPTH = LANES + 2 * TILE
GROUP = 32


def half_of(gy_size):
    core = lax.rem(lax.axis_index("mem"), 2)
    later = (lax.axis_index("gy") >= gy_size // 2).astype(jnp.int32)
    return lax.rem(core + later, 2)


def kept(*shape):
    return pltpu.VMEM(shape, F32)


def pinned(x):
    return pltpu.with_memory_space_constraint(x, pltpu.VMEM)


def in_hbm(x):
    return pltpu.with_memory_space_constraint(x, pltpu.HBM)


def tile(c):
    return slice(c * LANES, (c + 1) * LANES)


def lane_ids(rows):
    return lax.broadcasted_iota(jnp.int32, (rows, LANES), 1)


def row_ids(rows, width):
    return lax.broadcasted_iota(jnp.int32, (rows, width), 0)


def aligned(start):
    return pl.multiple_of(start, TILE)


def run(copies):
    for copy in copies:
        copy.start()
    for copy in copies:
        copy.wait()


def edge_kernel(gy_size, members, increment, zonal, merid, mask, sent, own, forcing, coef, mask_buf, sems):
    rows = increment.shape[1]
    half = half_of(gy_size)
    outer = pl.ds(aligned(half * (rows - TILE)), TILE)
    other = pl.ds(aligned((1 - half) * (rows - TILE)), TILE)
    run([
        pltpu.make_async_copy(members.at[0, :, other, :], sent, sems.at[0]),
        pltpu.make_async_copy(members.at[0, :, outer, :], own, sems.at[1]),
        pltpu.make_async_copy(increment.at[:, outer, :], forcing, sems.at[2]),
        pltpu.make_async_copy(zonal.at[outer, :], coef.at[0], sems.at[3]),
        pltpu.make_async_copy(merid.at[outer, :], coef.at[1], sems.at[4]),
        pltpu.make_async_copy(mask.at[outer, :], mask_buf, sems.at[5]),
    ])
    wet = mask_buf[...].astype(F32)
    coef[0] = coef[0] * wet
    coef[1] = coef[1] * wet
    coef[2] = wet
    forcing[...] = forcing[...] * wet[None]


def pack_rows_kernel(gy_size, own, other, forcing, coef, strip):
    levels, _, width = own.shape
    half = half_of(gy_size)
    j = lax.axis_index("gy")
    same_core = jnp.where(half == 0, j == gy_size // 2, j == gy_size // 2 - 1)
    low = row_ids(TILE, width) < TILE // 2

    def put(place, first, second):
        first = jnp.where(half == 0, first, pltpu.roll(first, TILE // 2, 0))
        second = jnp.where(half == 0, pltpu.roll(second, TILE // 2, 0), second)
        strip[place] = jnp.where(low, first, second)

    for level in range(levels):
        mine = own[level] * forcing[level]
        theirs = other[level] * forcing[level]
        put(level, jnp.where(same_core, mine, theirs), jnp.where(same_core, theirs, mine))
    put(levels, coef[0], coef[1])
    put(levels + 1, coef[2], coef[2])


def received(half, strip, place, cols):
    value = strip[place // 2, :, cols]
    natural = jnp.equal(half, 1 - place % 2)
    return jnp.where(natural, value, pltpu.roll(value, TILE // 2, 0))


def edge_columns(first, last):
    rows = first[0].shape[0]
    lane = lane_ids(rows)
    total = jnp.zeros((rows, LANES), F32)
    for level, (a, b) in enumerate(zip(first, last)):
        base = GROUP * level
        total = jnp.where((lane >= base + 8) & (lane < base + 16), pltpu.roll(a, base + 8, 1), total)
        total = jnp.where((lane >= base + 16) & (lane < base + 24), pltpu.roll(b, (base + 16 - 120) % LANES, 1), total)
    return total


def spread(value):
    value = value + pltpu.roll(value, GROUP, 1)
    return value + pltpu.roll(value, 2 * GROUP, 1)


def edge_coefficient(first, last):
    rows = first.shape[0]
    lane = lane_ids(rows)
    total = jnp.where((lane >= 8) & (lane < 16), pltpu.roll(first, 8, 1), 0.0)
    return spread(jnp.where((lane >= 16) & (lane < 24), pltpu.roll(last, 24, 1), total))


def outgoing(fields, coefs, west):
    rows = coefs[0].shape[0]
    lane = lane_ids(rows)
    start, step, source = (24, -4, 0) if west else (4, 4, 124)
    total = jnp.zeros((rows, LANES), F32)
    for k, value in enumerate(coefs):
        at = start + step * (k + 2)
        total = jnp.where((lane >= at) & (lane < at + 4), pltpu.roll(value, (at - source) % LANES, 1), total)
    total = spread(total)
    for k, member in enumerate(fields):
        for level, value in enumerate(member):
            at = GROUP * level + start + step * k
            total = jnp.where((lane >= at) & (lane < at + 4), pltpu.roll(value, (at - source) % LANES, 1), total)
    return total


def turn(ref, start, stride):
    return jnp.concatenate([ref[pl.ds(s, TILE, stride=stride), :] for s in start], axis=0).T


def refresh(ref, first, count):
    flat = ref.reshape(ref.shape[0] * DEPTH, LANES)

    def rows(j):
        return pl.ds(first * DEPTH + TILE + j, count, stride=DEPTH)

    flat[rows(-1), :] = pltpu.roll(flat[rows(LANES - 1), :], 1, 1)
    flat[rows(LANES), :] = pltpu.roll(flat[rows(0), :], LANES - 1, 1)


def sweep(source, target, east, north, first, last):
    refresh(source, first, last - first + 1)
    for start in range(TILE, TILE + LANES, TILE):
        at, ahead, behind = (slice(start + d, start + d + TILE) for d in (0, 1, -1))
        here = source[first, at, :]
        south = north[first - 1, at, :] * (here - source[first - 1, at, :])
        for p in range(first, last + 1):
            above = source[p + 1, at, :]
            flux = north[p, at, :] * (above - here)
            go_east = east[p, at, :] * (source[p, ahead, :] - here)
            go_west = east[p, behind, :] * (here - source[p, behind, :])
            target[p, at, :] = here + go_east - go_west + flux - south
            here, south = above, flux


def faces(zm, mm, wet, cols, width, rows):
    after = slice(cols.start + LANES, cols.stop + LANES) if cols.stop < width else cols
    lane = lane_ids(rows)
    here = pltpu.roll(wet[:rows, cols], LANES - 1, 1)
    beyond = pltpu.roll(wet[:rows, after], LANES - 1, 1)
    east = zm[:, cols] * jnp.where(lane == LANES - 1, beyond, here)
    north = mm[:, cols] * wet[1 : rows + 1, cols]
    return east, north


def interior_kernel(
    gy_size, members, others, increment, zonal, merid, mask,
    out, pack_own, pack_other, pack_coef, weight_own, weight_other, west_out, east_out,
    zm, mm, wet, field, face, u, u_next, east, north, result,
):
    _, levels, rows, width = members.shape
    tiles = width // LANES
    mid = rows // 2
    tall = mid + TILE
    offset = tall - 3 * TILE
    planes = tall - offset
    half = half_of(gy_size)
    part = pl.ds(aligned(half * (mid - TILE)), tall)
    wet[:tall, :] = mask[part, :].astype(F32)
    wet[tall:, :] = jnp.zeros((TILE, width), F32)
    zm[...] = zonal[part, :] * wet[:tall, :]
    mm[...] = merid[part, :] * wet[:tall, :]
    sources = (members, others)
    for c in range(tiles):
        cols = tile(c)
        face[pl.ds(c * tall, tall), :], face[pl.ds((tiles + c) * tall, tall), :] = faces(zm, mm, wet, cols, width, tall)
        for level in range(levels):
            force = increment[level, part, cols] * wet[:tall, cols]
            for k, member in enumerate(sources):
                field[pl.ds(((2 * level + k) * tiles + c) * tall, tall), :] = member[0, level, part, cols] * force

    def at(f, c):
        return field[pl.ds((f * tiles + c) * tall, tall), :]

    ends = (tile(0), tile(tiles - 1))
    lead = pl.ds(aligned((1 - half) * TILE), tall)
    for k, pack in enumerate((pack_own, pack_other)):
        pack[lead, :] = edge_columns(*([at(2 * level + k, c) for level in range(levels)] for c in (0, tiles - 1)))
    for k, ref in enumerate((zm, mm, wet)):
        pack_coef[k, lead, :] = edge_coefficient(*(ref[:tall, cols] for cols in ends))
    keep = pl.ds(aligned(half * mid), mid)
    for member, weight in zip(sources, (weight_own, weight_other)):
        weight[...] = edge_columns(*([member[0, level, keep, cols] for level in range(levels)] for cols in ends))
    for out_strip, c, west in ((west_out, 0, True), (east_out, tiles - 1, False)):
        out_strip[lead, :] = outgoing(
            [[at(2 * level + k, c) for level in range(levels)] for k in range(2)],
            [ref[:tall, tile(c)] for ref in (zm, mm, wet)],
            west,
        )

    fields = range(2 * levels)
    for q in range(planes):
        u[q, BODY, :] = turn(field, [f * tiles * tall + ch * offset + q for f in fields for ch in range(2)], tall)
        for k, ref in enumerate((east, north)):
            ref[q, BODY, :] = turn(face, [k * tiles * tall + ch * offset + q for f in fields for ch in range(2)], tall)
    refresh(east, 0, planes)
    source, target = u, u_next
    for step in range(STEPS):
        sweep(source, target, east, north, step + 1, planes - 2 - step)
        source, target = target, source
    for q in range(STEPS, planes - STEPS):
        flat = source[q, BODY, :].T
        for f in fields:
            for ch in range(2):
                group = (2 * f + ch) * tiles
                result[pl.ds(f * tiles * tall + ch * offset + q, tiles, stride=tall), :] = flat[group : group + tiles]
    for level in range(levels):
        for c in range(tiles):
            a, b = (
                result[pl.ds(aligned(((2 * level + k) * tiles + c) * tall + half * TILE), mid), :] for k in range(2)
            )
            out[level, :, tile(c)] = members[0, level, keep, tile(c)] * a + others[0, level, keep, tile(c)] * b


def halo_columns_kernel(gy_size, strip, west_in, east_in, west_out, east_out):
    levels = strip.shape[0] - 2
    width = strip.shape[2]
    half = half_of(gy_size)
    full = west_out.shape[0]
    halo = pl.ds(aligned(half * (full - TILE)), TILE)
    main = pl.ds(aligned((1 - half) * TILE), full - TILE)
    for source, out, cols, west in (
        (west_in, west_out, slice(0, LANES), True),
        (east_in, east_out, slice(width - LANES, width), False),
    ):
        out[main, :] = source[main, :]
        out[halo, :] = outgoing(
            [[received(half, strip, 2 * level + k, cols) for level in range(levels)] for k in range(2)],
            [received(half, strip, 2 * levels + k, cols) for k in range(3)],
            west,
        )


def outer_rows_kernel(
    gy_size, strip, own, other, forcing, coef, pack_own, pack_other, pack_coef,
    sums, full_own, full_other, full_coef,
    zm, mm, wet, field, face, u, u_next, east, north, result,
):
    levels, _, width = own.shape
    tiles = width // LANES
    half = half_of(gy_size)
    edge = pl.ds(aligned((1 - half) * TILE), TILE)
    halo = pl.ds(aligned(half * TILE), TILE)
    block = 2 * TILE
    every = slice(0, width)
    for k, ref in enumerate((zm, mm, wet)):
        ref[edge, :] = coef[k]
        ref[halo, :] = received(half, strip, 2 * levels + k, every)
    wet[block:, :] = jnp.zeros((TILE, width), F32)
    for c in range(tiles):
        cols = tile(c)
        face[pl.ds(c * block, block), :], face[pl.ds((tiles + c) * block, block), :] = faces(zm, mm, wet, cols, width, block)
        for level in range(levels):
            for k, member in enumerate((own, other)):
                base = ((2 * level + k) * tiles + c) * block
                field[pl.ds(aligned(base + (1 - half) * TILE), TILE), :] = member[level, :, cols] * forcing[level, :, cols]
                field[pl.ds(aligned(base + half * TILE), TILE), :] = received(half, strip, 2 * level + k, cols)

    fields = range(2 * levels)
    planes = 10
    lead = (1 - half) * 4
    for q in range(planes):
        u[q, BODY, :] = turn(field, [f * tiles * block + 2 * ch + q + lead for f in fields for ch in range(2)], block)
        for k, ref in enumerate((east, north)):
            ref[q, BODY, :] = turn(face, [k * tiles * block + 2 * ch + q + lead for f in fields for ch in range(2)], block)
    refresh(east, 0, planes)
    source, target = u, u_next
    for step in range(STEPS):
        sweep(source, target, east, north, step + 1, planes - 2 - step)
        source, target = target, source
    for p in range(2):
        flat = source[STEPS + p, BODY, :].T
        for f in fields:
            for ch in range(2):
                group = (2 * f + ch) * tiles
                result[pl.ds(f * tiles * TILE + 4 * half + 2 * ch + p, tiles, stride=TILE), :] = flat[group : group + tiles]
    natural = row_ids(TILE, LANES) // 4 == half
    for c in range(tiles):
        cols = tile(c)
        terms = []
        for level in range(levels):
            a, b = (result[pl.ds(((2 * level + k) * tiles + c) * TILE, TILE), :] for k in range(2))
            terms.append(own[level, :, cols] * a + other[level, :, cols] * b)
        for pair in range(levels // 2):
            sums[pl.ds((c * levels // 2 + pair) * TILE, TILE), :] = jnp.where(
                natural, terms[2 * pair], pltpu.roll(terms[2 * pair + 1], 4, 0)
            )

    full = full_own.shape[0]
    main = pl.ds(aligned((1 - half) * TILE), full - TILE)
    beyond = pl.ds(aligned(half * (full - TILE)), TILE)
    ends = (slice(0, LANES), slice(width - LANES, width))
    for k, (source, out) in enumerate(((pack_own, full_own), (pack_other, full_other))):
        out[main, :] = source[main, :]
        out[beyond, :] = edge_columns(
            *([received(half, strip, 2 * level + k, cols) for level in range(levels)] for cols in ends)
        )
    for k in range(3):
        full_coef[k, main, :] = pack_coef[k, main, :]
        full_coef[k, beyond, :] = edge_coefficient(*(received(half, strip, 2 * levels + k, cols) for cols in ends))


def end_columns_kernel(
    gy_size, from_west, from_east, own, other, coef, weight_own, weight_other, sums, out,
    a, b, a_next, b_next, east, north, wet,
):
    full = own.shape[0]
    body = pl.ds(TILE, full)
    place = lane_ids(full) % GROUP
    on_west = (place >= 4) & (place < 8)
    on_east = (place >= 24) & (place < 28)
    west, east_strip = from_west[...], from_east[...]

    def with_ends(value, k):
        value = jnp.where(on_west, pltpu.roll(west, (-4 * k) % LANES, 1), value)
        return jnp.where(on_east, pltpu.roll(east_strip, 4 * k, 1), value)

    blank = jnp.zeros((TILE, LANES), F32)
    for ref in (a, b, a_next, b_next, east, north, wet):
        ref[:TILE, :] = blank
        ref[full + TILE :, :] = blank
    a[body, :] = with_ends(own[...], 0)
    b[body, :] = with_ends(other[...], 1)
    wet[body, :] = with_ends(coef[2], 4)
    east[body, :] = with_ends(coef[0], 2) * pltpu.roll(wet[body, :], LANES - 1, 1)
    north[body, :] = with_ends(coef[1], 3) * wet[pl.ds(TILE + 1, full), :]
    now, later = (a, b), (a_next, b_next)
    for step in range(STEPS):
        for t in range(TILE, full + TILE, TILE):
            at, above, below = (pl.ds(t + d, TILE) for d in (0, 1, -1))
            e, n, s = east[at, :], north[at, :], north[below, :]
            for source, target in zip(now, later):
                here = source[at, :]
                flux = e * (pltpu.roll(here, LANES - 1, 1) - here)
                go_north = n * (source[above, :] - here)
                go_south = s * (here - source[below, :])
                target[at, :] = here + flux - pltpu.roll(flux, 1, 1) + go_north - go_south
        now, later = later, now
    mid = weight_own.shape[0]
    rows = pl.ds(2 * TILE, mid)
    out[:mid, :] = weight_own[...] * now[0][rows, :] + weight_other[...] * now[1][rows, :]
    out[mid:, :] = sums[...]


def join_kernel(gy_size, mine_in, theirs_in, mine_edge, theirs_edge, mine, theirs, out, sems):
    half = half_of(gy_size)
    levels, mid, width = mine.shape
    tiles = width // LANES
    lane = lane_ids(mid)
    copies = []
    for k, (ref, edges, where) in enumerate(((mine, mine_edge, half), (theirs, theirs_edge, 1 - half))):
        outer = pl.ds(aligned(where * (mid - TILE)), TILE)
        natural = row_ids(TILE, LANES) // 4 == where
        for level in range(levels):
            for c in range(tiles):
                value = edges[pl.ds(mid + (c * levels // 2 + level // 2) * TILE, TILE), :]
                if level % 2:
                    value = pltpu.roll(value, 4, 0)
                ref[level, outer, tile(c)] = jnp.where(natural, value, ref[level, outer, tile(c)])
            first, last = tile(0), tile(tiles - 1)
            base = GROUP * level
            packed = edges[:mid, :]
            ref[level, :, first] = jnp.where(lane < 4, pltpu.roll(packed, (-base - 8) % LANES, 1), ref[level, :, first])
            ref[level, :, last] = jnp.where(
                lane >= LANES - 4, pltpu.roll(packed, (LANES - 4 - base - 20) % LANES, 1), ref[level, :, last]
            )
            copies.append(
                pltpu.make_async_copy(
                    ref.at[level], out.at[level, pl.ds(aligned(where * mid), mid), :], sems.at[k, level]
                )
            )
            copies[-1].start()
    for copy in copies:
        copy.wait()


def shards(sizes, increment, members, zonal_diff, merid_diff, sea_mask):
    n_mem, n_gy, n_gx = sizes
    levels, rows, width = increment.shape
    tiles = width // LANES
    mid = rows // 2
    tall = mid + TILE
    full = tall + TILE
    planes = 3 * TILE
    assert tiles == TILE and 4 * levels * tiles == LANES and tall == 5 * TILE and n_mem % 2 == 0

    def call(kernel, ins, specs, outs, scratch=(), out_specs=None, aliases={}):
        return pl.pallas_call(
            functools.partial(kernel, n_gy),
            out_shape=outs,
            in_specs=specs,
            out_specs=out_specs if out_specs is not None else jax.tree.map(lambda _: VMEM, outs),
            scratch_shapes=scratch,
            input_output_aliases=aliases,
            compiler_params=pltpu.CompilerParams(vmem_limit_bytes=40 * 1024 * 1024),
        )(*ins)

    def held(kernel, ins, outs, scratch=(), **kw):
        got = call(kernel, [pinned(x) for x in ins], [VMEM] * len(ins), outs, scratch, **kw)
        return got

    def swap(x):
        return lax.ppermute(x, "mem", [(i, i ^ 1) for i in range(n_mem)])

    def along(x, shift):
        return lax.ppermute(x, "gx", [(i, (i + shift) % n_gx) for i in range(n_gx)])

    def across(x):
        def place(chip, core, j, i):
            return ((2 * chip + core) * n_gy + j) * n_gx + i

        first = [0 if j < n_gy // 2 else 1 for j in range(n_gy)]
        pairs = []
        for chip in range(n_mem // 2):
            for j in range(n_gy - 1):
                for i in range(n_gx):
                    a = place(chip, 1 - first[j], j, i)
                    b = place(chip, first[j + 1], j + 1, i)
                    pairs += [(a, b), (b, a)]
        return lax.ppermute(x, AXES, pairs)

    def scratch(*shape):
        return pltpu.VMEM(shape, F32)

    arrays = [members, increment, zonal_diff, merid_diff, sea_mask]
    sent, own, forcing, coef = call(
        edge_kernel,
        [in_hbm(x) for x in arrays],
        [HBM] * 5,
        [kept(levels, TILE, width)] * 3 + [kept(3, TILE, width)],
        [pltpu.VMEM((TILE, width), jnp.int32), pltpu.SemaphoreType.DMA((6,))],
    )
    other = swap(sent)
    members_later, other = lax.optimization_barrier((members, other))
    others = swap(members_later)
    strip = held(pack_rows_kernel, [own, other, forcing, coef], kept(levels + 2, TILE, width))
    zonal_later, strip = lax.optimization_barrier((zonal_diff, strip))
    strip = across(strip)

    end = kept(full, LANES)
    inside, pack_own, pack_other, pack_coef, weight_own, weight_other, west, east = held(
        interior_kernel,
        [members, others, increment, zonal_later, merid_diff, sea_mask],
        [kept(levels, mid, width), end, end, kept(3, full, LANES), kept(mid, LANES), kept(mid, LANES), end, end],
        [
            scratch(tall, width),
            scratch(tall, width),
            scratch(full, width),
            scratch(2 * levels * tiles * tall, LANES),
            scratch(2 * tiles * tall, LANES),
            scratch(planes, DEPTH, LANES),
            scratch(planes, DEPTH, LANES),
            scratch(planes, DEPTH, LANES),
            scratch(planes, DEPTH, LANES),
            scratch(2 * levels * tiles * tall, LANES),
        ],
    )
    west, east = held(halo_columns_kernel, [strip, west, east], [end, end])
    inside, west, east = lax.optimization_barrier((inside, west, east))
    from_west = along(east, 1)
    from_east = along(west, -1)
    sums, full_own, full_other, full_coef = held(
        outer_rows_kernel,
        [strip, own, other, forcing, coef, pack_own, pack_other, pack_coef],
        [kept(levels // 2 * tiles * TILE, LANES), end, end, kept(3, full, LANES)],
        [
            scratch(2 * TILE, width),
            scratch(2 * TILE, width),
            scratch(3 * TILE, width),
            scratch(2 * levels * tiles * 2 * TILE, LANES),
            scratch(2 * tiles * 2 * TILE, LANES),
            scratch(10, DEPTH, LANES),
            scratch(10, DEPTH, LANES),
            scratch(10, DEPTH, LANES),
            scratch(10, DEPTH, LANES),
            scratch(2 * levels * tiles * TILE, LANES),
        ],
    )
    edges = held(
        end_columns_kernel,
        [from_west, from_east, full_own, full_other, full_coef, weight_own, weight_other, sums],
        kept(mid + levels // 2 * tiles * TILE, LANES),
        [scratch(full + 2 * TILE, LANES)] * 7,
    )
    if n_mem > 2:
        groups = [list(range(k, n_mem, 2)) for k in range(2)]
        inside, edges = (lax.psum(x, "mem", axis_index_groups=groups) for x in (inside, edges))
    inside_theirs, edges_theirs = swap(inside), swap(edges)
    return held(
        join_kernel,
        [inside, inside_theirs, edges, edges_theirs],
        [kept(levels, mid, width)] * 2 + [jax.ShapeDtypeStruct(increment.shape, F32)],
        [pltpu.SemaphoreType.DMA((2, levels))],
        out_specs=[VMEM, VMEM, HBM],
        aliases={0: 0, 1: 1},
    )[2]


def solution(mesh):
    return jax.shard_map(
        functools.partial(shards, tuple(mesh.shape[axis] for axis in AXES)),
        mesh=mesh,
        in_specs=(
            P(None, "gy", "gx"),
            P("mem", None, "gy", "gx"),
            P("gy", "gx"),
            P("gy", "gx"),
            P("gy", "gx"),
        ),
        out_specs=P(None, "gy", "gx"),
        check_vma=False,
    )
```

```python
import functools
import jax
import jax.numpy as jnp
from jax import lax
from jax.experimental import pallas as pl
from jax.experimental.pallas import tpu as pltpu
from jax.sharding import PartitionSpec as P

STEPS = 4
TILE = 8
LANES = 128
AXES = ("mem", "gy", "gx")
F32 = jnp.float32
VMEM = pl.BlockSpec(memory_space=pltpu.VMEM)
HBM = pl.BlockSpec(memory_space=pltpu.HBM)

BODY = slice(TILE, TILE + LANES)
DEPTH = LANES + 2 * TILE
GROUP = 32


def half_of(gy_size):
    core = lax.rem(lax.axis_index("mem"), 2)
    later = (lax.axis_index("gy") >= gy_size // 2).astype(jnp.int32)
    return lax.rem(core + later, 2)


def kept(*shape):
    return pltpu.VMEM(shape, F32)


def pinned(x):
    return pltpu.with_memory_space_constraint(x, pltpu.VMEM)


def in_hbm(x):
    return pltpu.with_memory_space_constraint(x, pltpu.HBM)


def tile(c):
    return slice(c * LANES, (c + 1) * LANES)


def lane_ids(rows):
    return lax.broadcasted_iota(jnp.int32, (rows, LANES), 1)


def row_ids(rows, width):
    return lax.broadcasted_iota(jnp.int32, (rows, width), 0)


def aligned(start):
    return pl.multiple_of(start, TILE)


def run(copies):
    for copy in copies:
        copy.start()
    for copy in copies:
        copy.wait()


def pack_coefficients(half, coef, out):
    width = out.shape[1]
    zm, mm, wet = coef[0], coef[1], coef[2]
    row = row_ids(TILE, width)
    col = lax.broadcasted_iota(jnp.int32, (TILE, width), 1)
    east = zm * jnp.where(col == width - 1, 1.0, pltpu.roll(wet, width - 1, 1))
    north = mm * jnp.where(row == TILE - 1, 1.0, pltpu.roll(wet, TILE - 1, 0))
    upper = jnp.where(row < 4, north, pltpu.roll(east, 4, 0))
    upper = jnp.where(row == 3, pltpu.roll(wet, 3, 0), upper)
    lower = jnp.where(row < 4, pltpu.roll(north, 4, 0), east)
    out[...] = jnp.where(half == 0, upper, lower)
    first = wet[:, :LANES]
    lane, line = lane_ids(TILE), row_ids(TILE, LANES)
    value = out[:, :LANES]
    for r in range(4):
        moved = jnp.where(half == 0, pltpu.roll(first, 7 - r, 0), pltpu.roll(first, (-r) % TILE, 0))
        value = jnp.where((line == jnp.where(half == 0, 7, 4)) & (lane == r), pltpu.roll(moved, r, 1), value)
    out[:, :LANES] = value


def pack_rows_kernel(gy_size, own, others, forcing, weights, strip, other):
    levels, tall, width = own.shape
    half = half_of(gy_size)
    outer = pl.ds(aligned(half * (tall - TILE)), TILE)
    other[...] = others[0, :, pl.ds(aligned(half * (others.shape[2] - TILE)), TILE), :]
    j = lax.axis_index("gy")
    same_core = jnp.where(half == 0, j == gy_size // 2, j == gy_size // 2 - 1)
    low = row_ids(TILE, width) < TILE // 2
    for level in range(levels):
        force = forcing[level, outer, :]
        mine = own[level, outer, :] * force
        theirs = other[level] * force
        first, second = jnp.where(same_core, mine, theirs), jnp.where(same_core, theirs, mine)
        first = jnp.where(half == 0, first, pltpu.roll(first, TILE // 2, 0))
        second = jnp.where(half == 0, pltpu.roll(second, TILE // 2, 0), second)
        strip[level] = jnp.where(low, first, second)
    strip[levels] = weights[...]


def inside_domain(gy_size):
    half, j = half_of(gy_size), lax.axis_index("gy")
    return jnp.where(half == 0, j > 0, j < gy_size - 1)


def beyond(value, real):
    return jnp.where(real, value, 0.0)


def received(gy_size, strip, place, cols):
    value = strip[place // 2, :, cols]
    natural = jnp.equal(half_of(gy_size), 1 - place % 2)
    return beyond(jnp.where(natural, value, pltpu.roll(value, TILE // 2, 0)), inside_domain(gy_size))


def received_coefficients(gy_size, strip, cols):
    half, real = half_of(gy_size), inside_domain(gy_size)
    value = strip[strip.shape[0] - 1, :, cols]
    moved = pltpu.roll(value, TILE // 2, 0)
    zm = jnp.where(half == 0, value, moved)
    mm = jnp.where(half == 0, moved, value)
    row = row_ids(*value.shape)
    wet = jnp.where((half == 1) & (row == 0), pltpu.roll(value, 5, 0), 1.0)
    if cols.start == 0:
        lane, line = lane_ids(TILE), row_ids(TILE, LANES)
        first = value[:, :LANES]
        column = wet[:, :LANES]
        for r in range(4):
            shifted = jnp.where(half == 0, pltpu.roll(first, r, 0), pltpu.roll(first, (r + 1) % TILE, 0))
            at = (line == jnp.where(half == 0, 4 + r, r)) & (lane == 0)
            column = jnp.where(at, pltpu.roll(shifted, (-r) % LANES, 1), column)
        wet = jnp.concatenate([column, wet[:, LANES:]], axis=1) if value.shape[1] > LANES else column
    return [beyond(x, real) for x in (zm, mm, wet)]


def edge_columns(first, last):
    rows = first[0].shape[0]
    lane = lane_ids(rows)
    total = jnp.zeros((rows, LANES), F32)
    for level, (a, b) in enumerate(zip(first, last)):
        base = GROUP * level
        total = jnp.where((lane >= base + 8) & (lane < base + 16), pltpu.roll(a, base + 8, 1), total)
        total = jnp.where((lane >= base + 16) & (lane < base + 24), pltpu.roll(b, (base + 16 - 120) % LANES, 1), total)
    return total


def spread(value):
    value = value + pltpu.roll(value, GROUP, 1)
    return value + pltpu.roll(value, 2 * GROUP, 1)


def edge_coefficient(first, last):
    rows = first.shape[0]
    lane = lane_ids(rows)
    total = jnp.where((lane >= 8) & (lane < 16), pltpu.roll(first, 8, 1), 0.0)
    return spread(jnp.where((lane >= 16) & (lane < 24), pltpu.roll(last, 24, 1), total))


def outgoing_lanes(west):
    return (24, -4, 0) if west else (4, 4, 124)


def outgoing_coefficients(coefs, west):
    start, step, source = outgoing_lanes(west)
    lane = lane_ids(coefs[0].shape[0])
    total = jnp.zeros(lane.shape, F32)
    for k, value in enumerate(coefs):
        at = start + step * (k + 2)
        total = jnp.where((lane >= at) & (lane < at + 4), pltpu.roll(value, (at - source) % LANES, 1), total)
    return spread(total)


def outgoing(fields, total, west):
    start, step, source = outgoing_lanes(west)
    lane = lane_ids(total.shape[0])
    for k, member in enumerate(fields):
        for level, value in enumerate(member):
            at = GROUP * level + start + step * k
            total = jnp.where((lane >= at) & (lane < at + 4), pltpu.roll(value, (at - source) % LANES, 1), total)
    return total


def turn(ref, start, stride):
    return jnp.concatenate([ref[pl.ds(s, TILE, stride=stride), :] for s in start], axis=0).T


def refresh(ref, first, count):
    flat = ref.reshape(ref.shape[0] * DEPTH, LANES)

    def rows(j):
        return pl.ds(first * DEPTH + TILE + j, count, stride=DEPTH)

    flat[rows(-1), :] = pltpu.roll(flat[rows(LANES - 1), :], 1, 1)
    flat[rows(LANES), :] = pltpu.roll(flat[rows(0), :], LANES - 1, 1)


def sweep(source, target, east, north, first, last):
    refresh(source, first, last - first + 1)
    for start in range(TILE, TILE + LANES, TILE):
        at, ahead, behind = (slice(start + d, start + d + TILE) for d in (0, 1, -1))
        here = source[first, at, :]
        south = north[first - 1, at, :] * (here - source[first - 1, at, :])
        for p in range(first, last + 1):
            above = source[p + 1, at, :]
            flux = north[p, at, :] * (above - here)
            go_east = east[p, at, :] * (source[p, ahead, :] - here)
            go_west = east[p, behind, :] * (here - source[p, behind, :])
            target[p, at, :] = here + go_east - go_west + flux - south
            here, south = above, flux


def faces(zm, mm, wet, cols, width, rows):
    after = slice(cols.start + LANES, cols.stop + LANES) if cols.stop < width else cols
    lane = lane_ids(rows)
    here = pltpu.roll(wet[:rows, cols], LANES - 1, 1)
    beyond = pltpu.roll(wet[:rows, after], LANES - 1, 1)
    east = zm[:, cols] * jnp.where(lane == LANES - 1, beyond, here)
    north = mm[:, cols] * wet[1 : rows + 1, cols]
    return east, north


def load_kernel(
    gy_size, members, increment, zonal, merid, mask,
    own, forcing, coef, weights, east, north, pack_coef, west_out, east_out,
    mask_buf, zm, mm, wet, face, sems,
):
    _, tall, width = own.shape
    tiles = width // LANES
    planes = east.shape[0]
    offset = tall - planes
    half = half_of(gy_size)
    part = pl.ds(aligned(half * (tall - 2 * TILE)), tall)
    small = [
        pltpu.make_async_copy(mask.at[part, :], mask_buf, sems.at[0]),
        pltpu.make_async_copy(zonal.at[part, :], zm, sems.at[1]),
        pltpu.make_async_copy(merid.at[part, :], mm, sems.at[2]),
    ]
    large = [
        pltpu.make_async_copy(increment.at[:, part, :], forcing, sems.at[3]),
        pltpu.make_async_copy(members.at[0, :, part, :], own, sems.at[4]),
    ]
    for copy in small + large:
        copy.start()
    for copy in small:
        copy.wait()
    wet[:tall, :] = mask_buf[...].astype(F32)
    wet[tall:, :] = jnp.zeros((TILE, width), F32)
    zm[...] = zm[...] * wet[:tall, :]
    mm[...] = mm[...] * wet[:tall, :]
    outer = pl.ds(aligned(half * (tall - TILE)), TILE)
    for k, ref in enumerate((zm, mm, wet)):
        coef[k] = ref[outer, :]
    pack_coefficients(half, coef, weights)
    for c in range(tiles):
        face[pl.ds(c * tall, tall), :], face[pl.ds((tiles + c) * tall, tall), :] = faces(zm, mm, wet, tile(c), width, tall)
    for q in range(planes):
        for k, ref in enumerate((east, north)):
            ref[q, BODY, :] = turn(face, [k * tiles * tall + ch * offset + q for _ in range(TILE) for ch in range(2)], tall)
    refresh(east, 0, planes)
    lead = pl.ds(aligned((1 - half) * TILE), tall)
    ends = (tile(0), tile(tiles - 1))
    for k, ref in enumerate((zm, mm, wet)):
        pack_coef[k, lead, :] = edge_coefficient(*(ref[:tall, cols] for cols in ends))
    for out_strip, c, west in ((west_out, 0, True), (east_out, tiles - 1, False)):
        out_strip[lead, :] = outgoing_coefficients([ref[:tall, tile(c)] for ref in (zm, mm, wet)], west)
    large[0].wait()
    forcing[...] = forcing[...] * wet[:tall, :][None]
    large[1].wait()


def interior_kernel(
    gy_size, own, others, forcing, east, north, west_in, east_in,
    out, pack_own, pack_other, weight_own, weight_other, west_out, east_out,
    field, u, u_next, result,
):
    levels, tall, width = own.shape
    tiles = width // LANES
    mid = tall - TILE
    planes = east.shape[0]
    offset = tall - planes
    half = half_of(gy_size)
    part = pl.ds(aligned(half * (mid - TILE)), tall)
    keep_own, keep_other = pl.ds(aligned(half * TILE), mid), pl.ds(aligned(half * mid), mid)
    for c in range(tiles):
        cols = tile(c)
        for level in range(levels):
            force = forcing[level, :, cols]
            for k, member in enumerate((own[level, :, cols], others[0, level, part, cols])):
                field[pl.ds(((2 * level + k) * tiles + c) * tall, tall), :] = member * force

    def at(f, c):
        return field[pl.ds((f * tiles + c) * tall, tall), :]

    ends = (tile(0), tile(tiles - 1))
    lead = pl.ds(aligned((1 - half) * TILE), tall)
    for k, pack in enumerate((pack_own, pack_other)):
        pack[lead, :] = edge_columns(*([at(2 * level + k, c) for level in range(levels)] for c in (0, tiles - 1)))
    weight_own[...] = edge_columns(*([own[level, keep_own, cols] for level in range(levels)] for cols in ends))
    weight_other[...] = edge_columns(*([others[0, level, keep_other, cols] for level in range(levels)] for cols in ends))
    for source, out_strip, c, west in ((west_in, west_out, 0, True), (east_in, east_out, tiles - 1, False)):
        columns = [[at(2 * level + k, c) for level in range(levels)] for k in range(2)]
        out_strip[lead, :] = outgoing(columns, source[lead, :], west)

    fields = range(2 * levels)
    for q in range(planes):
        u[q, BODY, :] = turn(field, [f * tiles * tall + ch * offset + q for f in fields for ch in range(2)], tall)
    source, target = u, u_next
    for step in range(STEPS):
        sweep(source, target, east, north, step + 1, planes - 2 - step)
        source, target = target, source
    for q in range(STEPS, planes - STEPS):
        flat = source[q, BODY, :].T
        for f in fields:
            for ch in range(2):
                group = (2 * f + ch) * tiles
                result[pl.ds(f * tiles * tall + ch * offset + q, tiles, stride=tall), :] = flat[group : group + tiles]
    for level in range(levels):
        for c in range(tiles):
            a, b = (
                result[pl.ds(aligned(((2 * level + k) * tiles + c) * tall + half * TILE), mid), :] for k in range(2)
            )
            out[level, :, tile(c)] = own[level, keep_own, tile(c)] * a + others[0, level, keep_other, tile(c)] * b


def halo_columns_kernel(gy_size, strip, west_in, east_in, west_out, east_out):
    levels = strip.shape[0] - 1
    width = strip.shape[2]
    half = half_of(gy_size)
    full = west_out.shape[0]
    halo = pl.ds(aligned(half * (full - TILE)), TILE)
    main = pl.ds(aligned((1 - half) * TILE), full - TILE)
    for source, out, cols, west in (
        (west_in, west_out, slice(0, LANES), True),
        (east_in, east_out, slice(width - LANES, width), False),
    ):
        out[main, :] = source[main, :]
        out[halo, :] = outgoing(
            [[received(gy_size, strip, 2 * level + k, cols) for level in range(levels)] for k in range(2)],
            outgoing_coefficients(received_coefficients(gy_size, strip, cols), west),
            west,
        )


def outer_rows_kernel(
    gy_size, strip, own, other, forcing, coef, pack_own, pack_other, pack_coef,
    sums, full_own, full_other, full_coef,
    zm, mm, wet, field, face, u, u_next, east, north, result,
):
    levels, tall, width = own.shape
    tiles = width // LANES
    half = half_of(gy_size)
    outer = pl.ds(aligned(half * (tall - TILE)), TILE)
    edge = pl.ds(aligned((1 - half) * TILE), TILE)
    halo = pl.ds(aligned(half * TILE), TILE)
    block = 2 * TILE
    every = slice(0, width)
    for k, (ref, value) in enumerate(zip((zm, mm, wet), received_coefficients(gy_size, strip, every))):
        ref[edge, :] = coef[k]
        ref[halo, :] = value
    wet[block:, :] = jnp.zeros((TILE, width), F32)
    for c in range(tiles):
        cols = tile(c)
        face[pl.ds(c * block, block), :], face[pl.ds((tiles + c) * block, block), :] = faces(zm, mm, wet, cols, width, block)
        for level in range(levels):
            for k, member in enumerate((own[level, outer, cols], other[level, :, cols])):
                base = ((2 * level + k) * tiles + c) * block
                field[pl.ds(aligned(base + (1 - half) * TILE), TILE), :] = member * forcing[level, outer, cols]
                field[pl.ds(aligned(base + half * TILE), TILE), :] = received(gy_size, strip, 2 * level + k, cols)

    fields = range(2 * levels)
    planes = 10
    lead = (1 - half) * 4
    for q in range(planes):
        u[q, BODY, :] = turn(field, [f * tiles * block + 2 * ch + q + lead for f in fields for ch in range(2)], block)
        for k, ref in enumerate((east, north)):
            ref[q, BODY, :] = turn(face, [k * tiles * block + 2 * ch + q + lead for f in fields for ch in range(2)], block)
    refresh(east, 0, planes)
    source, target = u, u_next
    for step in range(STEPS):
        sweep(source, target, east, north, step + 1, planes - 2 - step)
        source, target = target, source
    for p in range(2):
        flat = source[STEPS + p, BODY, :].T
        for f in fields:
            for ch in range(2):
                group = (2 * f + ch) * tiles
                result[pl.ds(f * tiles * TILE + 4 * half + 2 * ch + p, tiles, stride=TILE), :] = flat[group : group + tiles]
    natural = row_ids(TILE, LANES) // 4 == half
    for c in range(tiles):
        cols = tile(c)
        terms = []
        for level in range(levels):
            a, b = (result[pl.ds(((2 * level + k) * tiles + c) * TILE, TILE), :] for k in range(2))
            terms.append(own[level, outer, cols] * a + other[level, :, cols] * b)
        for pair in range(levels // 2):
            sums[pl.ds((c * levels // 2 + pair) * TILE, TILE), :] = jnp.where(
                natural, terms[2 * pair], pltpu.roll(terms[2 * pair + 1], 4, 0)
            )

    full = full_own.shape[0]
    main = pl.ds(aligned((1 - half) * TILE), full - TILE)
    outside = pl.ds(aligned(half * (full - TILE)), TILE)
    ends = (slice(0, LANES), slice(width - LANES, width))
    for k, (source, out) in enumerate(((pack_own, full_own), (pack_other, full_other))):
        out[main, :] = source[main, :]
        out[outside, :] = edge_columns(
            *([received(gy_size, strip, 2 * level + k, cols) for level in range(levels)] for cols in ends)
        )
    for k, (first, last) in enumerate(zip(*(received_coefficients(gy_size, strip, cols) for cols in ends))):
        full_coef[k, main, :] = pack_coef[k, main, :]
        full_coef[k, outside, :] = edge_coefficient(first, last)


def end_columns_kernel(
    gy_size, from_west, from_east, own, other, coef, weight_own, weight_other, sums, out,
    a, b, a_next, b_next, east, north, wet,
):
    full = own.shape[0]
    body = pl.ds(TILE, full)
    place = lane_ids(full) % GROUP
    on_west = (place >= 4) & (place < 8)
    on_east = (place >= 24) & (place < 28)
    west, east_strip = from_west[...], from_east[...]

    def with_ends(value, k):
        value = jnp.where(on_west, pltpu.roll(west, (-4 * k) % LANES, 1), value)
        return jnp.where(on_east, pltpu.roll(east_strip, 4 * k, 1), value)

    blank = jnp.zeros((TILE, LANES), F32)
    for ref in (a, b, a_next, b_next, east, north, wet):
        ref[:TILE, :] = blank
        ref[full + TILE :, :] = blank
    a[body, :] = with_ends(own[...], 0)
    b[body, :] = with_ends(other[...], 1)
    wet[body, :] = with_ends(coef[2], 4)
    east[body, :] = with_ends(coef[0], 2) * pltpu.roll(wet[body, :], LANES - 1, 1)
    north[body, :] = with_ends(coef[1], 3) * wet[pl.ds(TILE + 1, full), :]
    now, later = (a, b), (a_next, b_next)
    for step in range(STEPS):
        for t in range(TILE, full + TILE, TILE):
            at, above, below = (pl.ds(t + d, TILE) for d in (0, 1, -1))
            e, n, s = east[at, :], north[at, :], north[below, :]
            for source, target in zip(now, later):
                here = source[at, :]
                flux = e * (pltpu.roll(here, LANES - 1, 1) - here)
                go_north = n * (source[above, :] - here)
                go_south = s * (here - source[below, :])
                target[at, :] = here + flux - pltpu.roll(flux, 1, 1) + go_north - go_south
        now, later = later, now
    mid = weight_own.shape[0]
    rows = pl.ds(2 * TILE, mid)
    out[:mid, :] = weight_own[...] * now[0][rows, :] + weight_other[...] * now[1][rows, :]
    out[mid:, :] = sums[...]


def join_kernel(gy_size, mine_in, theirs_in, mine_edge, theirs_edge, mine, theirs, out, sems):
    half = half_of(gy_size)
    levels, mid, width = mine.shape
    tiles = width // LANES
    lane = lane_ids(mid)
    copies = []
    for k, (ref, edges, where) in enumerate(((mine, mine_edge, half), (theirs, theirs_edge, 1 - half))):
        outer = pl.ds(aligned(where * (mid - TILE)), TILE)
        natural = row_ids(TILE, LANES) // 4 == where
        for level in range(levels):
            for c in range(tiles):
                value = edges[pl.ds(mid + (c * levels // 2 + level // 2) * TILE, TILE), :]
                if level % 2:
                    value = pltpu.roll(value, 4, 0)
                ref[level, outer, tile(c)] = jnp.where(natural, value, ref[level, outer, tile(c)])
            first, last = tile(0), tile(tiles - 1)
            base = GROUP * level
            packed = edges[:mid, :]
            ref[level, :, first] = jnp.where(lane < 4, pltpu.roll(packed, (-base - 8) % LANES, 1), ref[level, :, first])
            ref[level, :, last] = jnp.where(
                lane >= LANES - 4, pltpu.roll(packed, (LANES - 4 - base - 20) % LANES, 1), ref[level, :, last]
            )
            copies.append(
                pltpu.make_async_copy(
                    ref.at[level], out.at[level, pl.ds(aligned(where * mid), mid), :], sems.at[k, level]
                )
            )
            copies[-1].start()
    for copy in copies:
        copy.wait()


def shards(sizes, increment, members, zonal_diff, merid_diff, sea_mask):
    n_mem, n_gy, n_gx = sizes
    levels, rows, width = increment.shape
    tiles = width // LANES
    mid = rows // 2
    tall = mid + TILE
    full = tall + TILE
    planes = 3 * TILE
    assert tiles == TILE and 4 * levels * tiles == LANES and tall == 5 * TILE and n_mem % 2 == 0

    def call(kernel, ins, specs, outs, scratch=(), out_specs=None, aliases={}):
        return pl.pallas_call(
            functools.partial(kernel, n_gy),
            out_shape=outs,
            in_specs=specs,
            out_specs=out_specs if out_specs is not None else jax.tree.map(lambda _: VMEM, outs),
            scratch_shapes=scratch,
            input_output_aliases=aliases,
            compiler_params=pltpu.CompilerParams(vmem_limit_bytes=40 * 1024 * 1024),
        )(*ins)

    def held(kernel, ins, outs, scratch=(), **kw):
        got = call(kernel, [pinned(x) for x in ins], [VMEM] * len(ins), outs, scratch, **kw)
        return got

    def swap(x):
        return lax.ppermute(x, "mem", [(i, i ^ 1) for i in range(n_mem)])

    def along(x, shift):
        return lax.ppermute(x, "gx", [(i, (i + shift) % n_gx) for i in range(n_gx)])

    def across(x):
        def place(chip, core, j, i):
            return ((2 * chip + core) * n_gy + j) * n_gx + i

        first = [0 if j < n_gy // 2 else 1 for j in range(n_gy)]
        pairs = []
        for chip in range(n_mem // 2):
            for j in range(n_gy - 1):
                for i in range(n_gx):
                    a = place(chip, 1 - first[j], j, i)
                    b = place(chip, first[j + 1], j + 1, i)
                    pairs += [(a, b), (b, a)]
            for i in range(n_gx - n_gx % 2):
                pairs.append((place(chip, first[0], 0, i), place(chip, first[0], 0, i ^ 1)))
                pairs.append((place(chip, 1 - first[-1], n_gy - 1, i), place(chip, 1 - first[-1], n_gy - 1, i ^ 1)))
        return lax.ppermute(x, AXES, pairs)

    def scratch(*shape):
        return pltpu.VMEM(shape, F32)

    others = swap(members)
    end = kept(full, LANES)
    turned = kept(planes, DEPTH, LANES)
    own, forcing, coef, weights, face_east, face_north, pack_coef, west, east = call(
        load_kernel,
        [in_hbm(x) for x in (members, increment, zonal_diff, merid_diff, sea_mask)],
        [HBM] * 5,
        [kept(levels, tall, width)] * 2
        + [kept(3, TILE, width), kept(TILE, width), turned, turned, kept(3, full, LANES), end, end],
        [
            pltpu.VMEM((tall, width), jnp.int32),
            scratch(tall, width),
            scratch(tall, width),
            scratch(full, width),
            scratch(2 * tiles * tall, LANES),
            pltpu.SemaphoreType.DMA((5,)),
        ],
    )
    strip, other = held(
        pack_rows_kernel,
        [own, others, forcing, weights],
        [kept(levels + 1, TILE, width), kept(levels, TILE, width)],
    )
    forcing, strip = lax.optimization_barrier((forcing, strip))
    strip = across(strip)

    inside, pack_own, pack_other, weight_own, weight_other, west, east = held(
        interior_kernel,
        [own, others, forcing, face_east, face_north, west, east],
        [kept(levels, mid, width), end, end, kept(mid, LANES), kept(mid, LANES), end, end],
        [
            scratch(2 * levels * tiles * tall, LANES),
            scratch(planes, DEPTH, LANES),
            scratch(planes, DEPTH, LANES),
            scratch(2 * levels * tiles * tall, LANES),
        ],
    )
    west, east = held(halo_columns_kernel, [strip, west, east], [end, end])
    inside, west, east = lax.optimization_barrier((inside, west, east))
    from_west = along(east, 1)
    from_east = along(west, -1)
    sums, full_own, full_other, full_coef = held(
        outer_rows_kernel,
        [strip, own, other, forcing, coef, pack_own, pack_other, pack_coef],
        [kept(levels // 2 * tiles * TILE, LANES), end, end, kept(3, full, LANES)],
        [
            scratch(2 * TILE, width),
            scratch(2 * TILE, width),
            scratch(3 * TILE, width),
            scratch(2 * levels * tiles * 2 * TILE, LANES),
            scratch(2 * tiles * 2 * TILE, LANES),
            scratch(10, DEPTH, LANES),
            scratch(10, DEPTH, LANES),
            scratch(10, DEPTH, LANES),
            scratch(10, DEPTH, LANES),
            scratch(2 * levels * tiles * TILE, LANES),
        ],
    )
    edges = held(
        end_columns_kernel,
        [from_west, from_east, full_own, full_other, full_coef, weight_own, weight_other, sums],
        kept(mid + levels // 2 * tiles * TILE, LANES),
        [scratch(full + 2 * TILE, LANES)] * 7,
    )
    if n_mem > 2:
        groups = [list(range(k, n_mem, 2)) for k in range(2)]
        inside, edges = (lax.psum(x, "mem", axis_index_groups=groups) for x in (inside, edges))
    inside_theirs, edges_theirs = swap(inside), swap(edges)
    return held(
        join_kernel,
        [inside, inside_theirs, edges, edges_theirs],
        [kept(levels, mid, width)] * 2 + [jax.ShapeDtypeStruct(increment.shape, F32)],
        [pltpu.SemaphoreType.DMA((2, levels))],
        out_specs=[VMEM, VMEM, HBM],
        aliases={0: 0, 1: 1},
    )[2]


def solution(mesh):
    return jax.shard_map(
        functools.partial(shards, tuple(mesh.shape[axis] for axis in AXES)),
        mesh=mesh,
        in_specs=(
            P(None, "gy", "gx"),
            P("mem", None, "gy", "gx"),
            P("gy", "gx"),
            P("gy", "gx"),
            P("gy", "gx"),
        ),
        out_specs=P(None, "gy", "gx"),
        check_vma=False,
    )
```

```python
import functools
import jax
import jax.numpy as jnp
from jax import lax
from jax.experimental import pallas as pl
from jax.experimental.pallas import tpu as pltpu
from jax.sharding import PartitionSpec as P

STEPS = 4
FIRST_STEPS = 2
TILE = 8
LANES = 128
AXES = ("mem", "gy", "gx")
F32 = jnp.float32
VMEM = pl.BlockSpec(memory_space=pltpu.VMEM)
HBM = pl.BlockSpec(memory_space=pltpu.HBM)

BODY = slice(TILE, TILE + LANES)
DEPTH = LANES + 2 * TILE
GROUP = 32


def half_of(gy_size):
    core = lax.rem(lax.axis_index("mem"), 2)
    later = (lax.axis_index("gy") >= gy_size // 2).astype(jnp.int32)
    return lax.rem(core + later, 2)


def kept(*shape):
    return pltpu.VMEM(shape, F32)


def pinned(x):
    return pltpu.with_memory_space_constraint(x, pltpu.VMEM)


def in_hbm(x):
    return pltpu.with_memory_space_constraint(x, pltpu.HBM)


def tile(c):
    return slice(c * LANES, (c + 1) * LANES)


def lane_ids(rows):
    return lax.broadcasted_iota(jnp.int32, (rows, LANES), 1)


def row_ids(rows, width):
    return lax.broadcasted_iota(jnp.int32, (rows, width), 0)


def aligned(start):
    return pl.multiple_of(start, TILE)


def run(copies):
    for copy in copies:
        copy.start()
    for copy in copies:
        copy.wait()


def pack_coefficients_kernel(gy_size, coef, out):
    half = half_of(gy_size)
    width = out.shape[1]
    zm, mm, wet = coef[0], coef[1], coef[2]
    row = row_ids(TILE, width)
    col = lax.broadcasted_iota(jnp.int32, (TILE, width), 1)
    east = zm * jnp.where(col == width - 1, 1.0, pltpu.roll(wet, width - 1, 1))
    north = mm * jnp.where(row == TILE - 1, 1.0, pltpu.roll(wet, TILE - 1, 0))
    upper = jnp.where(row < 4, north, pltpu.roll(east, 4, 0))
    upper = jnp.where(row == 3, pltpu.roll(wet, 3, 0), upper)
    lower = jnp.where(row < 4, pltpu.roll(north, 4, 0), east)
    out[...] = jnp.where(half == 0, upper, lower)
    first = wet[:, :LANES]
    lane, line = lane_ids(TILE), row_ids(TILE, LANES)
    value = out[:, :LANES]
    for r in range(4):
        moved = jnp.where(half == 0, pltpu.roll(first, 7 - r, 0), pltpu.roll(first, (-r) % TILE, 0))
        value = jnp.where((line == jnp.where(half == 0, 7, 4)) & (lane == r), pltpu.roll(moved, r, 1), value)
    out[:, :LANES] = value


def outer_rows_of(gy_size, level, own, other, forcing, cols):
    half = half_of(gy_size)
    j = lax.axis_index("gy")
    same_core = jnp.where(half == 0, j == gy_size // 2, j == gy_size // 2 - 1)
    outer = pl.ds(aligned(half * (own.shape[1] - TILE)), TILE)
    force = forcing[level, outer, cols]
    mine = own[level, outer, cols] * force
    theirs = other[level, :, cols] * force
    first, second = jnp.where(same_core, mine, theirs), jnp.where(same_core, theirs, mine)
    first = jnp.where(half == 0, first, pltpu.roll(first, TILE // 2, 0))
    second = jnp.where(half == 0, pltpu.roll(second, TILE // 2, 0), second)
    return jnp.where(row_ids(*first.shape) < TILE // 2, first, second)


def pack_corner_kernel(gy_size, own, others, forcing, weights, other, corner):
    levels, _, width = own.shape
    other[...] = others[0, :, pl.ds(aligned(half_of(gy_size) * (others.shape[2] - TILE)), TILE), :]
    ends = (tile(0), slice(width - LANES, width))
    corner[:TILE, :] = edge_columns(
        *([outer_rows_of(gy_size, level, own, other, forcing, cols) for level in range(levels)] for cols in ends)
    )
    corner[TILE:, :] = edge_coefficient(*(weights[:, cols] for cols in ends))


def pack_rows_kernel(gy_size, own, other, forcing, weights, strip):
    levels, _, width = own.shape
    for level in range(levels):
        strip[level] = outer_rows_of(gy_size, level, own, other, forcing, slice(0, width))
    strip[levels] = weights[...]


def inside_domain(gy_size):
    half, j = half_of(gy_size), lax.axis_index("gy")
    return jnp.where(half == 0, j > 0, j < gy_size - 1)


def beyond(value, real):
    return jnp.where(real, value, 0.0)


def unfold(gy_size, value, place):
    natural = jnp.equal(half_of(gy_size), 1 - place % 2)
    return beyond(jnp.where(natural, value, pltpu.roll(value, TILE // 2, 0)), inside_domain(gy_size))


def unfold_weights(gy_size, value, packed):
    half, real = half_of(gy_size), inside_domain(gy_size)
    moved = pltpu.roll(value, TILE // 2, 0)
    zm = jnp.where(half == 0, value, moved)
    mm = jnp.where(half == 0, moved, value)
    line = row_ids(*value.shape)
    wet = jnp.where((half == 1) & (line == 0), pltpu.roll(value, 5, 0), 1.0)
    if packed:
        place = lane_ids(TILE) % GROUP
        for r in range(4):
            shifted = jnp.where(half == 0, pltpu.roll(value, r, 0), pltpu.roll(value, (r + 1) % TILE, 0))
            at = (line == jnp.where(half == 0, 4 + r, r)) & (place == 8)
            wet = jnp.where(at, pltpu.roll(shifted, (-r) % LANES, 1), wet)
    return [beyond(x, real) for x in (zm, mm, wet)]


def edge_columns(first, last):
    rows = first[0].shape[0]
    lane = lane_ids(rows)
    total = jnp.zeros((rows, LANES), F32)
    for level, (a, b) in enumerate(zip(first, last)):
        base = GROUP * level
        total = jnp.where((lane >= base + 8) & (lane < base + 16), pltpu.roll(a, base + 8, 1), total)
        total = jnp.where((lane >= base + 16) & (lane < base + 24), pltpu.roll(b, (base + 16 - 120) % LANES, 1), total)
    return total


def spread(value):
    value = value + pltpu.roll(value, GROUP, 1)
    return value + pltpu.roll(value, 2 * GROUP, 1)


def edge_coefficient(first, last):
    rows = first.shape[0]
    lane = lane_ids(rows)
    total = jnp.where((lane >= 8) & (lane < 16), pltpu.roll(first, 8, 1), 0.0)
    return spread(jnp.where((lane >= 16) & (lane < 24), pltpu.roll(last, 24, 1), total))


def outgoing(values, west):
    place = lane_ids(values[0].shape[0]) % GROUP
    start, step, source = (24, -4, 8) if west else (4, 4, 20)
    total = jnp.zeros(values[0].shape, F32)
    for k, value in enumerate(values):
        at = start + step * k
        total = jnp.where((place >= at) & (place < at + 4), pltpu.roll(value, (at - source) % LANES, 1), total)
    return total


def turn(ref, start, stride):
    return jnp.concatenate([ref[pl.ds(s, TILE, stride=stride), :] for s in start], axis=0).T


def refresh(ref, first, count):
    flat = ref.reshape(ref.shape[0] * DEPTH, LANES)

    def rows(j):
        return pl.ds(first * DEPTH + TILE + j, count, stride=DEPTH)

    flat[rows(-1), :] = pltpu.roll(flat[rows(LANES - 1), :], 1, 1)
    flat[rows(LANES), :] = pltpu.roll(flat[rows(0), :], LANES - 1, 1)


def sweep(source, target, east, north, first, last):
    for start in range(TILE, TILE + LANES, TILE):
        at, ahead, behind = (slice(start + d, start + d + TILE) for d in (0, 1, -1))
        here = source[first, at, :]
        south = north[first - 1, at, :] * (here - source[first - 1, at, :])
        for p in range(first, last + 1):
            above = source[p + 1, at, :]
            flux = north[p, at, :] * (above - here)
            go_east = east[p, at, :] * (source[p, ahead, :] - here)
            go_west = east[p, behind, :] * (here - source[p, behind, :])
            target[p, at, :] = here + go_east - go_west + flux - south
            here, south = above, flux


def faces(zm, mm, wet, cols, width, rows):
    after = slice(cols.start + LANES, cols.stop + LANES) if cols.stop < width else cols
    lane = lane_ids(rows)
    here = pltpu.roll(wet[:rows, cols], LANES - 1, 1)
    beyond = pltpu.roll(wet[:rows, after], LANES - 1, 1)
    east = zm[:, cols] * jnp.where(lane == LANES - 1, beyond, here)
    north = mm[:, cols] * wet[1 : rows + 1, cols]
    return east, north


def load_kernel(
    gy_size, members, increment, zonal, merid, mask,
    own, forcing, coef, east, north, pack_coef,
    mask_buf, zm, mm, wet, face, sems,
):
    _, tall, width = own.shape
    tiles = width // LANES
    planes = east.shape[0]
    offset = tall - planes
    half = half_of(gy_size)
    part = pl.ds(aligned(half * (tall - 2 * TILE)), tall)
    small = [
        pltpu.make_async_copy(mask.at[part, :], mask_buf, sems.at[0]),
        pltpu.make_async_copy(zonal.at[part, :], zm, sems.at[1]),
        pltpu.make_async_copy(merid.at[part, :], mm, sems.at[2]),
    ]
    large = [
        pltpu.make_async_copy(increment.at[:, part, :], forcing, sems.at[3]),
        pltpu.make_async_copy(members.at[0, :, part, :], own, sems.at[4]),
    ]
    for copy in small + large:
        copy.start()
    for copy in small:
        copy.wait()
    wet[:tall, :] = mask_buf[...].astype(F32)
    wet[tall:, :] = jnp.zeros((TILE, width), F32)
    zm[...] = zm[...] * wet[:tall, :]
    mm[...] = mm[...] * wet[:tall, :]
    outer = pl.ds(aligned(half * (tall - TILE)), TILE)
    for k, ref in enumerate((zm, mm, wet)):
        coef[k] = ref[outer, :]
    for c in range(tiles):
        face[pl.ds(c * tall, tall), :], face[pl.ds((tiles + c) * tall, tall), :] = faces(zm, mm, wet, tile(c), width, tall)
    for q in range(planes):
        for k, ref in enumerate((east, north)):
            ref[q, BODY, :] = turn(face, [k * tiles * tall + ch * offset + q for _ in range(TILE) for ch in range(2)], tall)
    refresh(east, 0, planes)
    ends = (tile(0), tile(tiles - 1))
    for k, ref in enumerate((zm, mm, wet)):
        pack_coef[k] = edge_coefficient(*(ref[:tall, cols] for cols in ends))
    large[0].wait()
    forcing[...] = forcing[...] * wet[:tall, :][None]
    large[1].wait()


def interior_kernel(
    gy_size, own, others, forcing, east, north,
    halfway, pack_own, pack_other, weight_own, weight_other,
    field, u, u_next,
):
    levels, tall, width = own.shape
    tiles = width // LANES
    mid = tall - TILE
    planes = east.shape[0]
    offset = tall - planes
    half = half_of(gy_size)
    part = pl.ds(aligned(half * (mid - TILE)), tall)
    keep_own, keep_other = pl.ds(aligned(half * TILE), mid), pl.ds(aligned(half * mid), mid)
    for c in range(tiles):
        cols = tile(c)
        for level in range(levels):
            force = forcing[level, :, cols]
            for k, member in enumerate((own[level, :, cols], others[0, level, part, cols])):
                field[pl.ds(((2 * level + k) * tiles + c) * tall, tall), :] = member * force

    def at(f, c):
        return field[pl.ds((f * tiles + c) * tall, tall), :]

    ends = (tile(0), tile(tiles - 1))
    for k, pack in enumerate((pack_own, pack_other)):
        pack[...] = edge_columns(*([at(2 * level + k, c) for level in range(levels)] for c in (0, tiles - 1)))
    weight_own[...] = edge_columns(*([own[level, keep_own, cols] for level in range(levels)] for cols in ends))
    weight_other[...] = edge_columns(*([others[0, level, keep_other, cols] for level in range(levels)] for cols in ends))
    fields = range(2 * levels)
    for q in range(planes):
        u[q, BODY, :] = turn(field, [f * tiles * tall + ch * offset + q for f in fields for ch in range(2)], tall)
    buffers = [u, u_next, halfway]
    for step in range(FIRST_STEPS):
        count = planes - 2 - 2 * step
        refresh(buffers[step], step + 1, count)
        sweep(buffers[step], buffers[step + 1], east, north, step + 1, step + count)
    refresh(halfway, FIRST_STEPS + 1, planes - 2 - 2 * FIRST_STEPS)


def interior_rest_kernel(gy_size, halfway, own, others, east, north, out, u, u_next, result):
    levels, tall, width = own.shape
    tiles = width // LANES
    mid = tall - TILE
    planes = east.shape[0]
    offset = tall - planes
    half = half_of(gy_size)
    keep_own, keep_other = pl.ds(aligned(half * TILE), mid), pl.ds(aligned(half * mid), mid)
    fields = range(2 * levels)
    source = halfway
    for step in range(FIRST_STEPS, STEPS):
        count = planes - 2 - 2 * step
        if step > FIRST_STEPS:
            refresh(source, step + 1, count)
        target = u if step % 2 == 0 else u_next
        sweep(source, target, east, north, step + 1, step + count)
        source = target
    for q in range(STEPS, planes - STEPS):
        flat = source[q, BODY, :].T
        for f in fields:
            for ch in range(2):
                group = (2 * f + ch) * tiles
                result[pl.ds(f * tiles * tall + ch * offset + q, tiles, stride=tall), :] = flat[group : group + tiles]
    for level in range(levels):
        for c in range(tiles):
            a, b = (
                result[pl.ds(aligned(((2 * level + k) * tiles + c) * tall + half * TILE), mid), :] for k in range(2)
            )
            out[level, :, tile(c)] = own[level, keep_own, tile(c)] * a + others[0, level, keep_other, tile(c)] * b


def halo_columns_kernel(
    gy_size, corner, pack_own, pack_other, pack_coef, full_own, full_other, full_coef, west_out, east_out
):
    half = half_of(gy_size)
    tall = pack_own.shape[0]
    halo = pl.ds(aligned(half * tall), TILE)
    main = pl.ds(aligned((1 - half) * TILE), tall)
    local = [pack_own[...], pack_other[...]] + [pack_coef[k] for k in range(3)]
    fields = [unfold(gy_size, corner[:TILE, :], k) for k in range(2)]
    received = fields + unfold_weights(gy_size, corner[TILE:, :], True)
    full = [full_own, full_other] + [full_coef.at[k] for k in range(3)]
    for rows, values in ((main, local), (halo, received)):
        west_out[rows, :] = outgoing(values, True)
        east_out[rows, :] = outgoing(values, False)
    for ref, inner, outer in zip(full, local, received):
        ref[main, :] = inner
        ref[halo, :] = outer


def outer_rows_kernel(
    gy_size, strip, own, other, forcing, coef, sums,
    zm, mm, wet, field, face, u, u_next, east, north, result,
):
    levels, tall, width = own.shape
    tiles = width // LANES
    half = half_of(gy_size)
    outer = pl.ds(aligned(half * (tall - TILE)), TILE)
    edge = pl.ds(aligned((1 - half) * TILE), TILE)
    halo = pl.ds(aligned(half * TILE), TILE)
    block = 2 * TILE
    for k, (ref, value) in enumerate(zip((zm, mm, wet), unfold_weights(gy_size, strip[levels], False))):
        ref[edge, :] = coef[k]
        ref[halo, :] = value
    wet[block:, :] = jnp.zeros((TILE, width), F32)
    for c in range(tiles):
        cols = tile(c)
        face[pl.ds(c * block, block), :], face[pl.ds((tiles + c) * block, block), :] = faces(zm, mm, wet, cols, width, block)
        for level in range(levels):
            for k, member in enumerate((own[level, outer, cols], other[level, :, cols])):
                base = ((2 * level + k) * tiles + c) * block
                field[pl.ds(aligned(base + (1 - half) * TILE), TILE), :] = member * forcing[level, outer, cols]
                field[pl.ds(aligned(base + half * TILE), TILE), :] = unfold(gy_size, strip[level, :, cols], k)

    fields = range(2 * levels)
    planes = 10
    lead = (1 - half) * 4
    for q in range(planes):
        u[q, BODY, :] = turn(field, [f * tiles * block + 2 * ch + q + lead for f in fields for ch in range(2)], block)
        for k, ref in enumerate((east, north)):
            ref[q, BODY, :] = turn(face, [k * tiles * block + 2 * ch + q + lead for f in fields for ch in range(2)], block)
    refresh(east, 0, planes)
    source, target = u, u_next
    for step in range(STEPS):
        count = planes - 2 - 2 * step
        refresh(source, step + 1, count)
        sweep(source, target, east, north, step + 1, step + count)
        source, target = target, source
    for p in range(2):
        flat = source[STEPS + p, BODY, :].T
        for f in fields:
            for ch in range(2):
                group = (2 * f + ch) * tiles
                result[pl.ds(f * tiles * TILE + 4 * half + 2 * ch + p, tiles, stride=TILE), :] = flat[group : group + tiles]
    natural = row_ids(TILE, LANES) // 4 == half
    for c in range(tiles):
        cols = tile(c)
        terms = []
        for level in range(levels):
            a, b = (result[pl.ds(((2 * level + k) * tiles + c) * TILE, TILE), :] for k in range(2))
            terms.append(own[level, outer, cols] * a + other[level, :, cols] * b)
        for pair in range(levels // 2):
            sums[pl.ds((c * levels // 2 + pair) * TILE, TILE), :] = jnp.where(
                natural, terms[2 * pair], pltpu.roll(terms[2 * pair + 1], 4, 0)
            )


def end_columns_kernel(
    gy_size, from_west, from_east, own, other, coef, weight_own, weight_other, sums, out,
    a, b, a_next, b_next, east, north, wet,
):
    full = own.shape[0]
    body = pl.ds(TILE, full)
    place = lane_ids(full) % GROUP
    on_west = (place >= 4) & (place < 8)
    on_east = (place >= 24) & (place < 28)
    west, east_strip = from_west[...], from_east[...]

    def with_ends(value, k):
        value = jnp.where(on_west, pltpu.roll(west, (-4 * k) % LANES, 1), value)
        return jnp.where(on_east, pltpu.roll(east_strip, 4 * k, 1), value)

    blank = jnp.zeros((TILE, LANES), F32)
    for ref in (a, b, a_next, b_next, east, north, wet):
        ref[:TILE, :] = blank
        ref[full + TILE :, :] = blank
    a[body, :] = with_ends(own[...], 0)
    b[body, :] = with_ends(other[...], 1)
    wet[body, :] = with_ends(coef[2], 4)
    east[body, :] = with_ends(coef[0], 2) * pltpu.roll(wet[body, :], LANES - 1, 1)
    north[body, :] = with_ends(coef[1], 3) * wet[pl.ds(TILE + 1, full), :]
    now, later = (a, b), (a_next, b_next)
    for step in range(STEPS):
        for t in range(TILE, full + TILE, TILE):
            at, above, below = (pl.ds(t + d, TILE) for d in (0, 1, -1))
            e, n, s = east[at, :], north[at, :], north[below, :]
            for source, target in zip(now, later):
                here = source[at, :]
                flux = e * (pltpu.roll(here, LANES - 1, 1) - here)
                go_north = n * (source[above, :] - here)
                go_south = s * (here - source[below, :])
                target[at, :] = here + flux - pltpu.roll(flux, 1, 1) + go_north - go_south
        now, later = later, now
    mid = weight_own.shape[0]
    rows = pl.ds(2 * TILE, mid)
    out[:mid, :] = weight_own[...] * now[0][rows, :] + weight_other[...] * now[1][rows, :]
    out[mid:, :] = sums[...]


def join_kernel(gy_size, mine_in, theirs_in, mine_edge, theirs_edge, mine, theirs, out, sems):
    half = half_of(gy_size)
    levels, mid, width = mine.shape
    tiles = width // LANES
    lane = lane_ids(mid)
    copies = []
    for k, (ref, edges, where) in enumerate(((mine, mine_edge, half), (theirs, theirs_edge, 1 - half))):
        outer = pl.ds(aligned(where * (mid - TILE)), TILE)
        natural = row_ids(TILE, LANES) // 4 == where
        for level in range(levels):
            for c in range(tiles):
                value = edges[pl.ds(mid + (c * levels // 2 + level // 2) * TILE, TILE), :]
                if level % 2:
                    value = pltpu.roll(value, 4, 0)
                ref[level, outer, tile(c)] = jnp.where(natural, value, ref[level, outer, tile(c)])
            first, last = tile(0), tile(tiles - 1)
            base = GROUP * level
            packed = edges[:mid, :]
            ref[level, :, first] = jnp.where(lane < 4, pltpu.roll(packed, (-base - 8) % LANES, 1), ref[level, :, first])
            ref[level, :, last] = jnp.where(
                lane >= LANES - 4, pltpu.roll(packed, (LANES - 4 - base - 20) % LANES, 1), ref[level, :, last]
            )
            copies.append(
                pltpu.make_async_copy(
                    ref.at[level], out.at[level, pl.ds(aligned(where * mid), mid), :], sems.at[k, level]
                )
            )
            copies[-1].start()
    for copy in copies:
        copy.wait()


def shards(sizes, increment, members, zonal_diff, merid_diff, sea_mask):
    n_mem, n_gy, n_gx = sizes
    levels, rows, width = increment.shape
    tiles = width // LANES
    mid = rows // 2
    tall = mid + TILE
    full = tall + TILE
    planes = 3 * TILE
    assert tiles == TILE and 4 * levels * tiles == LANES and tall == 5 * TILE and n_mem % 2 == 0

    def call(kernel, ins, specs, outs, scratch=(), out_specs=None, aliases={}):
        return pl.pallas_call(
            functools.partial(kernel, n_gy),
            out_shape=outs,
            in_specs=specs,
            out_specs=out_specs if out_specs is not None else jax.tree.map(lambda _: VMEM, outs),
            scratch_shapes=scratch,
            input_output_aliases=aliases,
            compiler_params=pltpu.CompilerParams(vmem_limit_bytes=40 * 1024 * 1024),
        )(*ins)

    def held(kernel, ins, outs, scratch=(), **kw):
        got = call(kernel, [pinned(x) for x in ins], [VMEM] * len(ins), outs, scratch, **kw)
        return got

    def swap(x):
        return lax.ppermute(x, "mem", [(i, i ^ 1) for i in range(n_mem)])

    def along(x, shift):
        return lax.ppermute(x, "gx", [(i, (i + shift) % n_gx) for i in range(n_gx)])

    def across(x):
        def place(chip, core, j, i):
            return ((2 * chip + core) * n_gy + j) * n_gx + i

        first = [0 if j < n_gy // 2 else 1 for j in range(n_gy)]
        pairs = []
        for chip in range(n_mem // 2):
            for j in range(n_gy - 1):
                for i in range(n_gx):
                    a = place(chip, 1 - first[j], j, i)
                    b = place(chip, first[j + 1], j + 1, i)
                    pairs += [(a, b), (b, a)]
            for i in range(n_gx - n_gx % 2):
                pairs.append((place(chip, first[0], 0, i), place(chip, first[0], 0, i ^ 1)))
                pairs.append((place(chip, 1 - first[-1], n_gy - 1, i), place(chip, 1 - first[-1], n_gy - 1, i ^ 1)))
        return lax.ppermute(x, AXES, pairs)

    def scratch(*shape):
        return pltpu.VMEM(shape, F32)

    others = swap(members)
    end = kept(full, LANES)
    turned = kept(planes, DEPTH, LANES)
    own, forcing, coef, face_east, face_north, pack_coef = call(
        load_kernel,
        [in_hbm(x) for x in (members, increment, zonal_diff, merid_diff, sea_mask)],
        [HBM] * 5,
        [kept(levels, tall, width)] * 2
        + [kept(3, TILE, width), turned, turned, kept(3, tall, LANES)],
        [
            pltpu.VMEM((tall, width), jnp.int32),
            scratch(tall, width),
            scratch(tall, width),
            scratch(full, width),
            scratch(2 * tiles * tall, LANES),
            pltpu.SemaphoreType.DMA((5,)),
        ],
    )
    weights = held(pack_coefficients_kernel, [coef], kept(TILE, width))
    other, corner = held(
        pack_corner_kernel,
        [own, others, forcing, weights],
        [kept(levels, TILE, width), kept(2 * TILE, LANES)],
    )
    forcing, corner = lax.optimization_barrier((forcing, corner))
    corner = across(corner)
    packed = kept(tall, LANES)
    halfway, pack_own, pack_other, weight_own, weight_other = held(
        interior_kernel,
        [own, others, forcing, face_east, face_north],
        [turned, packed, packed, kept(mid, LANES), kept(mid, LANES)],
        [scratch(2 * levels * tiles * tall, LANES), scratch(planes, DEPTH, LANES), scratch(planes, DEPTH, LANES)],
    )
    halfway, weights, corner = lax.optimization_barrier((halfway, weights, corner))
    strip = across(held(pack_rows_kernel, [own, other, forcing, weights], kept(levels + 1, TILE, width)))
    full_own, full_other, full_coef, west, east = held(
        halo_columns_kernel,
        [corner, pack_own, pack_other, pack_coef],
        [end, end, kept(3, full, LANES), end, end],
    )
    halfway, west, east = lax.optimization_barrier((halfway, west, east))
    from_west = along(east, 1)
    from_east = along(west, -1)
    inside = held(
        interior_rest_kernel,
        [halfway, own, others, face_east, face_north],
        kept(levels, mid, width),
        [
            scratch(planes, DEPTH, LANES),
            scratch(planes, DEPTH, LANES),
            scratch(2 * levels * tiles * tall, LANES),
        ],
    )
    inside, forcing = lax.optimization_barrier((inside, forcing))
    sums = held(
        outer_rows_kernel,
        [strip, own, other, forcing, coef],
        kept(levels // 2 * tiles * TILE, LANES),
        [
            scratch(2 * TILE, width),
            scratch(2 * TILE, width),
            scratch(3 * TILE, width),
            scratch(2 * levels * tiles * 2 * TILE, LANES),
            scratch(2 * tiles * 2 * TILE, LANES),
            scratch(10, DEPTH, LANES),
            scratch(10, DEPTH, LANES),
            scratch(10, DEPTH, LANES),
            scratch(10, DEPTH, LANES),
            scratch(2 * levels * tiles * TILE, LANES),
        ],
    )
    inside, sums, from_west, from_east = lax.optimization_barrier((inside, sums, from_west, from_east))
    edges = held(
        end_columns_kernel,
        [from_west, from_east, full_own, full_other, full_coef, weight_own, weight_other, sums],
        kept(mid + levels // 2 * tiles * TILE, LANES),
        [scratch(full + 2 * TILE, LANES)] * 7,
    )
    if n_mem > 2:
        groups = [list(range(k, n_mem, 2)) for k in range(2)]
        inside, edges = (lax.psum(x, "mem", axis_index_groups=groups) for x in (inside, edges))
    inside_theirs, edges_theirs = swap(inside), swap(edges)
    return held(
        join_kernel,
        [inside, inside_theirs, edges, edges_theirs],
        [kept(levels, mid, width)] * 2 + [jax.ShapeDtypeStruct(increment.shape, F32)],
        [pltpu.SemaphoreType.DMA((2, levels))],
        out_specs=[VMEM, VMEM, HBM],
        aliases={0: 0, 1: 1},
    )[2]


def solution(mesh):
    return jax.shard_map(
        functools.partial(shards, tuple(mesh.shape[axis] for axis in AXES)),
        mesh=mesh,
        in_specs=(
            P(None, "gy", "gx"),
            P("mem", None, "gy", "gx"),
            P("gy", "gx"),
            P("gy", "gx"),
            P("gy", "gx"),
        ),
        out_specs=P(None, "gy", "gx"),
        check_vma=False,
    )
```

```python
import functools
import jax
import jax.numpy as jnp
from jax import lax
from jax.experimental import pallas as pl
from jax.experimental.pallas import tpu as pltpu
from jax.sharding import PartitionSpec as P

STEPS = 4
FIRST_STEPS = 2
TILE = 8
LANES = 128
AXES = ("mem", "gy", "gx")
F32 = jnp.float32
VMEM = pl.BlockSpec(memory_space=pltpu.VMEM)
HBM = pl.BlockSpec(memory_space=pltpu.HBM)

BODY = slice(TILE, TILE + LANES)
DEPTH = LANES + 2 * TILE
GROUP = 32


def half_of(gy_size):
    core = lax.rem(lax.axis_index("mem"), 2)
    later = (lax.axis_index("gy") >= gy_size // 2).astype(jnp.int32)
    return lax.rem(core + later, 2)


def kept(*shape):
    return pltpu.VMEM(shape, F32)


def pinned(x):
    return pltpu.with_memory_space_constraint(x, pltpu.VMEM)


def in_hbm(x):
    return pltpu.with_memory_space_constraint(x, pltpu.HBM)


def tile(c):
    return slice(c * LANES, (c + 1) * LANES)


def lane_ids(rows):
    return lax.broadcasted_iota(jnp.int32, (rows, LANES), 1)


def row_ids(rows, width):
    return lax.broadcasted_iota(jnp.int32, (rows, width), 0)


def aligned(start):
    return pl.multiple_of(start, TILE)


def run(copies):
    for copy in copies:
        copy.start()
    for copy in copies:
        copy.wait()


def own_ends_kernel(gy_size, own, forcing, coef, out, ends, pack_own, weight_own):
    half = half_of(gy_size)
    width = out.shape[1]
    zm, mm, wet = coef[0], coef[1], coef[2]
    row = row_ids(TILE, width)
    col = lax.broadcasted_iota(jnp.int32, (TILE, width), 1)
    east = zm * jnp.where(col == width - 1, 1.0, pltpu.roll(wet, width - 1, 1))
    north = mm * jnp.where(row == TILE - 1, 1.0, pltpu.roll(wet, TILE - 1, 0))
    upper = jnp.where(row < 4, north, pltpu.roll(east, 4, 0))
    upper = jnp.where(row == 3, pltpu.roll(wet, 3, 0), upper)
    lower = jnp.where(row < 4, pltpu.roll(north, 4, 0), east)
    out[...] = jnp.where(half == 0, upper, lower)
    first = wet[:, :LANES]
    lane, line = lane_ids(TILE), row_ids(TILE, LANES)
    value = out[:, :LANES]
    for r in range(4):
        moved = jnp.where(half == 0, pltpu.roll(first, 7 - r, 0), pltpu.roll(first, (-r) % TILE, 0))
        value = jnp.where((line == jnp.where(half == 0, 7, 4)) & (lane == r), pltpu.roll(moved, r, 1), value)
    out[:, :LANES] = value
    both = (tile(0), slice(width - LANES, width))
    ends[...] = edge_coefficient(*(out[:, cols] for cols in both))
    levels, tall, _ = own.shape
    pack_own[...] = edge_columns(*([own[l, :, cols] * forcing[l, :, cols] for l in range(levels)] for cols in both))
    keep = pl.ds(aligned(half * TILE), tall - TILE)
    weight_own[...] = edge_columns(*([own[l, keep, cols] for l in range(levels)] for cols in both))


def outer_rows_of(gy_size, level, own, other, forcing, cols):
    half = half_of(gy_size)
    j = lax.axis_index("gy")
    same_core = jnp.where(half == 0, j == gy_size // 2, j == gy_size // 2 - 1)
    outer = pl.ds(aligned(half * (own.shape[1] - TILE)), TILE)
    force = forcing[level, outer, cols]
    mine = own[level, outer, cols] * force
    theirs = other[level, :, cols] * force
    first, second = jnp.where(same_core, mine, theirs), jnp.where(same_core, theirs, mine)
    first = jnp.where(half == 0, first, pltpu.roll(first, TILE // 2, 0))
    second = jnp.where(half == 0, pltpu.roll(second, TILE // 2, 0), second)
    return jnp.where(row_ids(*first.shape) < TILE // 2, first, second)


def pack_rows_kernel(gy_size, own, others, forcing, weights, coef_ends, other, strip):
    levels, _, width = own.shape
    tiles = width // LANES
    other[...] = others[0, :, pl.ds(aligned(half_of(gy_size) * (others.shape[2] - TILE)), TILE), :]
    ends = ([], [])
    for c in range(tiles):
        for level in range(levels):
            rows = outer_rows_of(gy_size, level, own, other, forcing, tile(c))
            strip[strip_rows(level, c, tiles), :] = rows
            if c in (0, tiles - 1):
                ends[c > 0].append(rows)
        strip[strip_rows(levels, c, tiles), :] = weights[:, tile(c)]
    last = (levels + 1) * tiles * TILE
    strip[last : last + TILE, :] = edge_columns(*ends)
    strip[last + TILE :, :] = coef_ends[...]


def strip_rows(place, c, tiles):
    return slice((place * tiles + c) * TILE, (place * tiles + c + 1) * TILE)


def inside_domain(gy_size):
    half, j = half_of(gy_size), lax.axis_index("gy")
    return jnp.where(half == 0, j > 0, j < gy_size - 1)


def beyond(value, real):
    return jnp.where(real, value, 0.0)


def unfold(gy_size, value, place):
    natural = jnp.equal(half_of(gy_size), 1 - place % 2)
    return beyond(jnp.where(natural, value, pltpu.roll(value, TILE // 2, 0)), inside_domain(gy_size))


def unfold_weights(gy_size, value, packed):
    half, real = half_of(gy_size), inside_domain(gy_size)
    moved = pltpu.roll(value, TILE // 2, 0)
    zm = jnp.where(half == 0, value, moved)
    mm = jnp.where(half == 0, moved, value)
    line = row_ids(*value.shape)
    wet = jnp.where((half == 1) & (line == 0), pltpu.roll(value, 5, 0), 1.0)
    if packed:
        place = lane_ids(TILE) % GROUP
        for r in range(4):
            shifted = jnp.where(half == 0, pltpu.roll(value, r, 0), pltpu.roll(value, (r + 1) % TILE, 0))
            at = (line == jnp.where(half == 0, 4 + r, r)) & (place == 8)
            wet = jnp.where(at, pltpu.roll(shifted, (-r) % LANES, 1), wet)
    return [beyond(x, real) for x in (zm, mm, wet)]


def edge_columns(first, last):
    rows = first[0].shape[0]
    lane = lane_ids(rows)
    total = jnp.zeros((rows, LANES), F32)
    for level, (a, b) in enumerate(zip(first, last)):
        base = GROUP * level
        total = jnp.where((lane >= base + 8) & (lane < base + 16), pltpu.roll(a, base + 8, 1), total)
        total = jnp.where((lane >= base + 16) & (lane < base + 24), pltpu.roll(b, (base + 16 - 120) % LANES, 1), total)
    return total


def spread(value):
    value = value + pltpu.roll(value, GROUP, 1)
    return value + pltpu.roll(value, 2 * GROUP, 1)


def edge_coefficient(first, last):
    rows = first.shape[0]
    lane = lane_ids(rows)
    total = jnp.where((lane >= 8) & (lane < 16), pltpu.roll(first, 8, 1), 0.0)
    return spread(jnp.where((lane >= 16) & (lane < 24), pltpu.roll(last, 24, 1), total))


def outgoing(values, west):
    place = lane_ids(values[0].shape[0]) % GROUP
    start, step, source = (24, -4, 8) if west else (4, 4, 20)
    total = jnp.zeros(values[0].shape, F32)
    for k, value in enumerate(values):
        at = start + step * k
        total = jnp.where((place >= at) & (place < at + 4), pltpu.roll(value, (at - source) % LANES, 1), total)
    return total


def turn(ref, start, stride):
    return jnp.concatenate([ref[pl.ds(s, TILE, stride=stride), :] for s in start], axis=0).T


def refresh(ref, first, count):
    flat = ref.reshape(ref.shape[0] * DEPTH, LANES)

    def rows(j):
        return pl.ds(first * DEPTH + TILE + j, count, stride=DEPTH)

    flat[rows(-1), :] = pltpu.roll(flat[rows(LANES - 1), :], 1, 1)
    flat[rows(LANES), :] = pltpu.roll(flat[rows(0), :], LANES - 1, 1)


def sweep(source, target, east, north, first, last):
    for start in range(TILE, TILE + LANES, TILE):
        at, ahead, behind = (slice(start + d, start + d + TILE) for d in (0, 1, -1))
        here = source[first, at, :]
        south = north[first - 1, at, :] * (here - source[first - 1, at, :])
        for p in range(first, last + 1):
            above = source[p + 1, at, :]
            flux = north[p, at, :] * (above - here)
            go_east = east[p, at, :] * (source[p, ahead, :] - here)
            go_west = east[p, behind, :] * (here - source[p, behind, :])
            target[p, at, :] = here + go_east - go_west + flux - south
            here, south = above, flux


def faces(zm, mm, wet, cols, width, rows):
    after = slice(cols.start + LANES, cols.stop + LANES) if cols.stop < width else cols
    lane = lane_ids(rows)
    here = pltpu.roll(wet[:rows, cols], LANES - 1, 1)
    beyond = pltpu.roll(wet[:rows, after], LANES - 1, 1)
    east = zm[:, cols] * jnp.where(lane == LANES - 1, beyond, here)
    north = mm[:, cols] * wet[1 : rows + 1, cols]
    return east, north


def load_kernel(
    gy_size, members, increment, zonal, merid, mask,
    own, forcing, coef, east, north, pack_coef,
    mask_buf, zm, mm, wet, face, sems,
):
    _, tall, width = own.shape
    tiles = width // LANES
    planes = east.shape[0]
    offset = tall - planes
    half = half_of(gy_size)
    part = pl.ds(aligned(half * (tall - 2 * TILE)), tall)
    small = [
        pltpu.make_async_copy(mask.at[part, :], mask_buf, sems.at[0]),
        pltpu.make_async_copy(zonal.at[part, :], zm, sems.at[1]),
        pltpu.make_async_copy(merid.at[part, :], mm, sems.at[2]),
    ]
    large = [
        pltpu.make_async_copy(increment.at[:, part, :], forcing, sems.at[3]),
        pltpu.make_async_copy(members.at[0, :, part, :], own, sems.at[4]),
    ]
    for copy in small + large:
        copy.start()
    for copy in small:
        copy.wait()
    wet[:tall, :] = mask_buf[...].astype(F32)
    wet[tall:, :] = jnp.zeros((TILE, width), F32)
    zm[...] = zm[...] * wet[:tall, :]
    mm[...] = mm[...] * wet[:tall, :]
    outer = pl.ds(aligned(half * (tall - TILE)), TILE)
    for k, ref in enumerate((zm, mm, wet)):
        coef[k] = ref[outer, :]
    for c in range(tiles):
        face[pl.ds(c * tall, tall), :], face[pl.ds((tiles + c) * tall, tall), :] = faces(zm, mm, wet, tile(c), width, tall)
    for q in range(planes):
        for k, ref in enumerate((east, north)):
            ref[q, BODY, :] = turn(face, [k * tiles * tall + ch * offset + q for _ in range(TILE) for ch in range(2)], tall)
    refresh(east, 0, planes)
    ends = (tile(0), tile(tiles - 1))
    for k, ref in enumerate((zm, mm, wet)):
        pack_coef[k] = edge_coefficient(*(ref[:tall, cols] for cols in ends))
    large[0].wait()
    forcing[...] = forcing[...] * wet[:tall, :][None]
    large[1].wait()


def interior_kernel(
    gy_size, own, others, forcing, east, north,
    halfway, pack_other, weight_other,
    field, u, u_next,
):
    levels, tall, width = own.shape
    tiles = width // LANES
    mid = tall - TILE
    planes = east.shape[0]
    offset = tall - planes
    half = half_of(gy_size)
    part = pl.ds(aligned(half * (mid - TILE)), tall)
    keep_other = pl.ds(aligned(half * mid), mid)
    for c in range(tiles):
        cols = tile(c)
        for level in range(levels):
            force = forcing[level, :, cols]
            for k, member in enumerate((own[level, :, cols], others[0, level, part, cols])):
                field[pl.ds(((2 * level + k) * tiles + c) * tall, tall), :] = member * force

    def at(f, c):
        return field[pl.ds((f * tiles + c) * tall, tall), :]

    ends = (tile(0), tile(tiles - 1))
    pack_other[...] = edge_columns(*([at(2 * level + 1, c) for level in range(levels)] for c in (0, tiles - 1)))
    weight_other[...] = edge_columns(*([others[0, level, keep_other, cols] for level in range(levels)] for cols in ends))
    fields = range(2 * levels)
    for q in range(planes):
        u[q, BODY, :] = turn(field, [f * tiles * tall + ch * offset + q for f in fields for ch in range(2)], tall)
    buffers = [u, u_next, u][:FIRST_STEPS] + [halfway]
    for step in range(FIRST_STEPS):
        count = planes - 2 - 2 * step
        refresh(buffers[step], step + 1, count)
        sweep(buffers[step], buffers[step + 1], east, north, step + 1, step + count)
    refresh(halfway, FIRST_STEPS + 1, planes - 2 - 2 * FIRST_STEPS)


def interior_rest_kernel(gy_size, halfway, own, others, east, north, out, u, u_next, result):
    levels, tall, width = own.shape
    tiles = width // LANES
    mid = tall - TILE
    planes = east.shape[0]
    offset = tall - planes
    half = half_of(gy_size)
    keep_own, keep_other = pl.ds(aligned(half * TILE), mid), pl.ds(aligned(half * mid), mid)
    fields = range(2 * levels)
    source = halfway
    for step in range(FIRST_STEPS, STEPS):
        count = planes - 2 - 2 * step
        if step > FIRST_STEPS:
            refresh(source, step + 1, count)
        target = u if step % 2 == 0 else u_next
        sweep(source, target, east, north, step + 1, step + count)
        source = target
    for q in range(STEPS, planes - STEPS):
        flat = source[q, BODY, :].T
        for f in fields:
            for ch in range(2):
                group = (2 * f + ch) * tiles
                result[pl.ds(f * tiles * tall + ch * offset + q, tiles, stride=tall), :] = flat[group : group + tiles]
    for level in range(levels):
        for c in range(tiles):
            a, b = (
                result[pl.ds(aligned(((2 * level + k) * tiles + c) * tall + half * TILE), mid), :] for k in range(2)
            )
            out[level, :, tile(c)] = own[level, keep_own, tile(c)] * a + others[0, level, keep_other, tile(c)] * b


def halo_columns_kernel(
    gy_size, strip, pack_own, pack_other, pack_coef, full_own, full_other, full_coef, west_out, east_out
):
    half = half_of(gy_size)
    tall = pack_own.shape[0]
    halo = pl.ds(aligned(half * tall), TILE)
    main = pl.ds(aligned((1 - half) * TILE), tall)
    local = [pack_own[...], pack_other[...]] + [pack_coef[k] for k in range(3)]
    corner = strip.shape[0] - 2 * TILE
    fields = [unfold(gy_size, strip[corner : corner + TILE, :], k) for k in range(2)]
    received = fields + unfold_weights(gy_size, strip[corner + TILE :, :], True)
    full = [full_own, full_other] + [full_coef.at[k] for k in range(3)]
    for rows, values in ((main, local), (halo, received)):
        west_out[rows, :] = outgoing(values, True)
        east_out[rows, :] = outgoing(values, False)
    for ref, inner, outer in zip(full, local, received):
        ref[main, :] = inner
        ref[halo, :] = outer


def outer_rows_kernel(
    gy_size, inside, strip, own, other, forcing, coef, sums,
    zm, mm, wet, field, face, u, u_next, east, north, result,
):
    levels, tall, width = own.shape
    tiles = width // LANES
    half = half_of(gy_size)
    outer = pl.ds(aligned(half * (tall - TILE)), TILE)
    edge = pl.ds(aligned((1 - half) * TILE), TILE)
    halo = pl.ds(aligned(half * TILE), TILE)
    block = 2 * TILE
    for k, ref in enumerate((zm, mm, wet)):
        ref[edge, :] = coef[k]
    for c in range(tiles):
        values = unfold_weights(gy_size, strip[strip_rows(levels, c, tiles), :], False)
        for ref, value in zip((zm, mm, wet), values):
            ref[halo, tile(c)] = value
    wet[block:, :] = jnp.zeros((TILE, width), F32)
    for c in range(tiles):
        cols = tile(c)
        face[pl.ds(c * block, block), :], face[pl.ds((tiles + c) * block, block), :] = faces(zm, mm, wet, cols, width, block)
        for level in range(levels):
            for k, member in enumerate((own[level, outer, cols], other[level, :, cols])):
                base = ((2 * level + k) * tiles + c) * block
                field[pl.ds(aligned(base + (1 - half) * TILE), TILE), :] = member * forcing[level, outer, cols]
                field[pl.ds(aligned(base + half * TILE), TILE), :] = unfold(gy_size, strip[strip_rows(level, c, tiles), :], k)

    fields = range(2 * levels)
    planes = 10
    lead = (1 - half) * 4
    for q in range(planes):
        u[q, BODY, :] = turn(field, [f * tiles * block + 2 * ch + q + lead for f in fields for ch in range(2)], block)
        for k, ref in enumerate((east, north)):
            if q == planes - 1 or (k == 0 and q == 0):
                continue
            ref[q, BODY, :] = turn(face, [k * tiles * block + 2 * ch + q + lead for f in fields for ch in range(2)], block)
    refresh(east, 0, planes)
    source, target = u, u_next
    for step in range(STEPS):
        count = planes - 2 - 2 * step
        refresh(source, step + 1, count)
        sweep(source, target, east, north, step + 1, step + count)
        source, target = target, source
    for p in range(2):
        flat = source[STEPS + p, BODY, :].T
        for f in fields:
            for ch in range(2):
                group = (2 * f + ch) * tiles
                result[pl.ds(f * tiles * TILE + 4 * half + 2 * ch + p, tiles, stride=TILE), :] = flat[group : group + tiles]
    mine = row_ids(TILE, LANES) // 4 == half
    place = pl.ds(aligned(half * (tall - 2 * TILE)), TILE)
    for c in range(tiles):
        cols = tile(c)
        for level in range(levels):
            a, b = (result[pl.ds(((2 * level + k) * tiles + c) * TILE, TILE), :] for k in range(2))
            term = own[level, outer, cols] * a + other[level, :, cols] * b
            sums[level, place, cols] = jnp.where(mine, term, sums[level, place, cols])


def end_columns_kernel(
    gy_size, from_west, from_east, own, other, coef, weight_own, weight_other, out,
    a, b, a_next, b_next, east, north, wet,
):
    full = own.shape[0]
    body = pl.ds(TILE, full)
    place = lane_ids(full) % GROUP
    on_west = (place >= 4) & (place < 8)
    on_east = (place >= 24) & (place < 28)
    west, east_strip = from_west[...], from_east[...]

    def with_ends(value, k):
        value = jnp.where(on_west, pltpu.roll(west, (-4 * k) % LANES, 1), value)
        return jnp.where(on_east, pltpu.roll(east_strip, 4 * k, 1), value)

    blank = jnp.zeros((TILE, LANES), F32)
    for ref in (a, b, a_next, b_next, east, north, wet):
        ref[:TILE, :] = blank
        ref[full + TILE :, :] = blank
    a[body, :] = with_ends(own[...], 0)
    b[body, :] = with_ends(other[...], 1)
    wet[body, :] = with_ends(coef[2], 4)
    east[body, :] = with_ends(coef[0], 2) * pltpu.roll(wet[body, :], LANES - 1, 1)
    north[body, :] = with_ends(coef[1], 3) * wet[pl.ds(TILE + 1, full), :]
    now, later = (a, b), (a_next, b_next)
    for step in range(STEPS):
        for t in range(TILE, full + TILE, TILE):
            at, above, below = (pl.ds(t + d, TILE) for d in (0, 1, -1))
            e, n, s = east[at, :], north[at, :], north[below, :]
            for source, target in zip(now, later):
                here = source[at, :]
                flux = e * (pltpu.roll(here, LANES - 1, 1) - here)
                go_north = n * (source[above, :] - here)
                go_south = s * (here - source[below, :])
                target[at, :] = here + flux - pltpu.roll(flux, 1, 1) + go_north - go_south
        now, later = later, now
    mid = weight_own.shape[0]
    rows = pl.ds(2 * TILE, mid)
    out[...] = weight_own[...] * now[0][rows, :] + weight_other[...] * now[1][rows, :]


def join_kernel(gy_size, mine_in, theirs_in, mine_edge, theirs_edge, mine, theirs, out, sems):
    half = half_of(gy_size)
    levels, mid, width = mine.shape
    lane = lane_ids(mid)
    first, last = slice(0, LANES), slice(width - LANES, width)
    copies = []
    for k, (ref, edges, where) in enumerate(((mine, mine_edge, half), (theirs, theirs_edge, 1 - half))):
        packed = edges[...]
        for level in range(levels):
            base = GROUP * level
            ref[level, :, first] = jnp.where(lane < 4, pltpu.roll(packed, (-base - 8) % LANES, 1), ref[level, :, first])
            ref[level, :, last] = jnp.where(
                lane >= LANES - 4, pltpu.roll(packed, (LANES - 4 - base - 20) % LANES, 1), ref[level, :, last]
            )
            copies.append(
                pltpu.make_async_copy(
                    ref.at[level], out.at[level, pl.ds(aligned(where * mid), mid), :], sems.at[k, level]
                )
            )
            copies[-1].start()
    for copy in copies:
        copy.wait()


def shards(sizes, increment, members, zonal_diff, merid_diff, sea_mask):
    n_mem, n_gy, n_gx = sizes
    levels, rows, width = increment.shape
    tiles = width // LANES
    mid = rows // 2
    tall = mid + TILE
    full = tall + TILE
    planes = 3 * TILE
    assert tiles == TILE and 4 * levels * tiles == LANES and tall == 5 * TILE and n_mem % 2 == 0

    def call(kernel, ins, specs, outs, scratch=(), out_specs=None, aliases={}):
        return pl.pallas_call(
            functools.partial(kernel, n_gy),
            out_shape=outs,
            in_specs=specs,
            out_specs=out_specs if out_specs is not None else jax.tree.map(lambda _: VMEM, outs),
            scratch_shapes=scratch,
            input_output_aliases=aliases,
            compiler_params=pltpu.CompilerParams(vmem_limit_bytes=40 * 1024 * 1024),
        )(*ins)

    def held(kernel, ins, outs, scratch=(), **kw):
        got = call(kernel, [pinned(x) for x in ins], [VMEM] * len(ins), outs, scratch, **kw)
        return got

    def swap(x):
        return lax.ppermute(x, "mem", [(i, i ^ 1) for i in range(n_mem)])

    def along(x, shift):
        return lax.ppermute(x, "gx", [(i, (i + shift) % n_gx) for i in range(n_gx)])

    def across(x):
        def place(chip, core, j, i):
            return ((2 * chip + core) * n_gy + j) * n_gx + i

        first = [0 if j < n_gy // 2 else 1 for j in range(n_gy)]
        pairs = []
        for chip in range(n_mem // 2):
            for j in range(n_gy - 1):
                for i in range(n_gx):
                    a = place(chip, 1 - first[j], j, i)
                    b = place(chip, first[j + 1], j + 1, i)
                    pairs += [(a, b), (b, a)]
            for i in range(n_gx - n_gx % 2):
                pairs.append((place(chip, first[0], 0, i), place(chip, first[0], 0, i ^ 1)))
                pairs.append((place(chip, 1 - first[-1], n_gy - 1, i), place(chip, 1 - first[-1], n_gy - 1, i ^ 1)))
        return lax.ppermute(x, AXES, pairs)

    def scratch(*shape):
        return pltpu.VMEM(shape, F32)

    others = swap(members)
    end = kept(full, LANES)
    turned = kept(planes, DEPTH, LANES)
    own, forcing, coef, face_east, face_north, pack_coef = call(
        load_kernel,
        [in_hbm(x) for x in (members, increment, zonal_diff, merid_diff, sea_mask)],
        [HBM] * 5,
        [kept(levels, tall, width)] * 2
        + [kept(3, TILE, width), turned, turned, kept(3, tall, LANES)],
        [
            pltpu.VMEM((tall, width), jnp.int32),
            scratch(tall, width),
            scratch(tall, width),
            scratch(full, width),
            scratch(2 * tiles * tall, LANES),
            pltpu.SemaphoreType.DMA((5,)),
        ],
    )
    packed = kept(tall, LANES)
    weights, coef_ends, pack_own, weight_own = held(
        own_ends_kernel, [own, forcing, coef], [kept(TILE, width), kept(TILE, LANES), packed, kept(mid, LANES)]
    )
    other, strip = held(
        pack_rows_kernel,
        [own, others, forcing, weights, coef_ends],
        [kept(levels, TILE, width), kept((levels + 1) * tiles * TILE + 2 * TILE, LANES)],
    )
    forcing, strip = lax.optimization_barrier((forcing, strip))
    strip = across(strip)
    halfway, pack_other, weight_other = held(
        interior_kernel,
        [own, others, forcing, face_east, face_north],
        [turned, packed, kept(mid, LANES)],
        [scratch(2 * levels * tiles * tall, LANES), scratch(planes, DEPTH, LANES), scratch(planes, DEPTH, LANES)],
    )
    inside = held(
        interior_rest_kernel,
        [halfway, own, others, face_east, face_north],
        kept(levels, mid, width),
        [
            scratch(planes, DEPTH, LANES),
            scratch(planes, DEPTH, LANES),
            scratch(2 * levels * tiles * tall, LANES),
        ],
    )
    inside, pack_other = lax.optimization_barrier((inside, pack_other))
    full_own, full_other, full_coef, west, east = held(
        halo_columns_kernel,
        [strip, pack_own, pack_other, pack_coef],
        [end, end, kept(3, full, LANES), end, end],
    )
    from_west = along(east, 1)
    from_east = along(west, -1)
    inside = held(
        outer_rows_kernel,
        [inside, strip, own, other, forcing, coef],
        kept(levels, mid, width),
        [
            scratch(2 * TILE, width),
            scratch(2 * TILE, width),
            scratch(3 * TILE, width),
            scratch(2 * levels * tiles * 2 * TILE, LANES),
            scratch(2 * tiles * 2 * TILE, LANES),
            scratch(10, DEPTH, LANES),
            scratch(10, DEPTH, LANES),
            scratch(10, DEPTH, LANES),
            scratch(10, DEPTH, LANES),
            scratch(2 * levels * tiles * TILE, LANES),
        ],
        aliases={0: 0},
    )
    inside, from_west, from_east = lax.optimization_barrier((inside, from_west, from_east))
    edges = held(
        end_columns_kernel,
        [from_west, from_east, full_own, full_other, full_coef, weight_own, weight_other],
        kept(mid, LANES),
        [scratch(full + 2 * TILE, LANES)] * 7,
    )
    if n_mem > 2:
        groups = [list(range(k, n_mem, 2)) for k in range(2)]
        inside, edges = (lax.psum(x, "mem", axis_index_groups=groups) for x in (inside, edges))
    inside_theirs, edges_theirs = swap(inside), swap(edges)
    return held(
        join_kernel,
        [inside, inside_theirs, edges, edges_theirs],
        [kept(levels, mid, width)] * 2 + [jax.ShapeDtypeStruct(increment.shape, F32)],
        [pltpu.SemaphoreType.DMA((2, levels))],
        out_specs=[VMEM, VMEM, HBM],
        aliases={0: 0, 1: 1},
    )[2]


def solution(mesh):
    return jax.shard_map(
        functools.partial(shards, tuple(mesh.shape[axis] for axis in AXES)),
        mesh=mesh,
        in_specs=(
            P(None, "gy", "gx"),
            P("mem", None, "gy", "gx"),
            P("gy", "gx"),
            P("gy", "gx"),
            P("gy", "gx"),
        ),
        out_specs=P(None, "gy", "gx"),
        check_vma=False,
    )
```

```python
import functools
import jax
import jax.numpy as jnp
from jax import lax
from jax.experimental import pallas as pl
from jax.experimental.pallas import tpu as pltpu
from jax.sharding import PartitionSpec as P

STEPS = 4
FIRST_STEPS = 2
TILE = 8
LANES = 128
AXES = ("mem", "gy", "gx")
F32 = jnp.float32
VMEM = pl.BlockSpec(memory_space=pltpu.VMEM)
HBM = pl.BlockSpec(memory_space=pltpu.HBM)

BODY = slice(TILE, TILE + LANES)
DEPTH = LANES + 2 * TILE
GROUP = 32


def half_of(gy_size):
    core = lax.rem(lax.axis_index("mem"), 2)
    later = (lax.axis_index("gy") >= gy_size // 2).astype(jnp.int32)
    return lax.rem(core + later, 2)


def kept(*shape):
    return pltpu.VMEM(shape, F32)


def pinned(x):
    return pltpu.with_memory_space_constraint(x, pltpu.VMEM)


def in_hbm(x):
    return pltpu.with_memory_space_constraint(x, pltpu.HBM)


def tile(c):
    return slice(c * LANES, (c + 1) * LANES)


def lane_ids(rows):
    return lax.broadcasted_iota(jnp.int32, (rows, LANES), 1)


def row_ids(rows, width):
    return lax.broadcasted_iota(jnp.int32, (rows, width), 0)


def aligned(start):
    return pl.multiple_of(start, TILE)


def run(copies):
    for copy in copies:
        copy.start()
    for copy in copies:
        copy.wait()


def own_ends_kernel(gy_size, own, forcing, coef, out, ends, pack_own, weight_own):
    half = half_of(gy_size)
    width = out.shape[1]
    zm, mm, wet = coef[0], coef[1], coef[2]
    row = row_ids(TILE, width)
    col = lax.broadcasted_iota(jnp.int32, (TILE, width), 1)
    east = zm * jnp.where(col == width - 1, 1.0, pltpu.roll(wet, width - 1, 1))
    north = mm * jnp.where(row == TILE - 1, 1.0, pltpu.roll(wet, TILE - 1, 0))
    upper = jnp.where(row < 4, north, pltpu.roll(east, 4, 0))
    upper = jnp.where(row == 3, pltpu.roll(wet, 3, 0), upper)
    lower = jnp.where(row < 4, pltpu.roll(north, 4, 0), east)
    out[...] = jnp.where(half == 0, upper, lower)
    first = wet[:, :LANES]
    lane, line = lane_ids(TILE), row_ids(TILE, LANES)
    value = out[:, :LANES]
    for r in range(4):
        moved = jnp.where(half == 0, pltpu.roll(first, 7 - r, 0), pltpu.roll(first, (-r) % TILE, 0))
        value = jnp.where((line == jnp.where(half == 0, 7, 4)) & (lane == r), pltpu.roll(moved, r, 1), value)
    out[:, :LANES] = value
    both = (tile(0), slice(width - LANES, width))
    ends[...] = edge_coefficient(*(out[:, cols] for cols in both))
    levels, tall, _ = own.shape
    pack_own[...] = edge_columns(*([own[l, :, cols] * forcing[l, :, cols] for l in range(levels)] for cols in both))
    keep = pl.ds(aligned(half * TILE), tall - TILE)
    weight_own[...] = edge_columns(*([own[l, keep, cols] for l in range(levels)] for cols in both))


def outer_rows_of(gy_size, level, own, other, forcing, cols):
    half = half_of(gy_size)
    j = lax.axis_index("gy")
    same_core = jnp.where(half == 0, j == gy_size // 2, j == gy_size // 2 - 1)
    outer = pl.ds(aligned(half * (own.shape[1] - TILE)), TILE)
    force = forcing[level, outer, cols]
    mine = own[level, outer, cols] * force
    theirs = other[level, :, cols] * force
    first, second = jnp.where(same_core, mine, theirs), jnp.where(same_core, theirs, mine)
    first = jnp.where(half == 0, first, pltpu.roll(first, TILE // 2, 0))
    second = jnp.where(half == 0, pltpu.roll(second, TILE // 2, 0), second)
    return jnp.where(row_ids(*first.shape) < TILE // 2, first, second)


def pack_rows_kernel(gy_size, own, others, forcing, weights, coef_ends, other, strip, more):
    levels, _, width = own.shape
    tiles = width // LANES
    other[...] = others[0, :, pl.ds(aligned(half_of(gy_size) * (others.shape[2] - TILE)), TILE), :]
    ends = ([], [])
    for c in range(tiles):
        for level in range(levels):
            rows = outer_rows_of(gy_size, level, own, other, forcing, tile(c))
            part, place = strip_place(level, levels, (strip, more))
            part[strip_rows(place, c, tiles), :] = rows
            if c in (0, tiles - 1):
                ends[c > 0].append(rows)
        strip[strip_rows(levels // 2, c, tiles), :] = weights[:, tile(c)]
    last = (levels // 2 + 1) * tiles * TILE
    strip[last : last + TILE, :] = edge_columns(*ends)
    strip[last + TILE :, :] = coef_ends[...]


def strip_place(level, levels, parts):
    return parts[level // (levels // 2)], level % (levels // 2)


def strip_rows(place, c, tiles):
    return slice((place * tiles + c) * TILE, (place * tiles + c + 1) * TILE)


def inside_domain(gy_size):
    half, j = half_of(gy_size), lax.axis_index("gy")
    return jnp.where(half == 0, j > 0, j < gy_size - 1)


def beyond(value, real):
    return jnp.where(real, value, 0.0)


def unfold(gy_size, value, place):
    natural = jnp.equal(half_of(gy_size), 1 - place % 2)
    return beyond(jnp.where(natural, value, pltpu.roll(value, TILE // 2, 0)), inside_domain(gy_size))


def unfold_weights(gy_size, value, packed):
    half, real = half_of(gy_size), inside_domain(gy_size)
    moved = pltpu.roll(value, TILE // 2, 0)
    zm = jnp.where(half == 0, value, moved)
    mm = jnp.where(half == 0, moved, value)
    line = row_ids(*value.shape)
    wet = jnp.where((half == 1) & (line == 0), pltpu.roll(value, 5, 0), 1.0)
    if packed:
        place = lane_ids(TILE) % GROUP
        for r in range(4):
            shifted = jnp.where(half == 0, pltpu.roll(value, r, 0), pltpu.roll(value, (r + 1) % TILE, 0))
            at = (line == jnp.where(half == 0, 4 + r, r)) & (place == 8)
            wet = jnp.where(at, pltpu.roll(shifted, (-r) % LANES, 1), wet)
    return [beyond(x, real) for x in (zm, mm, wet)]


def edge_columns(first, last):
    rows = first[0].shape[0]
    lane = lane_ids(rows)
    total = jnp.zeros((rows, LANES), F32)
    for level, (a, b) in enumerate(zip(first, last)):
        base = GROUP * level
        total = jnp.where((lane >= base + 8) & (lane < base + 16), pltpu.roll(a, base + 8, 1), total)
        total = jnp.where((lane >= base + 16) & (lane < base + 24), pltpu.roll(b, (base + 16 - 120) % LANES, 1), total)
    return total


def spread(value):
    value = value + pltpu.roll(value, GROUP, 1)
    return value + pltpu.roll(value, 2 * GROUP, 1)


def edge_coefficient(first, last):
    rows = first.shape[0]
    lane = lane_ids(rows)
    total = jnp.where((lane >= 8) & (lane < 16), pltpu.roll(first, 8, 1), 0.0)
    return spread(jnp.where((lane >= 16) & (lane < 24), pltpu.roll(last, 24, 1), total))


def outgoing(values, west):
    place = lane_ids(values[0].shape[0]) % GROUP
    start, step, source = (24, -4, 8) if west else (4, 4, 20)
    total = jnp.zeros(values[0].shape, F32)
    for k, value in enumerate(values):
        at = start + step * k
        total = jnp.where((place >= at) & (place < at + 4), pltpu.roll(value, (at - source) % LANES, 1), total)
    return total


def turn(ref, start, stride):
    return jnp.concatenate([ref[pl.ds(s, TILE, stride=stride), :] for s in start], axis=0).T


def refresh(ref, first, count):
    flat = ref.reshape(ref.shape[0] * DEPTH, LANES)

    def rows(j):
        return pl.ds(first * DEPTH + TILE + j, count, stride=DEPTH)

    flat[rows(-1), :] = pltpu.roll(flat[rows(LANES - 1), :], 1, 1)
    flat[rows(LANES), :] = pltpu.roll(flat[rows(0), :], LANES - 1, 1)


def sweep(source, target, east, north, first, last):
    for start in range(TILE, TILE + LANES, TILE):
        at, ahead, behind = (slice(start + d, start + d + TILE) for d in (0, 1, -1))
        here = source[first, at, :]
        south = north[first - 1, at, :] * (here - source[first - 1, at, :])
        for p in range(first, last + 1):
            above = source[p + 1, at, :]
            flux = north[p, at, :] * (above - here)
            go_east = east[p, at, :] * (source[p, ahead, :] - here)
            go_west = east[p, behind, :] * (here - source[p, behind, :])
            target[p, at, :] = here + go_east - go_west + flux - south
            here, south = above, flux


def faces(zm, mm, wet, cols, width, rows):
    after = slice(cols.start + LANES, cols.stop + LANES) if cols.stop < width else cols
    lane = lane_ids(rows)
    here = pltpu.roll(wet[:rows, cols], LANES - 1, 1)
    beyond = pltpu.roll(wet[:rows, after], LANES - 1, 1)
    east = zm[:, cols] * jnp.where(lane == LANES - 1, beyond, here)
    north = mm[:, cols] * wet[1 : rows + 1, cols]
    return east, north


def load_kernel(
    gy_size, members, increment, zonal, merid, mask,
    own, forcing, coef, east, north, pack_coef,
    mask_buf, zm, mm, wet, face, sems,
):
    _, tall, width = own.shape
    tiles = width // LANES
    planes = east.shape[0]
    offset = tall - planes
    half = half_of(gy_size)
    part = pl.ds(aligned(half * (tall - 2 * TILE)), tall)
    small = [
        pltpu.make_async_copy(mask.at[part, :], mask_buf, sems.at[0]),
        pltpu.make_async_copy(zonal.at[part, :], zm, sems.at[1]),
        pltpu.make_async_copy(merid.at[part, :], mm, sems.at[2]),
    ]
    large = [
        pltpu.make_async_copy(increment.at[:, part, :], forcing, sems.at[3]),
        pltpu.make_async_copy(members.at[0, :, part, :], own, sems.at[4]),
    ]
    for copy in small + large:
        copy.start()
    for copy in small:
        copy.wait()
    wet[:tall, :] = mask_buf[...].astype(F32)
    wet[tall:, :] = jnp.zeros((TILE, width), F32)
    zm[...] = zm[...] * wet[:tall, :]
    mm[...] = mm[...] * wet[:tall, :]
    outer = pl.ds(aligned(half * (tall - TILE)), TILE)
    for k, ref in enumerate((zm, mm, wet)):
        coef[k] = ref[outer, :]
    for c in range(tiles):
        face[pl.ds(c * tall, tall), :], face[pl.ds((tiles + c) * tall, tall), :] = faces(zm, mm, wet, tile(c), width, tall)
    for q in range(planes):
        for k, ref in enumerate((east, north)):
            ref[q, BODY, :] = turn(face, [k * tiles * tall + ch * offset + q for _ in range(TILE) for ch in range(2)], tall)
    refresh(east, 0, planes)
    ends = (tile(0), tile(tiles - 1))
    for k, ref in enumerate((zm, mm, wet)):
        pack_coef[k] = edge_coefficient(*(ref[:tall, cols] for cols in ends))
    large[0].wait()
    forcing[...] = forcing[...] * wet[:tall, :][None]
    large[1].wait()


def interior_kernel(
    gy_size, own, others, forcing, east, north,
    halfway, pack_other, weight_other,
    field, u, u_next,
):
    levels, tall, width = own.shape
    tiles = width // LANES
    mid = tall - TILE
    planes = east.shape[0]
    offset = tall - planes
    half = half_of(gy_size)
    part = pl.ds(aligned(half * (mid - TILE)), tall)
    keep_other = pl.ds(aligned(half * mid), mid)
    for c in range(tiles):
        cols = tile(c)
        for level in range(levels):
            force = forcing[level, :, cols]
            for k, member in enumerate((own[level, :, cols], others[0, level, part, cols])):
                field[pl.ds(((2 * level + k) * tiles + c) * tall, tall), :] = member * force

    def at(f, c):
        return field[pl.ds((f * tiles + c) * tall, tall), :]

    ends = (tile(0), tile(tiles - 1))
    pack_other[...] = edge_columns(*([at(2 * level + 1, c) for level in range(levels)] for c in (0, tiles - 1)))
    weight_other[...] = edge_columns(*([others[0, level, keep_other, cols] for level in range(levels)] for cols in ends))
    fields = range(2 * levels)
    for q in range(planes):
        u[q, BODY, :] = turn(field, [f * tiles * tall + ch * offset + q for f in fields for ch in range(2)], tall)
    buffers = [u, u_next, u][:FIRST_STEPS] + [halfway]
    for step in range(FIRST_STEPS):
        count = planes - 2 - 2 * step
        refresh(buffers[step], step + 1, count)
        sweep(buffers[step], buffers[step + 1], east, north, step + 1, step + count)
    refresh(halfway, FIRST_STEPS + 1, planes - 2 - 2 * FIRST_STEPS)


def interior_rest_kernel(gy_size, halfway, own, others, east, north, out, u, u_next, result):
    levels, tall, width = own.shape
    tiles = width // LANES
    mid = tall - TILE
    planes = east.shape[0]
    offset = tall - planes
    half = half_of(gy_size)
    keep_own, keep_other = pl.ds(aligned(half * TILE), mid), pl.ds(aligned(half * mid), mid)
    fields = range(2 * levels)
    source = halfway
    for step in range(FIRST_STEPS, STEPS):
        count = planes - 2 - 2 * step
        if step > FIRST_STEPS:
            refresh(source, step + 1, count)
        target = u if step % 2 == 0 else u_next
        sweep(source, target, east, north, step + 1, step + count)
        source = target
    for q in range(STEPS, planes - STEPS):
        flat = source[q, BODY, :].T
        for f in fields:
            for ch in range(2):
                group = (2 * f + ch) * tiles
                result[pl.ds(f * tiles * tall + ch * offset + q, tiles, stride=tall), :] = flat[group : group + tiles]
    for level in range(levels):
        for c in range(tiles):
            a, b = (
                result[pl.ds(aligned(((2 * level + k) * tiles + c) * tall + half * TILE), mid), :] for k in range(2)
            )
            out[level, :, tile(c)] = own[level, keep_own, tile(c)] * a + others[0, level, keep_other, tile(c)] * b


def halo_columns_kernel(
    gy_size, strip, pack_own, pack_other, pack_coef, full_own, full_other, full_coef, west_out, east_out
):
    half = half_of(gy_size)
    tall = pack_own.shape[0]
    halo = pl.ds(aligned(half * tall), TILE)
    main = pl.ds(aligned((1 - half) * TILE), tall)
    local = [pack_own[...], pack_other[...]] + [pack_coef[k] for k in range(3)]
    corner = strip.shape[0] - 2 * TILE
    fields = [unfold(gy_size, strip[corner : corner + TILE, :], k) for k in range(2)]
    received = fields + unfold_weights(gy_size, strip[corner + TILE :, :], True)
    full = [full_own, full_other] + [full_coef.at[k] for k in range(3)]
    for rows, values in ((main, local), (halo, received)):
        west_out[rows, :] = outgoing(values, True)
        east_out[rows, :] = outgoing(values, False)
    for ref, inner, outer in zip(full, local, received):
        ref[main, :] = inner
        ref[halo, :] = outer


def outer_rows_kernel(
    gy_size, inside, strip, more, own, other, forcing, coef, sums,
    zm, mm, wet, field, face, u, u_next, east, north, result,
):
    levels, tall, width = own.shape
    tiles = width // LANES
    half = half_of(gy_size)
    outer = pl.ds(aligned(half * (tall - TILE)), TILE)
    edge = pl.ds(aligned((1 - half) * TILE), TILE)
    halo = pl.ds(aligned(half * TILE), TILE)
    block = 2 * TILE
    for k, ref in enumerate((zm, mm, wet)):
        ref[edge, :] = coef[k]
    for c in range(tiles):
        values = unfold_weights(gy_size, strip[strip_rows(levels // 2, c, tiles), :], False)
        for ref, value in zip((zm, mm, wet), values):
            ref[halo, tile(c)] = value
    wet[block:, :] = jnp.zeros((TILE, width), F32)
    for c in range(tiles):
        cols = tile(c)
        face[pl.ds(c * block, block), :], face[pl.ds((tiles + c) * block, block), :] = faces(zm, mm, wet, cols, width, block)
        for level in range(levels):
            part, where = strip_place(level, levels, (strip, more))
            for k, member in enumerate((own[level, outer, cols], other[level, :, cols])):
                base = ((2 * level + k) * tiles + c) * block
                field[pl.ds(aligned(base + (1 - half) * TILE), TILE), :] = member * forcing[level, outer, cols]
                field[pl.ds(aligned(base + half * TILE), TILE), :] = unfold(gy_size, part[strip_rows(where, c, tiles), :], k)

    fields = range(2 * levels)
    planes = 10
    lead = (1 - half) * 4
    for q in range(planes):
        u[q, BODY, :] = turn(field, [f * tiles * block + 2 * ch + q + lead for f in fields for ch in range(2)], block)
        for k, ref in enumerate((east, north)):
            if q == planes - 1 or (k == 0 and q == 0):
                continue
            ref[q, BODY, :] = turn(face, [k * tiles * block + 2 * ch + q + lead for f in fields for ch in range(2)], block)
    refresh(east, 0, planes)
    source, target = u, u_next
    for step in range(STEPS):
        count = planes - 2 - 2 * step
        refresh(source, step + 1, count)
        sweep(source, target, east, north, step + 1, step + count)
        source, target = target, source
    for p in range(2):
        flat = source[STEPS + p, BODY, :].T
        for f in fields:
            for ch in range(2):
                group = (2 * f + ch) * tiles
                result[pl.ds(f * tiles * TILE + 4 * half + 2 * ch + p, tiles, stride=TILE), :] = flat[group : group + tiles]
    mine = row_ids(TILE, LANES) // 4 == half
    place = pl.ds(aligned(half * (tall - 2 * TILE)), TILE)
    for c in range(tiles):
        cols = tile(c)
        for level in range(levels):
            a, b = (result[pl.ds(((2 * level + k) * tiles + c) * TILE, TILE), :] for k in range(2))
            term = own[level, outer, cols] * a + other[level, :, cols] * b
            sums[level, place, cols] = jnp.where(mine, term, sums[level, place, cols])


def end_columns_kernel(
    gy_size, from_west, from_east, own, other, coef, weight_own, weight_other, out,
    a, b, a_next, b_next, east, north, wet,
):
    full = own.shape[0]
    body = pl.ds(TILE, full)
    place = lane_ids(full) % GROUP
    on_west = (place >= 4) & (place < 8)
    on_east = (place >= 24) & (place < 28)
    west, east_strip = from_west[...], from_east[...]

    def with_ends(value, k):
        value = jnp.where(on_west, pltpu.roll(west, (-4 * k) % LANES, 1), value)
        return jnp.where(on_east, pltpu.roll(east_strip, 4 * k, 1), value)

    blank = jnp.zeros((TILE, LANES), F32)
    for ref in (a, b, a_next, b_next, east, north, wet):
        ref[:TILE, :] = blank
        ref[full + TILE :, :] = blank
    a[body, :] = with_ends(own[...], 0)
    b[body, :] = with_ends(other[...], 1)
    wet[body, :] = with_ends(coef[2], 4)
    east[body, :] = with_ends(coef[0], 2) * pltpu.roll(wet[body, :], LANES - 1, 1)
    north[body, :] = with_ends(coef[1], 3) * wet[pl.ds(TILE + 1, full), :]
    now, later = (a, b), (a_next, b_next)
    for step in range(STEPS):
        for t in range(TILE, full + TILE, TILE):
            at, above, below = (pl.ds(t + d, TILE) for d in (0, 1, -1))
            e, n, s = east[at, :], north[at, :], north[below, :]
            for source, target in zip(now, later):
                here = source[at, :]
                flux = e * (pltpu.roll(here, LANES - 1, 1) - here)
                go_north = n * (source[above, :] - here)
                go_south = s * (here - source[below, :])
                target[at, :] = here + flux - pltpu.roll(flux, 1, 1) + go_north - go_south
        now, later = later, now
    mid = weight_own.shape[0]
    rows = pl.ds(2 * TILE, mid)
    out[...] = weight_own[...] * now[0][rows, :] + weight_other[...] * now[1][rows, :]


def join_kernel(gy_size, mine_in, theirs_in, mine_edge, theirs_edge, mine, theirs, out, sems):
    half = half_of(gy_size)
    levels, mid, width = mine.shape
    lane = lane_ids(mid)
    first, last, between = slice(0, LANES), slice(width - LANES, width), slice(LANES, width - LANES)
    halves = ((mine, mine_edge, half), (theirs, theirs_edge, 1 - half))
    copies = []

    def send(k, cols, place):
        ref, _, where = halves[k]
        rows = pl.ds(aligned(where * mid), mid)
        copies.append(pltpu.make_async_copy(ref.at[:, :, cols], out.at[:, rows, cols], sems.at[k, place]))
        copies[-1].start()

    for k in range(2):
        send(k, between, 0)
    for k, (ref, edges, _) in enumerate(halves):
        packed = edges[...]
        for level in range(levels):
            base = GROUP * level
            ref[level, :, first] = jnp.where(lane < 4, pltpu.roll(packed, (-base - 8) % LANES, 1), ref[level, :, first])
        send(k, first, 1)
        for level in range(levels):
            base = GROUP * level
            ref[level, :, last] = jnp.where(
                lane >= LANES - 4, pltpu.roll(packed, (LANES - 4 - base - 20) % LANES, 1), ref[level, :, last]
            )
        send(k, last, 2)
    for copy in copies:
        copy.wait()


def shards(sizes, increment, members, zonal_diff, merid_diff, sea_mask):
    n_mem, n_gy, n_gx = sizes
    levels, rows, width = increment.shape
    tiles = width // LANES
    mid = rows // 2
    tall = mid + TILE
    full = tall + TILE
    planes = 3 * TILE
    assert tiles == TILE and 4 * levels * tiles == LANES and tall == 5 * TILE and n_mem % 2 == 0

    def call(kernel, ins, specs, outs, scratch=(), out_specs=None, aliases={}):
        return pl.pallas_call(
            functools.partial(kernel, n_gy),
            out_shape=outs,
            in_specs=specs,
            out_specs=out_specs if out_specs is not None else jax.tree.map(lambda _: VMEM, outs),
            scratch_shapes=scratch,
            input_output_aliases=aliases,
            compiler_params=pltpu.CompilerParams(vmem_limit_bytes=40 * 1024 * 1024),
        )(*ins)

    def held(kernel, ins, outs, scratch=(), **kw):
        got = call(kernel, [pinned(x) for x in ins], [VMEM] * len(ins), outs, scratch, **kw)
        return got

    def swap(x):
        return lax.ppermute(x, "mem", [(i, i ^ 1) for i in range(n_mem)])

    def along(x, shift):
        return lax.ppermute(x, "gx", [(i, (i + shift) % n_gx) for i in range(n_gx)])

    def across(x):
        def place(chip, core, j, i):
            return ((2 * chip + core) * n_gy + j) * n_gx + i

        first = [0 if j < n_gy // 2 else 1 for j in range(n_gy)]
        pairs = []
        for chip in range(n_mem // 2):
            for j in range(n_gy - 1):
                for i in range(n_gx):
                    a = place(chip, 1 - first[j], j, i)
                    b = place(chip, first[j + 1], j + 1, i)
                    pairs += [(a, b), (b, a)]
            for i in range(n_gx - n_gx % 2):
                pairs.append((place(chip, first[0], 0, i), place(chip, first[0], 0, i ^ 1)))
                pairs.append((place(chip, 1 - first[-1], n_gy - 1, i), place(chip, 1 - first[-1], n_gy - 1, i ^ 1)))
        return lax.ppermute(x, AXES, pairs)

    def scratch(*shape):
        return pltpu.VMEM(shape, F32)

    others = swap(members)
    end = kept(full, LANES)
    turned = kept(planes, DEPTH, LANES)
    own, forcing, coef, face_east, face_north, pack_coef = call(
        load_kernel,
        [in_hbm(x) for x in (members, increment, zonal_diff, merid_diff, sea_mask)],
        [HBM] * 5,
        [kept(levels, tall, width)] * 2
        + [kept(3, TILE, width), turned, turned, kept(3, tall, LANES)],
        [
            pltpu.VMEM((tall, width), jnp.int32),
            scratch(tall, width),
            scratch(tall, width),
            scratch(full, width),
            scratch(2 * tiles * tall, LANES),
            pltpu.SemaphoreType.DMA((5,)),
        ],
    )
    packed = kept(tall, LANES)
    weights, coef_ends, pack_own, weight_own = held(
        own_ends_kernel, [own, forcing, coef], [kept(TILE, width), kept(TILE, LANES), packed, kept(mid, LANES)]
    )
    deep = levels // 2 * tiles * TILE
    other, strip, more = held(
        pack_rows_kernel,
        [own, others, forcing, weights, coef_ends],
        [kept(levels, TILE, width), kept(deep + tiles * TILE + 2 * TILE, LANES), kept(deep, LANES)],
    )
    forcing, strip, more = lax.optimization_barrier((forcing, strip, more))
    strip, more = across(strip), across(more)
    halfway, pack_other, weight_other = held(
        interior_kernel,
        [own, others, forcing, face_east, face_north],
        [turned, packed, kept(mid, LANES)],
        [scratch(2 * levels * tiles * tall, LANES), scratch(planes, DEPTH, LANES), scratch(planes, DEPTH, LANES)],
    )
    inside = held(
        interior_rest_kernel,
        [halfway, own, others, face_east, face_north],
        kept(levels, mid, width),
        [
            scratch(planes, DEPTH, LANES),
            scratch(planes, DEPTH, LANES),
            scratch(2 * levels * tiles * tall, LANES),
        ],
    )
    inside, pack_other = lax.optimization_barrier((inside, pack_other))
    full_own, full_other, full_coef, west, east = held(
        halo_columns_kernel,
        [strip, pack_own, pack_other, pack_coef],
        [end, end, kept(3, full, LANES), end, end],
    )
    from_west = along(east, 1)
    from_east = along(west, -1)
    inside = held(
        outer_rows_kernel,
        [inside, strip, more, own, other, forcing, coef],
        kept(levels, mid, width),
        [
            scratch(2 * TILE, width),
            scratch(2 * TILE, width),
            scratch(3 * TILE, width),
            scratch(2 * levels * tiles * 2 * TILE, LANES),
            scratch(2 * tiles * 2 * TILE, LANES),
            scratch(10, DEPTH, LANES),
            scratch(10, DEPTH, LANES),
            scratch(10, DEPTH, LANES),
            scratch(10, DEPTH, LANES),
            scratch(2 * levels * tiles * TILE, LANES),
        ],
        aliases={0: 0},
    )
    inside, from_west, from_east = lax.optimization_barrier((inside, from_west, from_east))
    edges = held(
        end_columns_kernel,
        [from_west, from_east, full_own, full_other, full_coef, weight_own, weight_other],
        kept(mid, LANES),
        [scratch(full + 2 * TILE, LANES)] * 7,
    )
    if n_mem > 2:
        groups = [list(range(k, n_mem, 2)) for k in range(2)]
        inside, edges = (lax.psum(x, "mem", axis_index_groups=groups) for x in (inside, edges))
    inside_theirs, edges_theirs = swap(inside), swap(edges)
    return held(
        join_kernel,
        [inside, inside_theirs, edges, edges_theirs],
        [kept(levels, mid, width)] * 2 + [jax.ShapeDtypeStruct(increment.shape, F32)],
        [pltpu.SemaphoreType.DMA((2, 3))],
        out_specs=[VMEM, VMEM, HBM],
        aliases={0: 0, 1: 1},
    )[2]


def solution(mesh):
    return jax.shard_map(
        functools.partial(shards, tuple(mesh.shape[axis] for axis in AXES)),
        mesh=mesh,
        in_specs=(
            P(None, "gy", "gx"),
            P("mem", None, "gy", "gx"),
            P("gy", "gx"),
            P("gy", "gx"),
            P("gy", "gx"),
        ),
        out_specs=P(None, "gy", "gx"),
        check_vma=False,
    )
```

```python
import functools
import jax
import jax.numpy as jnp
from jax import lax
from jax.experimental import pallas as pl
from jax.experimental.pallas import tpu as pltpu
from jax.sharding import PartitionSpec as P

STEPS = 4
FIRST_STEPS = 2
TILE = 8
LANES = 128
AXES = ("mem", "gy", "gx")
F32 = jnp.float32
VMEM = pl.BlockSpec(memory_space=pltpu.VMEM)
HBM = pl.BlockSpec(memory_space=pltpu.HBM)

BODY = slice(TILE, TILE + LANES)
DEPTH = LANES + 2 * TILE
GROUP = 32


def half_of(gy_size):
    core = lax.rem(lax.axis_index("mem"), 2)
    later = (lax.axis_index("gy") >= gy_size // 2).astype(jnp.int32)
    return lax.rem(core + later, 2)


def kept(*shape):
    return pltpu.VMEM(shape, F32)


def pinned(x):
    return pltpu.with_memory_space_constraint(x, pltpu.VMEM)


def in_hbm(x):
    return pltpu.with_memory_space_constraint(x, pltpu.HBM)


def tile(c):
    return slice(c * LANES, (c + 1) * LANES)


def lane_ids(rows):
    return lax.broadcasted_iota(jnp.int32, (rows, LANES), 1)


def row_ids(rows, width):
    return lax.broadcasted_iota(jnp.int32, (rows, width), 0)


def aligned(start):
    return pl.multiple_of(start, TILE)


def run(copies):
    for copy in copies:
        copy.start()
    for copy in copies:
        copy.wait()


def own_ends_kernel(gy_size, own, forcing, coef, out, ends, pack_own, weight_own):
    half = half_of(gy_size)
    width = out.shape[1]
    zm, mm, wet = coef[0], coef[1], coef[2]
    row = row_ids(TILE, width)
    col = lax.broadcasted_iota(jnp.int32, (TILE, width), 1)
    east = zm * jnp.where(col == width - 1, 1.0, pltpu.roll(wet, width - 1, 1))
    north = mm * jnp.where(row == TILE - 1, 1.0, pltpu.roll(wet, TILE - 1, 0))
    upper = jnp.where(row < 4, north, pltpu.roll(east, 4, 0))
    upper = jnp.where(row == 3, pltpu.roll(wet, 3, 0), upper)
    lower = jnp.where(row < 4, pltpu.roll(north, 4, 0), east)
    out[...] = jnp.where(half == 0, upper, lower)
    first = wet[:, :LANES]
    lane, line = lane_ids(TILE), row_ids(TILE, LANES)
    value = out[:, :LANES]
    for r in range(4):
        moved = jnp.where(half == 0, pltpu.roll(first, 7 - r, 0), pltpu.roll(first, (-r) % TILE, 0))
        value = jnp.where((line == jnp.where(half == 0, 7, 4)) & (lane == r), pltpu.roll(moved, r, 1), value)
    out[:, :LANES] = value
    both = (tile(0), slice(width - LANES, width))
    ends[...] = edge_coefficient(*(out[:, cols] for cols in both))
    levels, tall, _ = own.shape
    pack_own[...] = edge_columns(*([own[l, :, cols] * forcing[l, :, cols] for l in range(levels)] for cols in both))
    keep = pl.ds(aligned(half * TILE), tall - TILE)
    weight_own[...] = edge_columns(*([own[l, keep, cols] for l in range(levels)] for cols in both))


def outer_rows_of(gy_size, level, own, other, forcing, cols):
    half = half_of(gy_size)
    j = lax.axis_index("gy")
    same_core = jnp.where(half == 0, j == gy_size // 2, j == gy_size // 2 - 1)
    outer = pl.ds(aligned(half * (own.shape[1] - TILE)), TILE)
    force = forcing[level, outer, cols]
    mine = own[level, outer, cols] * force
    theirs = other[level, :, cols] * force
    first, second = jnp.where(same_core, mine, theirs), jnp.where(same_core, theirs, mine)
    first = jnp.where(half == 0, first, pltpu.roll(first, TILE // 2, 0))
    second = jnp.where(half == 0, pltpu.roll(second, TILE // 2, 0), second)
    return jnp.where(row_ids(*first.shape) < TILE // 2, first, second)


def pack_rows_kernel(gy_size, own, others, forcing, weights, coef_ends, other, strip, more):
    levels, _, width = own.shape
    tiles = width // LANES
    other[...] = others[0, :, pl.ds(aligned(half_of(gy_size) * (others.shape[2] - TILE)), TILE), :]
    ends = ([], [])
    for c in range(tiles):
        for level in range(levels):
            rows = outer_rows_of(gy_size, level, own, other, forcing, tile(c))
            part, place = strip_place(level, levels, (strip, more))
            part[strip_rows(place, c, tiles), :] = rows
            if c in (0, tiles - 1):
                ends[c > 0].append(rows)
        strip[strip_rows(levels // 2, c, tiles), :] = weights[:, tile(c)]
    last = (levels // 2 + 1) * tiles * TILE
    strip[last : last + TILE, :] = edge_columns(*ends)
    strip[last + TILE :, :] = coef_ends[...]


def strip_place(level, levels, parts):
    return parts[level // (levels // 2)], level % (levels // 2)


def strip_rows(place, c, tiles):
    return slice((place * tiles + c) * TILE, (place * tiles + c + 1) * TILE)


def inside_domain(gy_size):
    half, j = half_of(gy_size), lax.axis_index("gy")
    return jnp.where(half == 0, j > 0, j < gy_size - 1)


def beyond(value, real):
    return jnp.where(real, value, 0.0)


def unfold(gy_size, value, place):
    natural = jnp.equal(half_of(gy_size), 1 - place % 2)
    return beyond(jnp.where(natural, value, pltpu.roll(value, TILE // 2, 0)), inside_domain(gy_size))


def unfold_weights(gy_size, value, packed):
    half, real = half_of(gy_size), inside_domain(gy_size)
    moved = pltpu.roll(value, TILE // 2, 0)
    zm = jnp.where(half == 0, value, moved)
    mm = jnp.where(half == 0, moved, value)
    line = row_ids(*value.shape)
    wet = jnp.where((half == 1) & (line == 0), pltpu.roll(value, 5, 0), 1.0)
    if packed:
        place = lane_ids(TILE) % GROUP
        for r in range(4):
            shifted = jnp.where(half == 0, pltpu.roll(value, r, 0), pltpu.roll(value, (r + 1) % TILE, 0))
            at = (line == jnp.where(half == 0, 4 + r, r)) & (place == 8)
            wet = jnp.where(at, pltpu.roll(shifted, (-r) % LANES, 1), wet)
    return [beyond(x, real) for x in (zm, mm, wet)]


def edge_columns(first, last):
    rows = first[0].shape[0]
    lane = lane_ids(rows)
    total = jnp.zeros((rows, LANES), F32)
    for level, (a, b) in enumerate(zip(first, last)):
        base = GROUP * level
        total = jnp.where((lane >= base + 8) & (lane < base + 16), pltpu.roll(a, base + 8, 1), total)
        total = jnp.where((lane >= base + 16) & (lane < base + 24), pltpu.roll(b, (base + 16 - 120) % LANES, 1), total)
    return total


def spread(value):
    value = value + pltpu.roll(value, GROUP, 1)
    return value + pltpu.roll(value, 2 * GROUP, 1)


def edge_coefficient(first, last):
    rows = first.shape[0]
    lane = lane_ids(rows)
    total = jnp.where((lane >= 8) & (lane < 16), pltpu.roll(first, 8, 1), 0.0)
    return spread(jnp.where((lane >= 16) & (lane < 24), pltpu.roll(last, 24, 1), total))


def outgoing(values, west):
    place = lane_ids(values[0].shape[0]) % GROUP
    start, step, source = (24, -4, 8) if west else (4, 4, 20)
    total = jnp.zeros(values[0].shape, F32)
    for k, value in enumerate(values):
        at = start + step * k
        total = jnp.where((place >= at) & (place < at + 4), pltpu.roll(value, (at - source) % LANES, 1), total)
    return total


def turn(ref, start, stride):
    return jnp.concatenate([ref[pl.ds(s, TILE, stride=stride), :] for s in start], axis=0).T


def refresh(ref, first, count):
    flat = ref.reshape(ref.shape[0] * DEPTH, LANES)

    def rows(j):
        return pl.ds(first * DEPTH + TILE + j, count, stride=DEPTH)

    flat[rows(-1), :] = pltpu.roll(flat[rows(LANES - 1), :], 1, 1)
    flat[rows(LANES), :] = pltpu.roll(flat[rows(0), :], LANES - 1, 1)


def sweep(source, target, east, north, first, last):
    for start in range(TILE, TILE + LANES, TILE):
        at, ahead, behind = (slice(start + d, start + d + TILE) for d in (0, 1, -1))
        here = source[first, at, :]
        south = north[first - 1, at, :] * (here - source[first - 1, at, :])
        for p in range(first, last + 1):
            above = source[p + 1, at, :]
            flux = north[p, at, :] * (above - here)
            go_east = east[p, at, :] * (source[p, ahead, :] - here)
            go_west = east[p, behind, :] * (here - source[p, behind, :])
            target[p, at, :] = here + go_east - go_west + flux - south
            here, south = above, flux


def faces(zm, mm, wet, cols, width, rows):
    after = slice(cols.start + LANES, cols.stop + LANES) if cols.stop < width else cols
    lane = lane_ids(rows)
    here = pltpu.roll(wet[:rows, cols], LANES - 1, 1)
    beyond = pltpu.roll(wet[:rows, after], LANES - 1, 1)
    east = zm[:, cols] * jnp.where(lane == LANES - 1, beyond, here)
    north = mm[:, cols] * wet[1 : rows + 1, cols]
    return east, north


def load_kernel(
    gy_size, members, increment, zonal, merid, mask,
    own, forcing, coef, east, north, pack_coef,
    mask_buf, zm, mm, wet, face, sems,
):
    _, tall, width = own.shape
    tiles = width // LANES
    planes = east.shape[0]
    offset = planes - 2 * STEPS
    half = half_of(gy_size)
    base = half * STEPS
    part = pl.ds(aligned(half * (tall - 2 * TILE)), tall)
    small = [
        pltpu.make_async_copy(mask.at[part, :], mask_buf, sems.at[0]),
        pltpu.make_async_copy(zonal.at[part, :], zm, sems.at[1]),
        pltpu.make_async_copy(merid.at[part, :], mm, sems.at[2]),
    ]
    large = [
        pltpu.make_async_copy(increment.at[:, part, :], forcing, sems.at[3]),
        pltpu.make_async_copy(members.at[0, :, part, :], own, sems.at[4]),
    ]
    for copy in small + large:
        copy.start()
    for copy in small:
        copy.wait()
    wet[:tall, :] = mask_buf[...].astype(F32)
    wet[tall:, :] = jnp.zeros((TILE, width), F32)
    zm[...] = zm[...] * wet[:tall, :]
    mm[...] = mm[...] * wet[:tall, :]
    outer = pl.ds(aligned(half * (tall - TILE)), TILE)
    for k, ref in enumerate((zm, mm, wet)):
        coef[k] = ref[outer, :]
    for c in range(tiles):
        face[pl.ds(c * tall, tall), :], face[pl.ds((tiles + c) * tall, tall), :] = faces(zm, mm, wet, tile(c), width, tall)
    for q in range(planes):
        for k, ref in enumerate((east, north)):
            ref[q, BODY, :] = turn(face, [k * tiles * tall + ch * offset + q + base for _ in range(TILE) for ch in range(2)], tall)
    refresh(east, 0, planes)
    ends = (tile(0), tile(tiles - 1))
    for k, ref in enumerate((zm, mm, wet)):
        pack_coef[k] = edge_coefficient(*(ref[:tall, cols] for cols in ends))
    large[0].wait()
    forcing[...] = forcing[...] * wet[:tall, :][None]
    large[1].wait()


def interior_kernel(
    gy_size, own, others, forcing, east, north,
    halfway, pack_other, weight_other,
    field, u, u_next,
):
    levels, tall, width = own.shape
    tiles = width // LANES
    mid = tall - TILE
    planes = east.shape[0]
    offset = planes - 2 * STEPS
    half = half_of(gy_size)
    base = half * STEPS
    part = pl.ds(aligned(half * (mid - TILE)), tall)
    keep_other = pl.ds(aligned(half * mid), mid)
    for c in range(tiles):
        cols = tile(c)
        for level in range(levels):
            force = forcing[level, :, cols]
            for k, member in enumerate((own[level, :, cols], others[0, level, part, cols])):
                field[pl.ds(((2 * level + k) * tiles + c) * tall, tall), :] = member * force

    def at(f, c):
        return field[pl.ds((f * tiles + c) * tall, tall), :]

    ends = (tile(0), tile(tiles - 1))
    pack_other[...] = edge_columns(*([at(2 * level + 1, c) for level in range(levels)] for c in (0, tiles - 1)))
    weight_other[...] = edge_columns(*([others[0, level, keep_other, cols] for level in range(levels)] for cols in ends))
    fields = range(2 * levels)
    for q in range(planes):
        u[q, BODY, :] = turn(field, [f * tiles * tall + ch * offset + q + base for f in fields for ch in range(2)], tall)
    buffers = [u, u_next, u][:FIRST_STEPS] + [halfway]
    for step in range(FIRST_STEPS):
        count = planes - 2 - 2 * step
        refresh(buffers[step], step + 1, count)
        sweep(buffers[step], buffers[step + 1], east, north, step + 1, step + count)
    refresh(halfway, FIRST_STEPS + 1, planes - 2 - 2 * FIRST_STEPS)


def interior_rest_kernel(gy_size, halfway, own, others, east, north, out, u, u_next, result):
    levels, tall, width = own.shape
    tiles = width // LANES
    mid = tall - TILE
    planes = east.shape[0]
    offset = planes - 2 * STEPS
    half = half_of(gy_size)
    base = half * STEPS
    keep_own, keep_other = pl.ds(aligned(half * TILE), mid), pl.ds(aligned(half * mid), mid)
    fields = range(2 * levels)
    source = halfway
    for step in range(FIRST_STEPS, STEPS):
        count = planes - 2 - 2 * step
        if step > FIRST_STEPS:
            refresh(source, step + 1, count)
        target = u if step % 2 == 0 else u_next
        sweep(source, target, east, north, step + 1, step + count)
        source = target
    for q in range(STEPS, planes - STEPS):
        flat = source[q, BODY, :].T
        for f in fields:
            for ch in range(2):
                group = (2 * f + ch) * tiles
                result[pl.ds(f * tiles * tall + ch * offset + q + base, tiles, stride=tall), :] = flat[group : group + tiles]
    for level in range(levels):
        for c in range(tiles):
            a, b = (
                result[pl.ds(aligned(((2 * level + k) * tiles + c) * tall + half * TILE), mid), :] for k in range(2)
            )
            out[level, :, tile(c)] = own[level, keep_own, tile(c)] * a + others[0, level, keep_other, tile(c)] * b


def halo_columns_kernel(
    gy_size, strip, pack_own, pack_other, pack_coef, full_own, full_other, full_coef, west_out, east_out
):
    half = half_of(gy_size)
    tall = pack_own.shape[0]
    halo = pl.ds(aligned(half * tall), TILE)
    main = pl.ds(aligned((1 - half) * TILE), tall)
    local = [pack_own[...], pack_other[...]] + [pack_coef[k] for k in range(3)]
    corner = strip.shape[0] - 2 * TILE
    fields = [unfold(gy_size, strip[corner : corner + TILE, :], k) for k in range(2)]
    received = fields + unfold_weights(gy_size, strip[corner + TILE :, :], True)
    full = [full_own, full_other] + [full_coef.at[k] for k in range(3)]
    for rows, values in ((main, local), (halo, received)):
        west_out[rows, :] = outgoing(values, True)
        east_out[rows, :] = outgoing(values, False)
    for ref, inner, outer in zip(full, local, received):
        ref[main, :] = inner
        ref[halo, :] = outer


def outer_rows_kernel(
    gy_size, inside, strip, more, own, other, forcing, coef, sums,
    zm, mm, wet, field, face, u, u_next, east, north, result,
):
    levels, tall, width = own.shape
    tiles = width // LANES
    half = half_of(gy_size)
    outer = pl.ds(aligned(half * (tall - TILE)), TILE)
    edge = pl.ds(aligned((1 - half) * TILE), TILE)
    halo = pl.ds(aligned(half * TILE), TILE)
    block = 2 * TILE
    for k, ref in enumerate((zm, mm, wet)):
        ref[edge, :] = coef[k]
    for c in range(tiles):
        values = unfold_weights(gy_size, strip[strip_rows(levels // 2, c, tiles), :], False)
        for ref, value in zip((zm, mm, wet), values):
            ref[halo, tile(c)] = value
    wet[block:, :] = jnp.zeros((TILE, width), F32)
    for c in range(tiles):
        cols = tile(c)
        face[pl.ds(c * block, block), :], face[pl.ds((tiles + c) * block, block), :] = faces(zm, mm, wet, cols, width, block)
        for level in range(levels):
            part, where = strip_place(level, levels, (strip, more))
            for k, member in enumerate((own[level, outer, cols], other[level, :, cols])):
                base = ((2 * level + k) * tiles + c) * block
                field[pl.ds(aligned(base + (1 - half) * TILE), TILE), :] = member * forcing[level, outer, cols]
                field[pl.ds(aligned(base + half * TILE), TILE), :] = unfold(gy_size, part[strip_rows(where, c, tiles), :], k)

    fields = range(2 * levels)
    planes = 10
    lead = (1 - half) * 4
    for q in range(planes):
        u[q, BODY, :] = turn(field, [f * tiles * block + 2 * ch + q + lead for f in fields for ch in range(2)], block)
        for k, ref in enumerate((east, north)):
            if q == planes - 1 or (k == 0 and q == 0):
                continue
            ref[q, BODY, :] = turn(face, [k * tiles * block + 2 * ch + q + lead for f in fields for ch in range(2)], block)
    refresh(east, 0, planes)
    source, target = u, u_next
    for step in range(STEPS):
        count = planes - 2 - 2 * step
        refresh(source, step + 1, count)
        sweep(source, target, east, north, step + 1, step + count)
        source, target = target, source
    for p in range(2):
        flat = source[STEPS + p, BODY, :].T
        for f in fields:
            for ch in range(2):
                group = (2 * f + ch) * tiles
                result[pl.ds(f * tiles * TILE + 4 * half + 2 * ch + p, tiles, stride=TILE), :] = flat[group : group + tiles]
    mine = row_ids(TILE, LANES) // 4 == half
    place = pl.ds(aligned(half * (tall - 2 * TILE)), TILE)
    for c in range(tiles):
        cols = tile(c)
        for level in range(levels):
            a, b = (result[pl.ds(((2 * level + k) * tiles + c) * TILE, TILE), :] for k in range(2))
            term = own[level, outer, cols] * a + other[level, :, cols] * b
            sums[level, place, cols] = jnp.where(mine, term, sums[level, place, cols])


def end_columns_kernel(
    gy_size, from_west, from_east, own, other, coef, weight_own, weight_other, out,
    a, b, a_next, b_next, east, north, wet,
):
    full = own.shape[0]
    body = pl.ds(TILE, full)
    place = lane_ids(full) % GROUP
    on_west = (place >= 4) & (place < 8)
    on_east = (place >= 24) & (place < 28)
    west, east_strip = from_west[...], from_east[...]

    def with_ends(value, k):
        value = jnp.where(on_west, pltpu.roll(west, (-4 * k) % LANES, 1), value)
        return jnp.where(on_east, pltpu.roll(east_strip, 4 * k, 1), value)

    blank = jnp.zeros((TILE, LANES), F32)
    for ref in (a, b, a_next, b_next, east, north, wet):
        ref[:TILE, :] = blank
        ref[full + TILE :, :] = blank
    a[body, :] = with_ends(own[...], 0)
    b[body, :] = with_ends(other[...], 1)
    wet[body, :] = with_ends(coef[2], 4)
    east[body, :] = with_ends(coef[0], 2) * pltpu.roll(wet[body, :], LANES - 1, 1)
    north[body, :] = with_ends(coef[1], 3) * wet[pl.ds(TILE + 1, full), :]
    now, later = (a, b), (a_next, b_next)
    for step in range(STEPS):
        for t in range(TILE, full + TILE, TILE):
            at, above, below = (pl.ds(t + d, TILE) for d in (0, 1, -1))
            e, n, s = east[at, :], north[at, :], north[below, :]
            for source, target in zip(now, later):
                here = source[at, :]
                flux = e * (pltpu.roll(here, LANES - 1, 1) - here)
                go_north = n * (source[above, :] - here)
                go_south = s * (here - source[below, :])
                target[at, :] = here + flux - pltpu.roll(flux, 1, 1) + go_north - go_south
        now, later = later, now
    mid = weight_own.shape[0]
    rows = pl.ds(2 * TILE, mid)
    out[...] = weight_own[...] * now[0][rows, :] + weight_other[...] * now[1][rows, :]


def join_kernel(gy_size, mine_in, theirs_in, mine_edge, theirs_edge, mine, theirs, out, sems):
    half = half_of(gy_size)
    levels, mid, width = mine.shape
    lane = lane_ids(mid)
    first, last, between = slice(0, LANES), slice(width - LANES, width), slice(LANES, width - LANES)
    halves = ((mine, mine_edge, half), (theirs, theirs_edge, 1 - half))
    copies = []

    def send(k, cols, place):
        ref, _, where = halves[k]
        rows = pl.ds(aligned(where * mid), mid)
        copies.append(pltpu.make_async_copy(ref.at[:, :, cols], out.at[:, rows, cols], sems.at[k, place]))
        copies[-1].start()

    for k in range(2):
        send(k, between, 0)
    for k, (ref, edges, _) in enumerate(halves):
        packed = edges[...]
        for level in range(levels):
            base = GROUP * level
            ref[level, :, first] = jnp.where(lane < 4, pltpu.roll(packed, (-base - 8) % LANES, 1), ref[level, :, first])
        send(k, first, 1)
        for level in range(levels):
            base = GROUP * level
            ref[level, :, last] = jnp.where(
                lane >= LANES - 4, pltpu.roll(packed, (LANES - 4 - base - 20) % LANES, 1), ref[level, :, last]
            )
        send(k, last, 2)
    for copy in copies:
        copy.wait()


def shards(sizes, increment, members, zonal_diff, merid_diff, sea_mask):
    n_mem, n_gy, n_gx = sizes
    levels, rows, width = increment.shape
    tiles = width // LANES
    mid = rows // 2
    tall = mid + TILE
    full = tall + TILE
    planes = (mid - STEPS) // 2 + 2 * STEPS
    assert tiles == TILE and 4 * levels * tiles == LANES and tall == 5 * TILE and n_mem % 2 == 0

    def call(kernel, ins, specs, outs, scratch=(), out_specs=None, aliases={}):
        return pl.pallas_call(
            functools.partial(kernel, n_gy),
            out_shape=outs,
            in_specs=specs,
            out_specs=out_specs if out_specs is not None else jax.tree.map(lambda _: VMEM, outs),
            scratch_shapes=scratch,
            input_output_aliases=aliases,
            compiler_params=pltpu.CompilerParams(vmem_limit_bytes=40 * 1024 * 1024),
        )(*ins)

    def held(kernel, ins, outs, scratch=(), **kw):
        got = call(kernel, [pinned(x) for x in ins], [VMEM] * len(ins), outs, scratch, **kw)
        return got

    def swap(x):
        return lax.ppermute(x, "mem", [(i, i ^ 1) for i in range(n_mem)])

    def along(x, shift):
        return lax.ppermute(x, "gx", [(i, (i + shift) % n_gx) for i in range(n_gx)])

    def across(x):
        def place(chip, core, j, i):
            return ((2 * chip + core) * n_gy + j) * n_gx + i

        first = [0 if j < n_gy // 2 else 1 for j in range(n_gy)]
        pairs = []
        for chip in range(n_mem // 2):
            for j in range(n_gy - 1):
                for i in range(n_gx):
                    a = place(chip, 1 - first[j], j, i)
                    b = place(chip, first[j + 1], j + 1, i)
                    pairs += [(a, b), (b, a)]
            for i in range(n_gx - n_gx % 2):
                pairs.append((place(chip, first[0], 0, i), place(chip, first[0], 0, i ^ 1)))
                pairs.append((place(chip, 1 - first[-1], n_gy - 1, i), place(chip, 1 - first[-1], n_gy - 1, i ^ 1)))
        return lax.ppermute(x, AXES, pairs)

    def scratch(*shape):
        return pltpu.VMEM(shape, F32)

    others = swap(members)
    end = kept(full, LANES)
    turned = kept(planes, DEPTH, LANES)
    own, forcing, coef, face_east, face_north, pack_coef = call(
        load_kernel,
        [in_hbm(x) for x in (members, increment, zonal_diff, merid_diff, sea_mask)],
        [HBM] * 5,
        [kept(levels, tall, width)] * 2
        + [kept(3, TILE, width), turned, turned, kept(3, tall, LANES)],
        [
            pltpu.VMEM((tall, width), jnp.int32),
            scratch(tall, width),
            scratch(tall, width),
            scratch(full, width),
            scratch(2 * tiles * tall, LANES),
            pltpu.SemaphoreType.DMA((5,)),
        ],
    )
    packed = kept(tall, LANES)
    weights, coef_ends, pack_own, weight_own = held(
        own_ends_kernel, [own, forcing, coef], [kept(TILE, width), kept(TILE, LANES), packed, kept(mid, LANES)]
    )
    deep = levels // 2 * tiles * TILE
    other, strip, more = held(
        pack_rows_kernel,
        [own, others, forcing, weights, coef_ends],
        [kept(levels, TILE, width), kept(deep + tiles * TILE + 2 * TILE, LANES), kept(deep, LANES)],
    )
    forcing, strip, more = lax.optimization_barrier((forcing, strip, more))
    strip, more = across(strip), across(more)
    halfway, pack_other, weight_other = held(
        interior_kernel,
        [own, others, forcing, face_east, face_north],
        [turned, packed, kept(mid, LANES)],
        [scratch(2 * levels * tiles * tall, LANES), scratch(planes, DEPTH, LANES), scratch(planes, DEPTH, LANES)],
    )
    inside = held(
        interior_rest_kernel,
        [halfway, own, others, face_east, face_north],
        kept(levels, mid, width),
        [
            scratch(planes, DEPTH, LANES),
            scratch(planes, DEPTH, LANES),
            scratch(2 * levels * tiles * tall, LANES),
        ],
    )
    inside, pack_other = lax.optimization_barrier((inside, pack_other))
    full_own, full_other, full_coef, west, east = held(
        halo_columns_kernel,
        [strip, pack_own, pack_other, pack_coef],
        [end, end, kept(3, full, LANES), end, end],
    )
    from_west = along(east, 1)
    from_east = along(west, -1)
    inside = held(
        outer_rows_kernel,
        [inside, strip, more, own, other, forcing, coef],
        kept(levels, mid, width),
        [
            scratch(2 * TILE, width),
            scratch(2 * TILE, width),
            scratch(3 * TILE, width),
            scratch(2 * levels * tiles * 2 * TILE, LANES),
            scratch(2 * tiles * 2 * TILE, LANES),
            scratch(10, DEPTH, LANES),
            scratch(10, DEPTH, LANES),
            scratch(10, DEPTH, LANES),
            scratch(10, DEPTH, LANES),
            scratch(2 * levels * tiles * TILE, LANES),
        ],
        aliases={0: 0},
    )
    inside, from_west, from_east = lax.optimization_barrier((inside, from_west, from_east))
    edges = held(
        end_columns_kernel,
        [from_west, from_east, full_own, full_other, full_coef, weight_own, weight_other],
        kept(mid, LANES),
        [scratch(full + 2 * TILE, LANES)] * 7,
    )
    if n_mem > 2:
        groups = [list(range(k, n_mem, 2)) for k in range(2)]
        inside, edges = (lax.psum(x, "mem", axis_index_groups=groups) for x in (inside, edges))
    inside_theirs, edges_theirs = swap(inside), swap(edges)
    return held(
        join_kernel,
        [inside, inside_theirs, edges, edges_theirs],
        [kept(levels, mid, width)] * 2 + [jax.ShapeDtypeStruct(increment.shape, F32)],
        [pltpu.SemaphoreType.DMA((2, 3))],
        out_specs=[VMEM, VMEM, HBM],
        aliases={0: 0, 1: 1},
    )[2]


def solution(mesh):
    return jax.shard_map(
        functools.partial(shards, tuple(mesh.shape[axis] for axis in AXES)),
        mesh=mesh,
        in_specs=(
            P(None, "gy", "gx"),
            P("mem", None, "gy", "gx"),
            P("gy", "gx"),
            P("gy", "gx"),
            P("gy", "gx"),
        ),
        out_specs=P(None, "gy", "gx"),
        check_vma=False,
    )
```

```python
import functools
import jax
import jax.numpy as jnp
from jax import lax
from jax.experimental import pallas as pl
from jax.experimental.pallas import tpu as pltpu
from jax.sharding import PartitionSpec as P

STEPS = 4
FIRST_STEPS = 4
TILE = 8
LANES = 128
AXES = ("mem", "gy", "gx")
F32 = jnp.float32
VMEM = pl.BlockSpec(memory_space=pltpu.VMEM)
HBM = pl.BlockSpec(memory_space=pltpu.HBM)

BODY = slice(TILE, TILE + LANES)
DEPTH = LANES + 3 * TILE
GROUP = 32


def half_of(gy_size):
    core = lax.rem(lax.axis_index("mem"), 2)
    later = (lax.axis_index("gy") >= gy_size // 2).astype(jnp.int32)
    return lax.rem(core + later, 2)


def kept(*shape):
    return pltpu.VMEM(shape, F32)


def pinned(x):
    return pltpu.with_memory_space_constraint(x, pltpu.VMEM)


def in_hbm(x):
    return pltpu.with_memory_space_constraint(x, pltpu.HBM)


def tile(c):
    return slice(c * LANES, (c + 1) * LANES)


def lane_ids(rows):
    return lax.broadcasted_iota(jnp.int32, (rows, LANES), 1)


def row_ids(rows, width):
    return lax.broadcasted_iota(jnp.int32, (rows, width), 0)


def aligned(start):
    return pl.multiple_of(start, TILE)


def run(copies):
    for copy in copies:
        copy.start()
    for copy in copies:
        copy.wait()


def own_ends_kernel(gy_size, own, forcing, coef, out, ends, pack_own, weight_own):
    half = half_of(gy_size)
    width = out.shape[1]
    zm, mm, wet = coef[0], coef[1], coef[2]
    row = row_ids(TILE, width)
    col = lax.broadcasted_iota(jnp.int32, (TILE, width), 1)
    east = zm * jnp.where(col == width - 1, 1.0, pltpu.roll(wet, width - 1, 1))
    north = mm * jnp.where(row == TILE - 1, 1.0, pltpu.roll(wet, TILE - 1, 0))
    upper = jnp.where(row < 4, north, pltpu.roll(east, 4, 0))
    upper = jnp.where(row == 3, pltpu.roll(wet, 3, 0), upper)
    lower = jnp.where(row < 4, pltpu.roll(north, 4, 0), east)
    out[...] = jnp.where(half == 0, upper, lower)
    first = wet[:, :LANES]
    lane, line = lane_ids(TILE), row_ids(TILE, LANES)
    value = out[:, :LANES]
    for r in range(4):
        moved = jnp.where(half == 0, pltpu.roll(first, 7 - r, 0), pltpu.roll(first, (-r) % TILE, 0))
        value = jnp.where((line == jnp.where(half == 0, 7, 4)) & (lane == r), pltpu.roll(moved, r, 1), value)
    out[:, :LANES] = value
    both = (tile(0), slice(width - LANES, width))
    ends[...] = edge_coefficient(*(out[:, cols] for cols in both))
    levels, tall, _ = own.shape
    pack_own[...] = edge_columns(*([own[l, :, cols] * forcing[l, :, cols] for l in range(levels)] for cols in both))
    keep = pl.ds(aligned(half * TILE), tall - TILE)
    weight_own[...] = edge_columns(*([own[l, keep, cols] for l in range(levels)] for cols in both))


def outer_rows_of(gy_size, level, own, other, forcing, cols):
    half = half_of(gy_size)
    j = lax.axis_index("gy")
    same_core = jnp.where(half == 0, j == gy_size // 2, j == gy_size // 2 - 1)
    outer = pl.ds(aligned(half * (own.shape[1] - TILE)), TILE)
    force = forcing[level, outer, cols]
    mine = own[level, outer, cols] * force
    theirs = other[level, :, cols] * force
    first, second = jnp.where(same_core, mine, theirs), jnp.where(same_core, theirs, mine)
    first = jnp.where(half == 0, first, pltpu.roll(first, TILE // 2, 0))
    second = jnp.where(half == 0, pltpu.roll(second, TILE // 2, 0), second)
    return jnp.where(row_ids(*first.shape) < TILE // 2, first, second)


def pack_rows_kernel(gy_size, own, others, forcing, weights, coef_ends, other, strip, more):
    levels, _, width = own.shape
    tiles = width // LANES
    other[...] = others[0, :, pl.ds(aligned(half_of(gy_size) * (others.shape[2] - TILE)), TILE), :]
    ends = ([], [])
    for c in range(tiles):
        for level in range(levels):
            rows = outer_rows_of(gy_size, level, own, other, forcing, tile(c))
            part, place = strip_place(level, levels, (strip, more))
            part[strip_rows(place, c, tiles), :] = rows
            if c in (0, tiles - 1):
                ends[c > 0].append(rows)
        strip[strip_rows(levels // 2, c, tiles), :] = weights[:, tile(c)]
    last = (levels // 2 + 1) * tiles * TILE
    strip[last : last + TILE, :] = edge_columns(*ends)
    strip[last + TILE :, :] = coef_ends[...]


def strip_place(level, levels, parts):
    return parts[level // (levels // 2)], level % (levels // 2)


def strip_rows(place, c, tiles):
    return slice((place * tiles + c) * TILE, (place * tiles + c + 1) * TILE)


def inside_domain(gy_size):
    half, j = half_of(gy_size), lax.axis_index("gy")
    return jnp.where(half == 0, j > 0, j < gy_size - 1)


def beyond(value, real):
    return jnp.where(real, value, 0.0)


def unfold(gy_size, value, place):
    natural = jnp.equal(half_of(gy_size), 1 - place % 2)
    return beyond(jnp.where(natural, value, pltpu.roll(value, TILE // 2, 0)), inside_domain(gy_size))


def unfold_weights(gy_size, value, packed):
    half, real = half_of(gy_size), inside_domain(gy_size)
    moved = pltpu.roll(value, TILE // 2, 0)
    zm = jnp.where(half == 0, value, moved)
    mm = jnp.where(half == 0, moved, value)
    line = row_ids(*value.shape)
    wet = jnp.where((half == 1) & (line == 0), pltpu.roll(value, 5, 0), 1.0)
    if packed:
        place = lane_ids(TILE) % GROUP
        for r in range(4):
            shifted = jnp.where(half == 0, pltpu.roll(value, r, 0), pltpu.roll(value, (r + 1) % TILE, 0))
            at = (line == jnp.where(half == 0, 4 + r, r)) & (place == 8)
            wet = jnp.where(at, pltpu.roll(shifted, (-r) % LANES, 1), wet)
    return [beyond(x, real) for x in (zm, mm, wet)]


def edge_columns(first, last):
    rows = first[0].shape[0]
    lane = lane_ids(rows)
    total = jnp.zeros((rows, LANES), F32)
    for level, (a, b) in enumerate(zip(first, last)):
        base = GROUP * level
        total = jnp.where((lane >= base + 8) & (lane < base + 16), pltpu.roll(a, base + 8, 1), total)
        total = jnp.where((lane >= base + 16) & (lane < base + 24), pltpu.roll(b, (base + 16 - 120) % LANES, 1), total)
    return total


def spread(value):
    value = value + pltpu.roll(value, GROUP, 1)
    return value + pltpu.roll(value, 2 * GROUP, 1)


def edge_coefficient(first, last):
    rows = first.shape[0]
    lane = lane_ids(rows)
    total = jnp.where((lane >= 8) & (lane < 16), pltpu.roll(first, 8, 1), 0.0)
    return spread(jnp.where((lane >= 16) & (lane < 24), pltpu.roll(last, 24, 1), total))


def outgoing(values, west):
    place = lane_ids(values[0].shape[0]) % GROUP
    start, step, source = (24, -4, 8) if west else (4, 4, 20)
    total = jnp.zeros(values[0].shape, F32)
    for k, value in enumerate(values):
        at = start + step * k
        total = jnp.where((place >= at) & (place < at + 4), pltpu.roll(value, (at - source) % LANES, 1), total)
    return total


def turn(ref, start, stride):
    return jnp.concatenate([ref[pl.ds(s, TILE, stride=stride), :] for s in start], axis=0).T


def refresh(ref, first, count):
    flat = ref.reshape(ref.shape[0] * DEPTH, LANES)

    def rows(j):
        return pl.ds(first * DEPTH + TILE + j, count, stride=DEPTH)

    flat[rows(-1), :] = pltpu.roll(flat[rows(LANES - 1), :], 1, 1)
    flat[rows(LANES), :] = pltpu.roll(flat[rows(0), :], LANES - 1, 1)


def sweep(source, target, east, north, first, last):
    for start in range(TILE, TILE + LANES, TILE):
        at, ahead, behind = (slice(start + d, start + d + TILE) for d in (0, 1, -1))
        here = source[first, at, :]
        south = north[first - 1, at, :] * (here - source[first - 1, at, :])
        for p in range(first, last + 1):
            above = source[p + 1, at, :]
            flux = north[p, at, :] * (above - here)
            go_east = east[p, at, :] * (source[p, ahead, :] - here)
            go_west = east[p, behind, :] * (here - source[p, behind, :])
            target[p, at, :] = here + go_east - go_west + flux - south
            here, south = above, flux


def faces(zm, mm, wet, cols, width, rows):
    after = slice(cols.start + LANES, cols.stop + LANES) if cols.stop < width else cols
    lane = lane_ids(rows)
    here = pltpu.roll(wet[:rows, cols], LANES - 1, 1)
    beyond = pltpu.roll(wet[:rows, after], LANES - 1, 1)
    east = zm[:, cols] * jnp.where(lane == LANES - 1, beyond, here)
    north = mm[:, cols] * wet[1 : rows + 1, cols]
    return east, north


def load_kernel(
    gy_size, members, increment, zonal, merid, mask,
    own, forcing, coef, east, north, pack_coef,
    mask_buf, zm, mm, wet, face, sems,
):
    _, tall, width = own.shape
    tiles = width // LANES
    planes = east.shape[0]
    offset = planes - 2 * STEPS
    half = half_of(gy_size)
    base = half * STEPS
    part = pl.ds(aligned(half * (tall - 2 * TILE)), tall)
    small = [
        pltpu.make_async_copy(mask.at[part, :], mask_buf, sems.at[0]),
        pltpu.make_async_copy(zonal.at[part, :], zm, sems.at[1]),
        pltpu.make_async_copy(merid.at[part, :], mm, sems.at[2]),
    ]
    large = [
        pltpu.make_async_copy(increment.at[:, part, :], forcing, sems.at[3]),
        pltpu.make_async_copy(members.at[0, :, part, :], own, sems.at[4]),
    ]
    for copy in small + large:
        copy.start()
    for copy in small:
        copy.wait()
    wet[:tall, :] = mask_buf[...].astype(F32)
    wet[tall:, :] = jnp.zeros((TILE, width), F32)
    zm[...] = zm[...] * wet[:tall, :]
    mm[...] = mm[...] * wet[:tall, :]
    outer = pl.ds(aligned(half * (tall - TILE)), TILE)
    for k, ref in enumerate((zm, mm, wet)):
        coef[k] = ref[outer, :]
    for c in range(tiles):
        face[pl.ds(c * tall, tall), :], face[pl.ds((tiles + c) * tall, tall), :] = faces(zm, mm, wet, tile(c), width, tall)
    for q in range(planes):
        for k, ref in enumerate((east, north)):
            ref[q, BODY, :] = turn(face, [k * tiles * tall + ch * offset + q + base for _ in range(TILE) for ch in range(2)], tall)
    refresh(east, 0, planes)
    ends = (tile(0), tile(tiles - 1))
    for k, ref in enumerate((zm, mm, wet)):
        pack_coef[k] = edge_coefficient(*(ref[:tall, cols] for cols in ends))
    large[0].wait()
    forcing[...] = forcing[...] * wet[:tall, :][None]
    large[1].wait()


def interior_kernel(
    gy_size, own, others, forcing, east, north,
    halfway, pack_other, weight_other,
    field, u, u_next,
):
    levels, tall, width = own.shape
    tiles = width // LANES
    mid = tall - TILE
    planes = east.shape[0]
    offset = planes - 2 * STEPS
    half = half_of(gy_size)
    base = half * STEPS
    part = pl.ds(aligned(half * (mid - TILE)), tall)
    keep_other = pl.ds(aligned(half * mid), mid)
    for c in range(tiles):
        cols = tile(c)
        for level in range(levels):
            force = forcing[level, :, cols]
            for k, member in enumerate((own[level, :, cols], others[0, level, part, cols])):
                field[pl.ds(((2 * level + k) * tiles + c) * tall, tall), :] = member * force

    def at(f, c):
        return field[pl.ds((f * tiles + c) * tall, tall), :]

    ends = (tile(0), tile(tiles - 1))
    pack_other[...] = edge_columns(*([at(2 * level + 1, c) for level in range(levels)] for c in (0, tiles - 1)))
    weight_other[...] = edge_columns(*([others[0, level, keep_other, cols] for level in range(levels)] for cols in ends))
    fields = range(2 * levels)
    for q in range(planes):
        u[q, BODY, :] = turn(field, [f * tiles * tall + ch * offset + q + base for f in fields for ch in range(2)], tall)
    buffers = [u, u_next, u, u_next][:FIRST_STEPS] + [halfway]
    for step in range(FIRST_STEPS):
        count = planes - 2 - 2 * step
        refresh(buffers[step], step + 1, count)
        sweep(buffers[step], buffers[step + 1], east, north, step + 1, step + count)
    if FIRST_STEPS < STEPS:
        refresh(halfway, FIRST_STEPS + 1, planes - 2 - 2 * FIRST_STEPS)


def interior_rest_kernel(gy_size, halfway, own, others, east, north, out, u, u_next, result):
    levels, tall, width = own.shape
    tiles = width // LANES
    mid = tall - TILE
    planes = east.shape[0]
    offset = planes - 2 * STEPS
    half = half_of(gy_size)
    base = half * STEPS
    keep_own, keep_other = pl.ds(aligned(half * TILE), mid), pl.ds(aligned(half * mid), mid)
    fields = range(2 * levels)
    source = halfway
    for step in range(FIRST_STEPS, STEPS):
        count = planes - 2 - 2 * step
        if step > FIRST_STEPS:
            refresh(source, step + 1, count)
        target = u if step % 2 == 0 else u_next
        sweep(source, target, east, north, step + 1, step + count)
        source = target
    for q in range(STEPS, planes - STEPS):
        flat = source[q, BODY, :].T
        for f in fields:
            for ch in range(2):
                group = (2 * f + ch) * tiles
                result[pl.ds(f * tiles * tall + ch * offset + q + base, tiles, stride=tall), :] = flat[group : group + tiles]
    for level in range(levels):
        for c in range(tiles):
            a, b = (
                result[pl.ds(aligned(((2 * level + k) * tiles + c) * tall + half * TILE), mid), :] for k in range(2)
            )
            out[level, :, tile(c)] = own[level, keep_own, tile(c)] * a + others[0, level, keep_other, tile(c)] * b


def halo_columns_kernel(
    gy_size, strip, pack_own, pack_other, pack_coef, full_own, full_other, full_coef, west_out, east_out
):
    half = half_of(gy_size)
    tall = pack_own.shape[0]
    halo = pl.ds(aligned(half * tall), TILE)
    main = pl.ds(aligned((1 - half) * TILE), tall)
    local = [pack_own[...], pack_other[...]] + [pack_coef[k] for k in range(3)]
    corner = strip.shape[0] - 2 * TILE
    fields = [unfold(gy_size, strip[corner : corner + TILE, :], k) for k in range(2)]
    received = fields + unfold_weights(gy_size, strip[corner + TILE :, :], True)
    full = [full_own, full_other] + [full_coef.at[k] for k in range(3)]
    for rows, values in ((main, local), (halo, received)):
        west_out[rows, :] = outgoing(values, True)
        east_out[rows, :] = outgoing(values, False)
    for ref, inner, outer in zip(full, local, received):
        ref[main, :] = inner
        ref[halo, :] = outer


def outer_rows_kernel(
    gy_size, inside, strip, more, own, other, forcing, coef, sums,
    zm, mm, wet, field, face, u, u_next, east, north, result,
):
    levels, tall, width = own.shape
    tiles = width // LANES
    half = half_of(gy_size)
    outer = pl.ds(aligned(half * (tall - TILE)), TILE)
    edge = pl.ds(aligned((1 - half) * TILE), TILE)
    halo = pl.ds(aligned(half * TILE), TILE)
    block = 2 * TILE
    for k, ref in enumerate((zm, mm, wet)):
        ref[edge, :] = coef[k]
    for c in range(tiles):
        values = unfold_weights(gy_size, strip[strip_rows(levels // 2, c, tiles), :], False)
        for ref, value in zip((zm, mm, wet), values):
            ref[halo, tile(c)] = value
    wet[block:, :] = jnp.zeros((TILE, width), F32)
    for c in range(tiles):
        cols = tile(c)
        face[pl.ds(c * block, block), :], face[pl.ds((tiles + c) * block, block), :] = faces(zm, mm, wet, cols, width, block)
        for level in range(levels):
            part, where = strip_place(level, levels, (strip, more))
            for k, member in enumerate((own[level, outer, cols], other[level, :, cols])):
                base = ((2 * level + k) * tiles + c) * block
                field[pl.ds(aligned(base + (1 - half) * TILE), TILE), :] = member * forcing[level, outer, cols]
                field[pl.ds(aligned(base + half * TILE), TILE), :] = unfold(gy_size, part[strip_rows(where, c, tiles), :], k)

    fields = range(2 * levels)
    planes = 10
    lead = (1 - half) * 4
    for q in range(planes):
        u[q, BODY, :] = turn(field, [f * tiles * block + 2 * ch + q + lead for f in fields for ch in range(2)], block)
        for k, ref in enumerate((east, north)):
            if q == planes - 1 or (k == 0 and q == 0):
                continue
            ref[q, BODY, :] = turn(face, [k * tiles * block + 2 * ch + q + lead for f in fields for ch in range(2)], block)
    refresh(east, 0, planes)
    source, target = u, u_next
    for step in range(STEPS):
        count = planes - 2 - 2 * step
        refresh(source, step + 1, count)
        sweep(source, target, east, north, step + 1, step + count)
        source, target = target, source
    for p in range(2):
        flat = source[STEPS + p, BODY, :].T
        for f in fields:
            for ch in range(2):
                group = (2 * f + ch) * tiles
                result[pl.ds(f * tiles * TILE + 4 * half + 2 * ch + p, tiles, stride=TILE), :] = flat[group : group + tiles]
    mine = row_ids(TILE, LANES) // 4 == half
    place = pl.ds(aligned(half * (tall - 2 * TILE)), TILE)
    for c in range(tiles):
        cols = tile(c)
        for level in range(levels):
            a, b = (result[pl.ds(((2 * level + k) * tiles + c) * TILE, TILE), :] for k in range(2))
            term = own[level, outer, cols] * a + other[level, :, cols] * b
            sums[level, place, cols] = jnp.where(mine, term, sums[level, place, cols])


def end_columns_kernel(
    gy_size, from_west, from_east, own, other, coef, weight_own, weight_other, out,
    a, b, a_next, b_next, east, north, wet,
):
    full = own.shape[0]
    body = pl.ds(TILE, full)
    place = lane_ids(full) % GROUP
    on_west = (place >= 4) & (place < 8)
    on_east = (place >= 24) & (place < 28)
    west, east_strip = from_west[...], from_east[...]

    def with_ends(value, k):
        value = jnp.where(on_west, pltpu.roll(west, (-4 * k) % LANES, 1), value)
        return jnp.where(on_east, pltpu.roll(east_strip, 4 * k, 1), value)

    blank = jnp.zeros((TILE, LANES), F32)
    for ref in (a, b, a_next, b_next, east, north, wet):
        ref[:TILE, :] = blank
        ref[full + TILE :, :] = blank
    a[body, :] = with_ends(own[...], 0)
    b[body, :] = with_ends(other[...], 1)
    wet[body, :] = with_ends(coef[2], 4)
    east[body, :] = with_ends(coef[0], 2) * pltpu.roll(wet[body, :], LANES - 1, 1)
    north[body, :] = with_ends(coef[1], 3) * wet[pl.ds(TILE + 1, full), :]
    now, later = (a, b), (a_next, b_next)
    for step in range(STEPS):
        for t in range(TILE, full + TILE, TILE):
            at, above, below = (pl.ds(t + d, TILE) for d in (0, 1, -1))
            e, n, s = east[at, :], north[at, :], north[below, :]
            for source, target in zip(now, later):
                here = source[at, :]
                flux = e * (pltpu.roll(here, LANES - 1, 1) - here)
                go_north = n * (source[above, :] - here)
                go_south = s * (here - source[below, :])
                target[at, :] = here + flux - pltpu.roll(flux, 1, 1) + go_north - go_south
        now, later = later, now
    mid = weight_own.shape[0]
    rows = pl.ds(2 * TILE, mid)
    out[...] = weight_own[...] * now[0][rows, :] + weight_other[...] * now[1][rows, :]


def join_kernel(gy_size, mine_in, theirs_in, mine_edge, theirs_edge, mine, theirs, out, sems):
    half = half_of(gy_size)
    levels, mid, width = mine.shape
    lane = lane_ids(mid)
    first, last, between = slice(0, LANES), slice(width - LANES, width), slice(LANES, width - LANES)
    halves = ((mine, mine_edge, half), (theirs, theirs_edge, 1 - half))
    copies = []

    def send(k, cols, place):
        ref, _, where = halves[k]
        rows = pl.ds(aligned(where * mid), mid)
        copies.append(pltpu.make_async_copy(ref.at[:, :, cols], out.at[:, rows, cols], sems.at[k, place]))
        copies[-1].start()

    for k in range(2):
        send(k, between, 0)
    for k, (ref, edges, _) in enumerate(halves):
        packed = edges[...]
        for level in range(levels):
            base = GROUP * level
            ref[level, :, first] = jnp.where(lane < 4, pltpu.roll(packed, (-base - 8) % LANES, 1), ref[level, :, first])
        send(k, first, 1)
        for level in range(levels):
            base = GROUP * level
            ref[level, :, last] = jnp.where(
                lane >= LANES - 4, pltpu.roll(packed, (LANES - 4 - base - 20) % LANES, 1), ref[level, :, last]
            )
        send(k, last, 2)
    for copy in copies:
        copy.wait()


def shards(sizes, increment, members, zonal_diff, merid_diff, sea_mask):
    n_mem, n_gy, n_gx = sizes
    levels, rows, width = increment.shape
    tiles = width // LANES
    mid = rows // 2
    tall = mid + TILE
    full = tall + TILE
    planes = (mid - STEPS) // 2 + 2 * STEPS
    assert tiles == TILE and 4 * levels * tiles == LANES and tall == 5 * TILE and n_mem % 2 == 0

    def call(kernel, ins, specs, outs, scratch=(), out_specs=None, aliases={}):
        return pl.pallas_call(
            functools.partial(kernel, n_gy),
            out_shape=outs,
            in_specs=specs,
            out_specs=out_specs if out_specs is not None else jax.tree.map(lambda _: VMEM, outs),
            scratch_shapes=scratch,
            input_output_aliases=aliases,
            compiler_params=pltpu.CompilerParams(vmem_limit_bytes=40 * 1024 * 1024),
        )(*ins)

    def held(kernel, ins, outs, scratch=(), **kw):
        got = call(kernel, [pinned(x) for x in ins], [VMEM] * len(ins), outs, scratch, **kw)
        return got

    def swap(x):
        return lax.ppermute(x, "mem", [(i, i ^ 1) for i in range(n_mem)])

    def along(x, shift):
        return lax.ppermute(x, "gx", [(i, (i + shift) % n_gx) for i in range(n_gx)])

    def across(x):
        def place(chip, core, j, i):
            return ((2 * chip + core) * n_gy + j) * n_gx + i

        first = [0 if j < n_gy // 2 else 1 for j in range(n_gy)]
        pairs = []
        for chip in range(n_mem // 2):
            for j in range(n_gy - 1):
                for i in range(n_gx):
                    a = place(chip, 1 - first[j], j, i)
                    b = place(chip, first[j + 1], j + 1, i)
                    pairs += [(a, b), (b, a)]
            for i in range(n_gx - n_gx % 2):
                pairs.append((place(chip, first[0], 0, i), place(chip, first[0], 0, i ^ 1)))
                pairs.append((place(chip, 1 - first[-1], n_gy - 1, i), place(chip, 1 - first[-1], n_gy - 1, i ^ 1)))
        return lax.ppermute(x, AXES, pairs)

    def scratch(*shape):
        return pltpu.VMEM(shape, F32)

    others = swap(members)
    end = kept(full, LANES)
    turned = kept(planes, DEPTH, LANES)
    own, forcing, coef, face_east, face_north, pack_coef = call(
        load_kernel,
        [in_hbm(x) for x in (members, increment, zonal_diff, merid_diff, sea_mask)],
        [HBM] * 5,
        [kept(levels, tall, width)] * 2
        + [kept(3, TILE, width), turned, turned, kept(3, tall, LANES)],
        [
            pltpu.VMEM((tall, width), jnp.int32),
            scratch(tall, width),
            scratch(tall, width),
            scratch(full, width),
            scratch(2 * tiles * tall, LANES),
            pltpu.SemaphoreType.DMA((5,)),
        ],
    )
    packed = kept(tall, LANES)
    weights, coef_ends, pack_own, weight_own = held(
        own_ends_kernel, [own, forcing, coef], [kept(TILE, width), kept(TILE, LANES), packed, kept(mid, LANES)]
    )
    deep = levels // 2 * tiles * TILE
    other, strip, more = held(
        pack_rows_kernel,
        [own, others, forcing, weights, coef_ends],
        [kept(levels, TILE, width), kept(deep + tiles * TILE + 2 * TILE, LANES), kept(deep, LANES)],
    )
    forcing, strip, more = lax.optimization_barrier((forcing, strip, more))
    strip, more = across(strip), across(more)
    halfway, pack_other, weight_other = held(
        interior_kernel,
        [own, others, forcing, face_east, face_north],
        [turned, packed, kept(mid, LANES)],
        [scratch(2 * levels * tiles * tall, LANES), scratch(planes, DEPTH, LANES), scratch(planes, DEPTH, LANES)],
    )
    full_own, full_other, full_coef, west, east = held(
        halo_columns_kernel,
        [strip, pack_own, pack_other, pack_coef],
        [end, end, kept(3, full, LANES), end, end],
    )
    halfway, west, east = lax.optimization_barrier((halfway, west, east))
    from_west = along(east, 1)
    from_east = along(west, -1)
    inside = held(
        interior_rest_kernel,
        [halfway, own, others, face_east, face_north],
        kept(levels, mid, width),
        [
            scratch(planes, DEPTH, LANES),
            scratch(planes, DEPTH, LANES),
            scratch(2 * levels * tiles * tall, LANES),
        ],
    )
    inside, forcing = lax.optimization_barrier((inside, forcing))
    inside = held(
        outer_rows_kernel,
        [inside, strip, more, own, other, forcing, coef],
        kept(levels, mid, width),
        [
            scratch(2 * TILE, width),
            scratch(2 * TILE, width),
            scratch(3 * TILE, width),
            scratch(2 * levels * tiles * 2 * TILE, LANES),
            scratch(2 * tiles * 2 * TILE, LANES),
            scratch(10, DEPTH, LANES),
            scratch(10, DEPTH, LANES),
            scratch(10, DEPTH, LANES),
            scratch(10, DEPTH, LANES),
            scratch(2 * levels * tiles * TILE, LANES),
        ],
        aliases={0: 0},
    )
    inside, from_west, from_east = lax.optimization_barrier((inside, from_west, from_east))
    edges = held(
        end_columns_kernel,
        [from_west, from_east, full_own, full_other, full_coef, weight_own, weight_other],
        kept(mid, LANES),
        [scratch(full + 2 * TILE, LANES)] * 7,
    )
    if n_mem > 2:
        groups = [list(range(k, n_mem, 2)) for k in range(2)]
        inside, edges = (lax.psum(x, "mem", axis_index_groups=groups) for x in (inside, edges))
    inside_theirs, edges_theirs = swap(inside), swap(edges)
    return held(
        join_kernel,
        [inside, inside_theirs, edges, edges_theirs],
        [kept(levels, mid, width)] * 2 + [jax.ShapeDtypeStruct(increment.shape, F32)],
        [pltpu.SemaphoreType.DMA((2, 3))],
        out_specs=[VMEM, VMEM, HBM],
        aliases={0: 0, 1: 1},
    )[2]


def solution(mesh):
    return jax.shard_map(
        functools.partial(shards, tuple(mesh.shape[axis] for axis in AXES)),
        mesh=mesh,
        in_specs=(
            P(None, "gy", "gx"),
            P("mem", None, "gy", "gx"),
            P("gy", "gx"),
            P("gy", "gx"),
            P("gy", "gx"),
        ),
        out_specs=P(None, "gy", "gx"),
        check_vma=False,
    )
```
